32 devices in a mesh: ctx: 16 (over z, y, x), head: 2 (over core).
Axes of the slice: x: 2, y: 2, z: 4, core: 2. Of those that a mesh axis runs over, the one named last changes fastest.
Arguments:
- query: bfloat16 [4096, 8192], P(('ctx', 'head')), may hold values from -20 to 20
- key: bfloat16 [4096, 1024], P(('ctx', 'head')), may hold values from -6 to 6
- value: bfloat16 [4096, 1024], P(('ctx', 'head')), may hold values from -6 to 6
- doc_lengths: int32 [4], replicated, may hold values from 256 to 2048, as said below
- block_place: int32 [256], replicated, may hold values from 0 to 255, as said below
Outputs:
- attended: bfloat16 [4096, 8192], P('ctx', 'head')
The draws below stay inside these ranges and needn't reach their ends.
Inputs may be any that keep to these rules, and one draw needn't show every extreme that they name: `doc_lengths`: 4 lengths that sum to 4096; the longest is exactly 2048 and the shortest exactly 256. `block_place`: A permutation of the blocks. The 8 blocks of one loading device (one index of ctx+head, ctx slowest) go to distinct context shards; context shard s holds packed blocks s * 16 to (s + 1) * 16 - 1.
All inputs are finite; a program needn't handle non-finite values.
Results may differ from the reference program's by a relative error of at most 0.0028.
Values may be sent and summed in bfloat16 or wider, within the bound.
No kernel may reach another device: no remote copies, remote signals or barrier semaphores. Data moves between devices by JAX's collectives and lax.ppermute only.
A program may use at most 192 MiB of HBM per device.

```python
import jax
import jax.numpy as jnp
from jax import lax

TOK_DEV = 256
QH = 64
KVH = 8
HD = 128
SPAN = 8
SHARDS = 16
GROUPS = 2
SEQ = 4096
BLK = 16
NBLK = 256
NDOC = 4


def draw_query(key, part):
    key = jax.random.fold_in(key, 1)
    values = 3.0 * jax.random.truncated_normal(key, -6.0, 6.0, (SEQ, QH, HD))
    return values.reshape(SEQ, QH * HD).astype(jnp.bfloat16)


def draw_key(key, part):
    key = jax.random.fold_in(key, 2)
    values = jax.random.truncated_normal(key, -6.0, 6.0, (SEQ, KVH, HD))
    return values.reshape(SEQ, KVH * HD).astype(jnp.bfloat16)


def draw_doc_lengths(key, part):
    key = jax.random.fold_in(key, 3)
    weight_key, order_key = jax.random.split(key)
    remaining = SEQ - (SPAN + 1) * TOK_DEV - (NDOC - 2) * TOK_DEV
    weights = jax.random.randint(weight_key, (NDOC - 2,), 500, 1000)
    extras = remaining * weights // jnp.sum(weights)
    leftover = remaining - jnp.sum(extras)
    extras = extras + (jnp.arange(NDOC - 2) < leftover).astype(jnp.int32)
    lengths = jnp.concatenate([jnp.array([SPAN * TOK_DEV, TOK_DEV], dtype=jnp.int32), TOK_DEV + extras.astype(jnp.int32)])
    shuffle = jax.random.permutation(order_key, NDOC)
    return lengths[shuffle].astype(jnp.int32)


def draw_block_place(key, part):
    key = jax.random.fold_in(key, 4)
    rotate_key, offset_key, tie_key = jax.random.split(key, 3)
    per_loader = SHARDS // GROUPS
    rotation = jax.vmap(lambda subkey: jax.random.permutation(subkey, SHARDS))(jax.random.split(rotate_key, GROUPS))
    offsets = jax.vmap(lambda subkey: jax.random.permutation(subkey, SHARDS)[:per_loader])(jax.random.split(offset_key, GROUPS))
    target = (jnp.transpose(rotation)[:, :, None] + offsets[None, :, :]) % SHARDS
    target = target.reshape(NBLK)
    tiebreak = jax.random.permutation(tie_key, NBLK)
    scores = target * NBLK + tiebreak
    ranking = jnp.argsort(scores)
    placed = jnp.argsort(ranking)
    return placed.astype(jnp.int32)


def block_levels(own_key, extent, cuts, least, top_value):
    def one(axis_at, shards_of):
        heights = jax.random.uniform(jax.random.fold_in(jax.random.fold_in(own_key, 6), axis_at), (shards_of,), jnp.float32, least / len(cuts), top_value / len(cuts))
        return jnp.repeat(jnp.exp(heights), extent[axis_at] // shards_of).reshape((-1,) + (1,) * (len(extent) - axis_at - 1))

    level = one(*cuts[0])
    for cut in cuts[1:]:
        level = level * one(*cut)
    return level


def normal_values(rng, dims, width, reach, cuts=(), held_as=jnp.bfloat16):
    drawn = jax.random.normal(rng, dims, jnp.float32) * width
    if len(cuts) > 0:
        drawn = block_levels(rng, dims, cuts, -0.22, 0.18) * drawn
    return jnp.clip(drawn, min=-reach, max=reach).astype(held_as)


def setup_inputs(seed: int = 0) -> dict:
    streams_of = jax.random.split(jax.random.key(seed), 6)
    query = draw_query(jax.random.fold_in(streams_of[5], 71), 0)
    key = draw_key(jax.random.fold_in(streams_of[5], 71), 0)
    value = normal_values(streams_of[2], (SEQ, KVH * HD), 1.0, 6.0, ((0, 32),))
    doc_lengths = draw_doc_lengths(jax.random.fold_in(streams_of[5], 71), 0)
    block_place = draw_block_place(jax.random.fold_in(streams_of[5], 71), 0)
    return dict(query=query, key=key, value=value, doc_lengths=doc_lengths, block_place=block_place)


def doc_starts(positions, doc_lengths):
    doc_ends = jnp.cumsum(doc_lengths).astype(jnp.int32)
    before = jnp.where(positions[:, None] >= doc_ends[None, :], doc_lengths[None, :], 0)
    return jnp.sum(before, axis=1).astype(jnp.int32)


def reference(query, key, value, doc_lengths, block_place):
    inverse = jnp.argsort(block_place).astype(jnp.int32)

    def packed(loaded):
        blocks = loaded.reshape(NBLK, BLK, loaded.shape[1])
        return jnp.take(blocks, inverse, axis=0).reshape(SEQ, loaded.shape[1])

    query_packed = packed(query).reshape(SEQ, KVH, QH // KVH, HD)
    reach_rows = SPAN * TOK_DEV
    key_packed = packed(key).reshape(SEQ, KVH, HD)
    value_packed = packed(value).reshape(SEQ, KVH, HD)
    keys_padded = jnp.concatenate([jnp.zeros((reach_rows, KVH, HD), key_packed.dtype), key_packed], axis=0)
    values_padded = jnp.concatenate([jnp.zeros((reach_rows, KVH, HD), value_packed.dtype), value_packed], axis=0)
    positions = jnp.arange(SEQ, dtype=jnp.int32)
    doc_start = doc_starts(positions, doc_lengths)
    score_scale = HD ** -0.5

    def attend_block(block_index):
        first_row = block_index * TOK_DEV
        query_block = lax.dynamic_slice_in_dim(query_packed, first_row, TOK_DEV, 0).astype(jnp.float32)
        key_window = lax.dynamic_slice_in_dim(keys_padded, first_row, reach_rows + TOK_DEV, 0).astype(jnp.float32)
        value_window = lax.dynamic_slice_in_dim(values_padded, first_row, reach_rows + TOK_DEV, 0).astype(jnp.float32)
        query_rows = first_row + jnp.arange(TOK_DEV, dtype=jnp.int32)
        key_rows = first_row - reach_rows + jnp.arange(reach_rows + TOK_DEV, dtype=jnp.int32)
        query_start = lax.dynamic_slice_in_dim(doc_start, first_row, TOK_DEV, 0)
        visible = (key_rows[None, :] >= query_start[:, None]) & (key_rows[None, :] <= query_rows[:, None])
        scores = jnp.einsum("tkgd,skd->kgts", query_block, key_window) * score_scale
        scores = jnp.where(visible, scores, -1e30)
        row_max = jnp.max(scores, axis=-1, keepdims=True)
        weights = jnp.where(visible, jnp.exp(scores - row_max), 0.0)
        row_sum = jnp.sum(weights, axis=-1)
        rounded = lax.optimization_barrier(weights.astype(jnp.bfloat16)).astype(jnp.float32)
        numerator = jnp.einsum("kgts,skd->kgtd", rounded, value_window)
        output_block = (numerator / row_sum[..., None]).astype(jnp.bfloat16)
        return jnp.transpose(output_block, (2, 0, 1, 3)).reshape(TOK_DEV, QH * HD)

    blocks = lax.map(attend_block, jnp.arange(SEQ // TOK_DEV, dtype=jnp.int32))
    return blocks.reshape(SEQ, QH * HD)
```

```python
import functools

import jax
import jax.numpy as jnp
import numpy as np
from jax import lax
from jax.experimental import pallas as pl
from jax.experimental.pallas import tpu as pltpu
from jax.sharding import PartitionSpec as P

HD = 128
SPAN = 8
MASKED = -1e30
EXP2_SCALE = float(HD ** (-0.5) * np.log2(np.e))
VMEM_LIMIT = 48 * 1024 * 1024
ANY = pl.BlockSpec(memory_space=pl.ANY)


def pack_kernel(chunks, place_ref, loader_ref, query, key, value, *refs):
    outs, (own, other, sems) = refs[:chunks], refs[chunks:]
    per_loader = query.shape[0]
    group = loader_ref[1]
    half = key.shape[1] // 2
    width = outs[0].shape[2]
    copies = []

    def start(src, dst):
        copy = pltpu.make_async_copy(src, dst, sems.at[len(copies)])
        copy.start()
        copies.append(copy)

    for out, which in ((own, group), (other, 1 - group)):
        columns = pl.ds(pl.multiple_of(which * half, half), half)
        start(key.at[:, columns], out.at[:, pl.ds(0, half)])
        start(value.at[:, columns], out.at[:, pl.ds(half, half)])
    for chunk in range(chunks):
        for j in range(per_loader):
            target = place_ref[loader_ref[0] * per_loader + j] // loader_ref[2]
            for side in range(2):
                start(
                    query.at[j, :, pl.ds((side * chunks + chunk) * width, width)],
                    outs[chunk].at[target * 2 + side],
                )
    for copy in copies:
        copy.wait()


def pack(query, key, value, block_place, loader, shard_blocks, slots, chunks):
    rows, columns = query.shape
    per_loader = block_place.shape[0] // slots
    block_rows = rows // per_loader
    width = columns // 2 // chunks
    half = key.shape[1] // 2
    blocks = query.reshape(per_loader, block_rows, columns)
    if block_rows % 16:
        group = loader % 2
        assigned = lax.dynamic_slice_in_dim(block_place, loader * per_loader, per_loader)
        targets = assigned // shard_blocks
        matched = targets[None, :] == jnp.arange(slots // 2, dtype=jnp.int32)[:, None]
        sources = jnp.argmax(matched, axis=1)
        picked = jnp.take(blocks, sources, axis=0)
        picked = picked.reshape(slots // 2, block_rows, 2, chunks, width)
        sends = [
            jnp.swapaxes(picked[:, :, :, chunk], 1, 2).reshape(slots, block_rows, width)
            for chunk in range(chunks)
        ]
        pairs = [
            jnp.concatenate(
                [lax.dynamic_slice_in_dim(x, which * half, half, 1) for x in (key, value)], axis=1
            )
            for which in (group, 1 - group)
        ]
        return sends, pairs[0], pairs[1]
    scalars = jnp.stack([loader, loader % 2, jnp.int32(shard_blocks)]).astype(jnp.int32)
    outs = pl.pallas_call(
        functools.partial(pack_kernel, chunks),
        out_shape=[jax.ShapeDtypeStruct((slots, block_rows, width), query.dtype)] * chunks
        + [jax.ShapeDtypeStruct((rows, 2 * half), key.dtype)] * 2,
        grid_spec=pltpu.PrefetchScalarGridSpec(
            num_scalar_prefetch=2,
            grid=(1,),
            in_specs=[ANY] * 3,
            out_specs=[ANY] * (chunks + 2),
            scratch_shapes=[pltpu.SemaphoreType.DMA((4 + 2 * chunks * per_loader,))],
        ),
        name="pack",
    )(block_place, scalars, blocks, key, value)
    return outs[:chunks], outs[chunks], outs[chunks + 1]


def window_kernel(count, rows_ref, same, cross, out, sem):
    limit = same.shape[0]

    def start(w, carry):
        source = rows_ref[w]

        @pl.when(source < limit)
        def _():
            pltpu.make_async_copy(same.at[source], out.at[w], sem).start()

        @pl.when(source >= limit)
        def _():
            pltpu.make_async_copy(cross.at[source - limit], out.at[w], sem).start()

        return carry

    lax.fori_loop(0, count, start, 0)
    pltpu.make_async_copy(out, out, sem).wait()


def pick_window(sources, same, cross):
    count = sources.shape[0]
    if same.shape[1] % 16:
        return jnp.take(jnp.concatenate([same, cross]), sources, axis=0)
    return pl.pallas_call(
        functools.partial(window_kernel, count),
        out_shape=jax.ShapeDtypeStruct((count,) + same.shape[1:], same.dtype),
        grid_spec=pltpu.PrefetchScalarGridSpec(
            num_scalar_prefetch=1,
            grid=(1,),
            in_specs=[ANY, ANY],
            out_specs=ANY,
            scratch_shapes=[pltpu.SemaphoreType.DMA(())],
        ),
        name="window",
        cost_estimate=pl.CostEstimate(
            flops=0, transcendentals=0, bytes_accessed=4 * count * same.shape[1] * same.shape[2]
        ),
    )(sources, same, cross)


def attend_kernel(
    docs, heads, tile, slot_ref, lengths_ref, shard_ref, *refs
):
    arrived, keys, values = refs[0], refs[1], refs[2]
    out, queries, maxes, sums, sem = refs[-5:]
    blocks, block_rows, width = queries.shape
    rows = blocks * block_rows
    copies = []
    for i in range(blocks):
        copy = pltpu.make_async_copy(arrived.at[slot_ref[i]], queries.at[i], sem.at[i])
        copy.start()
        copies.append(copy)
    first_row = shard_ref[0] * rows
    query_rows = first_row + lax.broadcasted_iota(jnp.int32, (1, rows), 1)
    starts = jnp.zeros((1, rows), jnp.int32)
    first_start = jnp.int32(0)
    end = jnp.int32(0)
    for d in range(docs):
        length = lengths_ref[d]
        end = end + length
        starts = starts + jnp.where(query_rows >= end, length, 0)
        first_start = first_start + jnp.where(first_row >= end, length, 0)
    tiles = keys.shape[0] // tile
    window_start = first_row + rows - keys.shape[0]
    diagonal = tiles - 1
    first_tile = (first_start - window_start) // tile
    for h in range(heads):
        maxes[h] = jnp.full((1, rows), MASKED, jnp.float32)
        sums[h] = jnp.zeros(sums.shape[1:], jnp.float32)
    for copy in copies:
        copy.wait()

    def step(index, masked, last):
        span = pl.ds(pl.multiple_of(index * tile, tile), tile)
        tile_keys = keys[span, :]
        tile_values = values[span, :]
        extended = jnp.concatenate([tile_values, jnp.ones((tile, HD), tile_values.dtype)], axis=1)
        turned = extended.T[: HD + 16]
        if masked:
            key_rows = window_start + index * tile + lax.broadcasted_iota(jnp.int32, (tile, rows), 0)
            visible = (key_rows >= starts) & (key_rows <= query_rows)
        if last:
            later = starts >= first_row

        def score(h):
            query = queries[:, :, h * HD : (h + 1) * HD].reshape(rows, HD)
            return lax.dot_general(
                tile_keys, query, (((1,), (1,)), ((), ())), preferred_element_type=jnp.float32
            )

        ahead = score(0)
        for h in range(heads):
            scores = ahead
            if h + 1 < heads:
                ahead = score(h + 1)
            if masked:
                scores = jnp.where(visible, scores, MASKED)
            old = maxes[h]
            if last:
                old = jnp.where(later, MASKED, old)
            new = jnp.maximum(old, jnp.max(scores, axis=0, keepdims=True))
            scaled = new * EXP2_SCALE
            weights = jnp.exp2(scores * EXP2_SCALE - scaled).astype(jnp.bfloat16)
            factor = jnp.exp2(old * EXP2_SCALE - scaled)
            product = jnp.dot(turned, weights, preferred_element_type=jnp.float32)
            total = sums[h] * factor + product
            if last:
                result = total[:HD] / total[HD : HD + 1]
                out[:, h * HD : (h + 1) * HD] = result.T.astype(out.dtype)
            else:
                maxes[h] = new
                sums[h] = total

    @pl.when(first_tile < diagonal)
    def _():
        step(first_tile, True, False)

    def middle(index, carry):
        step(index, False, False)
        return carry

    lax.fori_loop(first_tile + 1, diagonal, middle, 0)
    step(diagonal, True, True)


def attend(arrived, window, slots, doc_lengths, shard, chunk, chunks, result, shard_rows):
    block_rows, width = arrived.shape[1:]
    blocks = shard_rows // block_rows
    if block_rows % 16:
        arrived = jnp.take(arrived, slots, axis=0).reshape(shard_rows // 16, 16, width)
        block_rows, blocks = 16, shard_rows // 16
        slots = jnp.arange(blocks, dtype=jnp.int32)
    heads = width // HD
    key_heads = window.shape[1] // 2 // HD
    per_key = window.shape[0]
    aliased = [] if result is None else [result]
    return pl.pallas_call(
        functools.partial(attend_kernel, doc_lengths.shape[0], heads, shard_rows),
        out_shape=jax.ShapeDtypeStruct((shard_rows, chunks * width), arrived.dtype),
        grid_spec=pltpu.PrefetchScalarGridSpec(
            num_scalar_prefetch=3,
            grid=(1,),
            in_specs=[
                ANY,
                pl.BlockSpec((per_key, HD), lambda i, *_: (0, chunk)),
                pl.BlockSpec((per_key, HD), lambda i, *_: (0, key_heads + chunk)),
            ]
            + [ANY] * len(aliased),
            out_specs=pl.BlockSpec((shard_rows, width), lambda i, *_: (0, chunk)),
            scratch_shapes=[
                pltpu.VMEM((blocks, block_rows, width), arrived.dtype),
                pltpu.VMEM((heads, 1, shard_rows), jnp.float32),
                pltpu.VMEM((heads, HD + 16, shard_rows), jnp.float32),
                pltpu.SemaphoreType.DMA((blocks,)),
            ],
        ),
        input_output_aliases={6: 0} if aliased else {},
        compiler_params=pltpu.CompilerParams(vmem_limit_bytes=VMEM_LIMIT),
        name=f"attend{chunk}",
        cost_estimate=pl.CostEstimate(
            flops=4 * shard_rows * per_key * width,
            transcendentals=shard_rows * per_key * heads,
            bytes_accessed=4 * shard_rows * width + 4 * per_key * HD,
        ),
    )(slots, doc_lengths, shard, arrived, window, window, *aliased)


def body(query, key, value, doc_lengths, block_place):
    ctx_count = lax.axis_size("ctx")
    head_count = lax.axis_size("head")
    loaded_rows = query.shape[0]
    shard_rows = loaded_rows * head_count
    block_rows = shard_rows // ctx_count
    per_loader = loaded_rows // block_rows
    shard_blocks = shard_rows // block_rows
    shard = lax.axis_index("ctx").astype(jnp.int32)
    group = lax.axis_index("head").astype(jnp.int32)
    loader = shard * head_count + group
    slots = ctx_count * head_count
    chunks = key.shape[1] // head_count // HD
    sends, own, other = pack(
        query, key, value, block_place, loader, shard_blocks, slots, chunks
    )
    swapped = lax.ppermute(other, "head", [(0, 1), (1, 0)])
    same = lax.all_gather(own, "ctx", tiled=True)
    cross = lax.all_gather(swapped, "ctx", tiled=True)
    arrived = [
        lax.all_to_all(send, ("ctx", "head"), split_axis=0, concat_axis=0, tiled=True)
        for send in sends
    ]
    wanted = (shard - SPAN) * shard_blocks + jnp.arange((SPAN + 1) * shard_blocks, dtype=jnp.int32)
    wanted = jnp.maximum(wanted, 0)
    places = jnp.arange(block_place.shape[0], dtype=jnp.int32)
    inverse = jnp.sum(jnp.where(wanted[:, None] == block_place[None, :], places[None, :], 0), axis=1)
    source = inverse // per_loader
    half_blocks = ctx_count * per_loader
    sources = (
        source // head_count * per_loader
        + inverse % per_loader
        + jnp.where(source % head_count == group, 0, half_blocks)
    )
    width = same.shape[1]
    window = pick_window(
        sources,
        same.reshape(half_blocks, block_rows, width),
        cross.reshape(half_blocks, block_rows, width),
    )
    window = window.reshape((SPAN + 1) * shard_rows, width)
    result = None
    for chunk in range(chunks):
        result = attend(
            arrived[chunk],
            window,
            source[SPAN * shard_blocks :],
            doc_lengths,
            shard[None],
            chunk,
            chunks,
            result,
            shard_rows,
        )
    return result


def solution(mesh):
    placed = (
        P(("ctx", "head"), None),
        P(("ctx", "head"), None),
        P(("ctx", "head"), None),
        P(),
        P(),
    )
    return jax.shard_map(
        body, mesh=mesh, in_specs=placed, out_specs=P("ctx", "head"), check_vma=False
    )
```

```python
import functools

import jax
import jax.numpy as jnp
import numpy as np
from jax import lax
from jax.experimental import pallas as pl
from jax.experimental.pallas import tpu as pltpu
from jax.sharding import PartitionSpec as P

HD = 128
SPAN = 8
MASKED = -1e30
EXP2_SCALE = float(HD ** (-0.5) * np.log2(np.e))
VMEM_LIMIT = 48 * 1024 * 1024
ANY = pl.BlockSpec(memory_space=pl.ANY)


def pack_kernel(chunks, place_ref, loader_ref, query, key, value, *refs):
    outs, (own, other, sems) = refs[:chunks], refs[chunks:]
    per_loader = query.shape[0]
    group = loader_ref[1]
    half = key.shape[1] // 2
    width = outs[0].shape[2]
    copies = []

    def start(src, dst):
        copy = pltpu.make_async_copy(src, dst, sems.at[len(copies)])
        copy.start()
        copies.append(copy)

    for out, which in ((own, group), (other, 1 - group)):
        columns = pl.ds(pl.multiple_of(which * half, half), half)
        start(key.at[:, columns], out.at[:, pl.ds(0, half)])
        start(value.at[:, columns], out.at[:, pl.ds(half, half)])
    for chunk in range(chunks):
        for j in range(per_loader):
            target = place_ref[loader_ref[0] * per_loader + j] // loader_ref[2]
            for side in range(2):
                start(
                    query.at[j, :, pl.ds((side * chunks + chunk) * width, width)],
                    outs[chunk].at[target * 2 + side],
                )
    for copy in copies:
        copy.wait()


def pack(query, key, value, block_place, loader, shard_blocks, slots, chunks):
    rows, columns = query.shape
    per_loader = block_place.shape[0] // slots
    block_rows = rows // per_loader
    width = columns // 2 // chunks
    half = key.shape[1] // 2
    blocks = query.reshape(per_loader, block_rows, columns)
    if block_rows % 16:
        group = loader % 2
        assigned = lax.dynamic_slice_in_dim(block_place, loader * per_loader, per_loader)
        targets = assigned // shard_blocks
        matched = targets[None, :] == jnp.arange(slots // 2, dtype=jnp.int32)[:, None]
        sources = jnp.argmax(matched, axis=1)
        picked = jnp.take(blocks, sources, axis=0)
        picked = picked.reshape(slots // 2, block_rows, 2, chunks, width)
        sends = [
            jnp.swapaxes(picked[:, :, :, chunk], 1, 2).reshape(slots, block_rows, width)
            for chunk in range(chunks)
        ]
        pairs = [
            jnp.concatenate(
                [lax.dynamic_slice_in_dim(x, which * half, half, 1) for x in (key, value)], axis=1
            )
            for which in (group, 1 - group)
        ]
        return sends, pairs[0], pairs[1]
    scalars = jnp.stack([loader, loader % 2, jnp.int32(shard_blocks)]).astype(jnp.int32)
    outs = pl.pallas_call(
        functools.partial(pack_kernel, chunks),
        out_shape=[jax.ShapeDtypeStruct((slots, block_rows, width), query.dtype)] * chunks
        + [jax.ShapeDtypeStruct((rows, 2 * half), key.dtype)] * 2,
        grid_spec=pltpu.PrefetchScalarGridSpec(
            num_scalar_prefetch=2,
            grid=(1,),
            in_specs=[
                pl.BlockSpec(blocks.shape, lambda i, *_: (0, 0, 0)),
                pl.BlockSpec(key.shape, lambda i, *_: (0, 0)),
                pl.BlockSpec(value.shape, lambda i, *_: (0, 0)),
            ],
            out_specs=[ANY] * (chunks + 2),
            scratch_shapes=[pltpu.SemaphoreType.DMA((4 + 2 * chunks * per_loader,))],
        ),
        compiler_params=pltpu.CompilerParams(vmem_limit_bytes=VMEM_LIMIT),
        name="pack",
    )(block_place, scalars, blocks, key, value)
    return outs[:chunks], outs[chunks], outs[chunks + 1]


def window_kernel(count, rows_ref, blocks, out, sem):
    def start(w, carry):
        pltpu.make_async_copy(blocks.at[rows_ref[w]], out.at[w], sem).start()
        return carry

    lax.fori_loop(0, count, start, 0, unroll=8)
    pltpu.make_async_copy(out, out, sem).wait()


def pick_window(sources, blocks):
    count = sources.shape[0]
    shape = (count,) + blocks.shape[1:]
    if blocks.shape[1] % 16:
        return jnp.take(blocks, sources, axis=0)
    return pl.pallas_call(
        functools.partial(window_kernel, count),
        out_shape=jax.ShapeDtypeStruct(shape, blocks.dtype),
        grid_spec=pltpu.PrefetchScalarGridSpec(
            num_scalar_prefetch=1,
            grid=(1,),
            in_specs=[ANY],
            out_specs=pl.BlockSpec(shape, lambda i, *_: (0, 0, 0)),
            scratch_shapes=[pltpu.SemaphoreType.DMA(())],
        ),
        compiler_params=pltpu.CompilerParams(vmem_limit_bytes=VMEM_LIMIT),
        name="window",
        cost_estimate=pl.CostEstimate(
            flops=0, transcendentals=0, bytes_accessed=4 * count * shape[1] * shape[2]
        ),
    )(sources, blocks)


def attend_kernel(
    docs, heads, tile, slot_ref, lengths_ref, shard_ref, *refs
):
    arrived, keys, values = refs[0], refs[1], refs[2]
    out, queries, maxes, sums, sem = refs[-5:]
    blocks, block_rows, width = queries.shape
    rows = blocks * block_rows
    copies = []
    for i in range(blocks):
        copy = pltpu.make_async_copy(arrived.at[slot_ref[i]], queries.at[i], sem.at[i])
        copy.start()
        copies.append(copy)
    first_row = shard_ref[0] * rows
    query_rows = first_row + lax.broadcasted_iota(jnp.int32, (1, rows), 1)
    starts = jnp.zeros((1, rows), jnp.int32)
    first_start = jnp.int32(0)
    end = jnp.int32(0)
    for d in range(docs):
        length = lengths_ref[d]
        end = end + length
        starts = starts + jnp.where(query_rows >= end, length, 0)
        first_start = first_start + jnp.where(first_row >= end, length, 0)
    tiles = keys.shape[0] // tile
    window_start = first_row + rows - keys.shape[0]
    diagonal = tiles - 1
    first_tile = (first_start - window_start) // tile
    for h in range(heads):
        maxes[h] = jnp.full((1, rows), MASKED, jnp.float32)
        sums[h] = jnp.zeros(sums.shape[1:], jnp.float32)
    for copy in copies:
        copy.wait()

    def step(index, masked, last):
        span = pl.ds(pl.multiple_of(index * tile, tile), tile)
        tile_keys = keys[span, :]
        tile_values = values[span, :]
        extended = jnp.concatenate([tile_values, jnp.ones((tile, HD), tile_values.dtype)], axis=1)
        turned = extended.T[: HD + 16]
        if masked:
            key_rows = window_start + index * tile + lax.broadcasted_iota(jnp.int32, (tile, rows), 0)
            visible = (key_rows >= starts) & (key_rows <= query_rows)
        if last:
            later = starts >= first_row

        def score(h):
            query = queries[:, :, h * HD : (h + 1) * HD].reshape(rows, HD)
            return lax.dot_general(
                tile_keys, query, (((1,), (1,)), ((), ())), preferred_element_type=jnp.float32
            )

        ahead = score(0)
        for h in range(heads):
            scores = ahead
            if h + 1 < heads:
                ahead = score(h + 1)
            if masked:
                scores = jnp.where(visible, scores, MASKED)
            old = maxes[h]
            if last:
                old = jnp.where(later, MASKED, old)
            new = jnp.maximum(old, jnp.max(scores, axis=0, keepdims=True))
            scaled = new * EXP2_SCALE
            weights = jnp.exp2(scores * EXP2_SCALE - scaled).astype(jnp.bfloat16)
            factor = jnp.exp2(old * EXP2_SCALE - scaled)
            product = jnp.dot(turned, weights, preferred_element_type=jnp.float32)
            total = sums[h] * factor + product
            if last:
                result = total[:HD] / total[HD : HD + 1]
                out[:, h * HD : (h + 1) * HD] = result.T.astype(out.dtype)
            else:
                maxes[h] = new
                sums[h] = total

    @pl.when(first_tile < diagonal)
    def _():
        step(first_tile, True, False)

    def middle(index, carry):
        step(index, False, False)
        return carry

    lax.fori_loop(first_tile + 1, diagonal, middle, 0)
    step(diagonal, True, True)


def attend(arrived, window, slots, doc_lengths, shard, chunk, chunks, result, shard_rows):
    block_rows, width = arrived.shape[1:]
    blocks = shard_rows // block_rows
    if block_rows % 16:
        arrived = jnp.take(arrived, slots, axis=0).reshape(shard_rows // 16, 16, width)
        block_rows, blocks = 16, shard_rows // 16
        slots = jnp.arange(blocks, dtype=jnp.int32)
    heads = width // HD
    key_heads = window.shape[1] // 2 // HD
    per_key = window.shape[0]
    aliased = [] if result is None else [result]
    return pl.pallas_call(
        functools.partial(attend_kernel, doc_lengths.shape[0], heads, shard_rows),
        out_shape=jax.ShapeDtypeStruct((shard_rows, chunks * width), arrived.dtype),
        grid_spec=pltpu.PrefetchScalarGridSpec(
            num_scalar_prefetch=3,
            grid=(1,),
            in_specs=[
                ANY,
                pl.BlockSpec((per_key, HD), lambda i, *_: (0, chunk)),
                pl.BlockSpec((per_key, HD), lambda i, *_: (0, key_heads + chunk)),
            ]
            + [ANY] * len(aliased),
            out_specs=pl.BlockSpec((shard_rows, width), lambda i, *_: (0, chunk)),
            scratch_shapes=[
                pltpu.VMEM((blocks, block_rows, width), arrived.dtype),
                pltpu.VMEM((heads, 1, shard_rows), jnp.float32),
                pltpu.VMEM((heads, HD + 16, shard_rows), jnp.float32),
                pltpu.SemaphoreType.DMA((blocks,)),
            ],
        ),
        input_output_aliases={6: 0} if aliased else {},
        compiler_params=pltpu.CompilerParams(vmem_limit_bytes=VMEM_LIMIT),
        name=f"attend{chunk}",
        cost_estimate=pl.CostEstimate(
            flops=4 * shard_rows * per_key * width,
            transcendentals=shard_rows * per_key * heads,
            bytes_accessed=4 * shard_rows * width + 4 * per_key * HD,
        ),
    )(slots, doc_lengths, shard, arrived, window, window, *aliased)


def body(query, key, value, doc_lengths, block_place):
    ctx_count = lax.axis_size("ctx")
    head_count = lax.axis_size("head")
    loaded_rows = query.shape[0]
    shard_rows = loaded_rows * head_count
    block_rows = shard_rows // ctx_count
    per_loader = loaded_rows // block_rows
    shard_blocks = shard_rows // block_rows
    shard = lax.axis_index("ctx").astype(jnp.int32)
    group = lax.axis_index("head").astype(jnp.int32)
    loader = shard * head_count + group
    slots = ctx_count * head_count
    chunks = key.shape[1] // head_count // HD
    sends, own, other = pack(
        query, key, value, block_place, loader, shard_blocks, slots, chunks
    )
    swapped = lax.ppermute(other, "head", [(0, 1), (1, 0)])
    gathered = lax.all_gather(jnp.concatenate([own, swapped]), "ctx", tiled=True)
    arrived = [
        lax.all_to_all(send, ("ctx", "head"), split_axis=0, concat_axis=0, tiled=True)
        for send in sends
    ]
    wanted = (shard - SPAN) * shard_blocks + jnp.arange((SPAN + 1) * shard_blocks, dtype=jnp.int32)
    wanted = jnp.maximum(wanted, 0)
    places = jnp.arange(block_place.shape[0], dtype=jnp.int32)
    inverse = jnp.sum(jnp.where(wanted[:, None] == block_place[None, :], places[None, :], 0), axis=1)
    source = inverse // per_loader
    sources = (
        source // head_count * (head_count * per_loader)
        + inverse % per_loader
        + jnp.where(source % head_count == group, 0, per_loader)
    )
    width = gathered.shape[1]
    window = pick_window(sources, gathered.reshape(-1, block_rows, width))
    window = window.reshape((SPAN + 1) * shard_rows, width)
    result = None
    for chunk in range(chunks):
        result = attend(
            arrived[chunk],
            window,
            source[SPAN * shard_blocks :],
            doc_lengths,
            shard[None],
            chunk,
            chunks,
            result,
            shard_rows,
        )
    return result


def solution(mesh):
    placed = (
        P(("ctx", "head"), None),
        P(("ctx", "head"), None),
        P(("ctx", "head"), None),
        P(),
        P(),
    )
    return jax.shard_map(
        body, mesh=mesh, in_specs=placed, out_specs=P("ctx", "head"), check_vma=False
    )
```

```python
import functools

import jax
import jax.numpy as jnp
import numpy as np
from jax import lax
from jax.experimental import pallas as pl
from jax.experimental.pallas import tpu as pltpu
from jax.sharding import PartitionSpec as P

HD = 128
SPAN = 8
MASKED = -1e30
EXP2_SCALE = float(HD ** (-0.5) * np.log2(np.e))
VMEM_LIMIT = 48 * 1024 * 1024
ANY = pl.BlockSpec(memory_space=pl.ANY)


def pack_query_kernel(chunks, place_ref, loader_ref, query, *refs):
    outs, sems = refs[:chunks], refs[chunks]
    per_loader = query.shape[0]
    width = outs[0].shape[2]
    copies = []
    for chunk in range(chunks):
        for j in range(per_loader):
            target = place_ref[loader_ref[0] * per_loader + j] // loader_ref[1]
            for side in range(2):
                copy = pltpu.make_async_copy(
                    query.at[j, :, pl.ds((side * chunks + chunk) * width, width)],
                    outs[chunk].at[target * 2 + side],
                    sems.at[len(copies)],
                )
                copy.start()
                copies.append(copy)
    for copy in copies:
        copy.wait()


def pack_pair_kernel(place_ref, loader_ref, key, value, out, sems):
    per_loader = key.shape[0]
    half = key.shape[2] // 2
    copies = []
    for j in range(per_loader):
        target = place_ref[loader_ref[0] * per_loader + j] // loader_ref[1]
        for side in range(2):
            for at, source in enumerate((key, value)):
                copy = pltpu.make_async_copy(
                    source.at[j, :, pl.ds(side * half, half)],
                    out.at[target * 2 + side, :, pl.ds(at * half, half)],
                    sems.at[len(copies)],
                )
                copy.start()
                copies.append(copy)
    for copy in copies:
        copy.wait()


def whole(shape):
    return pl.BlockSpec(shape, lambda i, *_: (0,) * len(shape))


def call(kernel, scalars, arrays, in_specs, outs, out_specs, scratch, name, **more):
    return pl.pallas_call(
        kernel,
        out_shape=outs,
        grid_spec=pltpu.PrefetchScalarGridSpec(
            num_scalar_prefetch=len(scalars),
            grid=(1,),
            in_specs=in_specs,
            out_specs=out_specs,
            scratch_shapes=scratch,
        ),
        compiler_params=pltpu.CompilerParams(vmem_limit_bytes=VMEM_LIMIT),
        name=name,
        **more,
    )(*scalars, *arrays)


def moved(count):
    return pl.CostEstimate(flops=0, transcendentals=0, bytes_accessed=count)


def pick_for_targets(blocks, block_place, loader, shard_blocks, shards):
    per_loader = blocks.shape[0]
    assigned = lax.dynamic_slice_in_dim(block_place, loader * per_loader, per_loader)
    matched = (assigned // shard_blocks)[None, :] == jnp.arange(shards, dtype=jnp.int32)[:, None]
    return jnp.take(blocks, jnp.argmax(matched, axis=1), axis=0)


def pack_query(query, block_place, loader, shard_blocks, slots, chunks):
    rows, columns = query.shape
    per_loader = block_place.shape[0] // slots
    block_rows = rows // per_loader
    width = columns // 2 // chunks
    blocks = query.reshape(per_loader, block_rows, columns)
    if block_rows % 16:
        picked = pick_for_targets(blocks, block_place, loader, shard_blocks, slots // 2)
        picked = picked.reshape(slots // 2, block_rows, 2, chunks, width)
        return [
            jnp.swapaxes(picked[:, :, :, chunk], 1, 2).reshape(slots, block_rows, width)
            for chunk in range(chunks)
        ]
    return call(
        functools.partial(pack_query_kernel, chunks),
        (block_place, jnp.stack([loader, jnp.int32(shard_blocks)])),
        (blocks,),
        [whole(blocks.shape)],
        [jax.ShapeDtypeStruct((slots, block_rows, width), query.dtype)] * chunks,
        [ANY] * chunks,
        [pltpu.SemaphoreType.DMA((2 * chunks * per_loader,))],
        "pack_query",
        cost_estimate=moved(4 * rows * columns),
    )


def pack_pair(key, value, block_place, loader, shard_blocks, slots):
    rows, columns = key.shape
    per_loader = block_place.shape[0] // slots
    block_rows = rows // per_loader
    keys, values = (x.reshape(per_loader, block_rows, columns) for x in (key, value))
    if block_rows % 16:
        both = jnp.stack([keys, values], axis=2).reshape(
            per_loader, block_rows, 2, 2, columns // 2
        )
        picked = pick_for_targets(both, block_place, loader, shard_blocks, slots // 2)
        return jnp.transpose(picked, (0, 3, 1, 2, 4)).reshape(slots, block_rows, columns)
    return call(
        pack_pair_kernel,
        (block_place, jnp.stack([loader, jnp.int32(shard_blocks)])),
        (keys, values),
        [whole(keys.shape)] * 2,
        jax.ShapeDtypeStruct((slots, block_rows, columns), key.dtype),
        ANY,
        [pltpu.SemaphoreType.DMA((4 * per_loader,))],
        "pack_pair",
        cost_estimate=moved(8 * rows * columns),
    )


def pick_kernel(rows_ref, blocks, out, sem):
    copies = []
    for i in range(out.shape[0]):
        copy = pltpu.make_async_copy(blocks.at[rows_ref[i]], out.at[i], sem.at[i])
        copy.start()
        copies.append(copy)
    for copy in copies:
        copy.wait()


def pick_unit(arrived, sources):
    count = sources.shape[0]
    block_rows, width = arrived.shape[1:]
    if block_rows % 16:
        unit = jnp.take(arrived, sources, axis=0)
    else:
        shape = (count, block_rows, width)
        unit = call(
            pick_kernel,
            (sources,),
            (arrived,),
            [ANY],
            jax.ShapeDtypeStruct(shape, arrived.dtype),
            whole(shape),
            [pltpu.SemaphoreType.DMA((count,))],
            "pick_unit",
            cost_estimate=moved(4 * count * block_rows * width),
        )
    return unit.reshape(count * block_rows, width)


def window_kernel(places_ref, *refs):
    units, out, sem = refs[:-2], refs[-2], refs[-1]
    copies = []
    for at, unit in enumerate(units):
        copy = pltpu.make_async_copy(unit, out.at[places_ref[at]], sem.at[at])
        copy.start()
        copies.append(copy)
    for copy in copies:
        copy.wait()


def spread(unit, shard):
    shards = lax.axis_size("ctx")
    plane = SPAN // 2
    place = shard % plane

    def forward(x):
        return lax.ppermute(x, "ctx", [(s, s + plane) for s in range(shards - plane)])

    before = forward(unit)
    oldest = forward(before)
    units = [unit, before, oldest]
    places = [jnp.int32(SPAN), jnp.int32(plane), jnp.int32(0)]
    sent = {}
    for mask in range(1, plane):
        partner = place ^ mask
        lower = place < partner
        bit = mask.bit_length()
        if bit not in sent:
            sent[bit] = jnp.where(lower, unit, oldest)
        route = [(s, s ^ mask) for s in range(shards)]
        units.append(lax.ppermute(before, "ctx", route))
        places.append(plane - place + partner)
        units.append(lax.ppermute(sent[bit], "ctx", route))
        places.append(jnp.where(lower, 0, SPAN) - place + partner)
    shape = (SPAN + 1,) + unit.shape
    window = call(
        window_kernel,
        (jnp.stack(places).astype(jnp.int32),),
        units,
        [ANY] * len(units),
        jax.ShapeDtypeStruct(shape, unit.dtype),
        whole(shape),
        [pltpu.SemaphoreType.DMA((len(units),))],
        "window",
        cost_estimate=moved(4 * (SPAN + 1) * unit.shape[0] * unit.shape[1]),
    )
    return window.reshape((SPAN + 1) * unit.shape[0], unit.shape[1])


def attend_kernel(
    docs, heads, tile, slot_ref, lengths_ref, shard_ref, *refs
):
    arrived, keys, values = refs[0], refs[1], refs[2]
    out, queries, maxes, sums, sem = refs[-5:]
    blocks, block_rows, width = queries.shape
    rows = blocks * block_rows
    copies = []
    for i in range(blocks):
        copy = pltpu.make_async_copy(arrived.at[slot_ref[i]], queries.at[i], sem.at[i])
        copy.start()
        copies.append(copy)
    first_row = shard_ref[0] * rows
    query_rows = first_row + lax.broadcasted_iota(jnp.int32, (1, rows), 1)
    starts = jnp.zeros((1, rows), jnp.int32)
    first_start = jnp.int32(0)
    end = jnp.int32(0)
    for d in range(docs):
        length = lengths_ref[d]
        end = end + length
        starts = starts + jnp.where(query_rows >= end, length, 0)
        first_start = first_start + jnp.where(first_row >= end, length, 0)
    tiles = keys.shape[0] // tile
    window_start = first_row + rows - keys.shape[0]
    diagonal = tiles - 1
    first_tile = (first_start - window_start) // tile
    for h in range(heads):
        maxes[h] = jnp.full((1, rows), MASKED, jnp.float32)
        sums[h] = jnp.zeros(sums.shape[1:], jnp.float32)
    for copy in copies:
        copy.wait()

    def step(index, masked, last):
        span = pl.ds(pl.multiple_of(index * tile, tile), tile)
        tile_keys = keys[span, :]
        tile_values = values[span, :]
        extended = jnp.concatenate([tile_values, jnp.ones((tile, HD), tile_values.dtype)], axis=1)
        turned = extended.T[: HD + 16]
        if masked:
            key_rows = window_start + index * tile + lax.broadcasted_iota(jnp.int32, (tile, rows), 0)
            visible = (key_rows >= starts) & (key_rows <= query_rows)
        if last:
            later = starts >= first_row

        def score(h):
            query = queries[:, :, h * HD : (h + 1) * HD].reshape(rows, HD)
            return lax.dot_general(
                tile_keys, query, (((1,), (1,)), ((), ())), preferred_element_type=jnp.float32
            )

        ahead = score(0)
        for h in range(heads):
            scores = ahead
            if h + 1 < heads:
                ahead = score(h + 1)
            if masked:
                scores = jnp.where(visible, scores, MASKED)
            old = maxes[h]
            if last:
                old = jnp.where(later, MASKED, old)
            new = jnp.maximum(old, jnp.max(scores, axis=0, keepdims=True))
            scaled = new * EXP2_SCALE
            weights = jnp.exp2(scores * EXP2_SCALE - scaled).astype(jnp.bfloat16)
            factor = jnp.exp2(old * EXP2_SCALE - scaled)
            product = jnp.dot(turned, weights, preferred_element_type=jnp.float32)
            total = sums[h] * factor + product
            if last:
                result = total[:HD] / total[HD : HD + 1]
                out[:, h * HD : (h + 1) * HD] = result.T.astype(out.dtype)
            else:
                maxes[h] = new
                sums[h] = total

    @pl.when(first_tile < diagonal)
    def _():
        step(first_tile, True, False)

    def middle(index, carry):
        step(index, False, False)
        return carry

    lax.fori_loop(first_tile + 1, diagonal, middle, 0)
    step(diagonal, True, True)


def attend(arrived, window, slots, doc_lengths, shard, chunk, chunks, result, shard_rows):
    block_rows, width = arrived.shape[1:]
    blocks = shard_rows // block_rows
    if block_rows % 16:
        arrived = jnp.take(arrived, slots, axis=0).reshape(shard_rows // 16, 16, width)
        block_rows, blocks = 16, shard_rows // 16
        slots = jnp.arange(blocks, dtype=jnp.int32)
    heads = width // HD
    key_heads = window.shape[1] // 2 // HD
    per_key = window.shape[0]
    aliased = [] if result is None else [result]
    return pl.pallas_call(
        functools.partial(attend_kernel, doc_lengths.shape[0], heads, shard_rows),
        out_shape=jax.ShapeDtypeStruct((shard_rows, chunks * width), arrived.dtype),
        grid_spec=pltpu.PrefetchScalarGridSpec(
            num_scalar_prefetch=3,
            grid=(1,),
            in_specs=[
                ANY,
                pl.BlockSpec((per_key, HD), lambda i, *_: (0, chunk)),
                pl.BlockSpec((per_key, HD), lambda i, *_: (0, key_heads + chunk)),
            ]
            + [ANY] * len(aliased),
            out_specs=pl.BlockSpec((shard_rows, width), lambda i, *_: (0, chunk)),
            scratch_shapes=[
                pltpu.VMEM((blocks, block_rows, width), arrived.dtype),
                pltpu.VMEM((heads, 1, shard_rows), jnp.float32),
                pltpu.VMEM((heads, HD + 16, shard_rows), jnp.float32),
                pltpu.SemaphoreType.DMA((blocks,)),
            ],
        ),
        input_output_aliases={6: 0} if aliased else {},
        compiler_params=pltpu.CompilerParams(vmem_limit_bytes=VMEM_LIMIT),
        name=f"attend{chunk}",
        cost_estimate=pl.CostEstimate(
            flops=4 * shard_rows * per_key * width,
            transcendentals=shard_rows * per_key * heads,
            bytes_accessed=4 * shard_rows * width + 4 * per_key * HD,
        ),
    )(slots, doc_lengths, shard, arrived, window, window, *aliased)


def body(query, key, value, doc_lengths, block_place):
    ctx_count = lax.axis_size("ctx")
    head_count = lax.axis_size("head")
    loaded_rows = query.shape[0]
    shard_rows = loaded_rows * head_count
    block_rows = shard_rows // ctx_count
    per_loader = loaded_rows // block_rows
    shard_blocks = shard_rows // block_rows
    shard = lax.axis_index("ctx").astype(jnp.int32)
    group = lax.axis_index("head").astype(jnp.int32)
    loader = shard * head_count + group
    slots = ctx_count * head_count
    chunks = key.shape[1] // head_count // HD
    def exchange(sends):
        return lax.all_to_all(sends, ("ctx", "head"), split_axis=0, concat_axis=0, tiled=True)

    pair = exchange(pack_pair(key, value, block_place, loader, shard_blocks, slots))
    sends = pack_query(query, block_place, loader, shard_blocks, slots, chunks)
    arrived = [exchange(send) for send in sends]
    wanted = shard * shard_blocks + jnp.arange(shard_blocks, dtype=jnp.int32)
    places = jnp.arange(block_place.shape[0], dtype=jnp.int32)
    inverse = jnp.sum(jnp.where(wanted[:, None] == block_place[None, :], places[None, :], 0), axis=1)
    sources = inverse // per_loader
    window = spread(pick_unit(pair, sources), shard)
    result = None
    for chunk in range(chunks):
        result = attend(
            arrived[chunk],
            window,
            sources,
            doc_lengths,
            shard[None],
            chunk,
            chunks,
            result,
            shard_rows,
        )
    return result


def solution(mesh):
    placed = (
        P(("ctx", "head"), None),
        P(("ctx", "head"), None),
        P(("ctx", "head"), None),
        P(),
        P(),
    )
    return jax.shard_map(
        body, mesh=mesh, in_specs=placed, out_specs=P("ctx", "head"), check_vma=False
    )
```

```python
import functools

import jax
import jax.numpy as jnp
import numpy as np
from jax import lax
from jax.experimental import pallas as pl
from jax.experimental.pallas import tpu as pltpu
from jax.sharding import PartitionSpec as P

HD = 128
SPAN = 8
MASKED = -1e30
EXP2_SCALE = float(HD ** (-0.5) * np.log2(np.e))
VMEM_LIMIT = 60 * 1024 * 1024
ANY = pl.BlockSpec(memory_space=pl.ANY)


def pack_query_kernel(chunks, place_ref, loader_ref, query, *refs):
    outs, sems = refs[:chunks], refs[chunks]
    per_loader = query.shape[0]
    width = outs[0].shape[2]
    copies = []
    for chunk in range(chunks):
        for j in range(per_loader):
            target = place_ref[loader_ref[0] * per_loader + j] // loader_ref[1]
            for side in range(2):
                copy = pltpu.make_async_copy(
                    query.at[j, :, pl.ds((side * chunks + chunk) * width, width)],
                    outs[chunk].at[target * 2 + side],
                    sems.at[len(copies)],
                )
                copy.start()
                copies.append(copy)
    for copy in copies:
        copy.wait()


def pack_pair_kernel(place_ref, loader_ref, key, value, out, sems):
    per_loader = key.shape[0]
    half = key.shape[2] // 2
    copies = []
    for j in range(per_loader):
        target = place_ref[loader_ref[0] * per_loader + j] // loader_ref[1]
        for side in range(2):
            for at, source in enumerate((key, value)):
                copy = pltpu.make_async_copy(
                    source.at[j, :, pl.ds(side * half, half)],
                    out.at[target * 2 + side, :, pl.ds(at * half, half)],
                    sems.at[len(copies)],
                )
                copy.start()
                copies.append(copy)
    for copy in copies:
        copy.wait()


def whole(shape):
    return pl.BlockSpec(shape, lambda i, *_: (0,) * len(shape))


def call(kernel, scalars, arrays, in_specs, outs, out_specs, scratch, name, **more):
    return pl.pallas_call(
        kernel,
        out_shape=outs,
        grid_spec=pltpu.PrefetchScalarGridSpec(
            num_scalar_prefetch=len(scalars),
            grid=(1,),
            in_specs=in_specs,
            out_specs=out_specs,
            scratch_shapes=scratch,
        ),
        compiler_params=pltpu.CompilerParams(vmem_limit_bytes=VMEM_LIMIT),
        name=name,
        **more,
    )(*scalars, *arrays)


def moved(count):
    return pl.CostEstimate(flops=0, transcendentals=0, bytes_accessed=count)


def pick_for_targets(blocks, block_place, loader, shard_blocks, shards):
    per_loader = blocks.shape[0]
    assigned = lax.dynamic_slice_in_dim(block_place, loader * per_loader, per_loader)
    matched = (assigned // shard_blocks)[None, :] == jnp.arange(shards, dtype=jnp.int32)[:, None]
    return jnp.take(blocks, jnp.argmax(matched, axis=1), axis=0)


def pack_query(query, block_place, loader, shard_blocks, slots, chunks):
    rows, columns = query.shape
    per_loader = block_place.shape[0] // slots
    block_rows = rows // per_loader
    width = columns // 2 // chunks
    blocks = query.reshape(per_loader, block_rows, columns)
    if block_rows % 16:
        picked = pick_for_targets(blocks, block_place, loader, shard_blocks, slots // 2)
        picked = picked.reshape(slots // 2, block_rows, 2, chunks, width)
        return [
            jnp.swapaxes(picked[:, :, :, chunk], 1, 2).reshape(slots, block_rows, width)
            for chunk in range(chunks)
        ]
    return call(
        functools.partial(pack_query_kernel, chunks),
        (block_place, jnp.stack([loader, jnp.int32(shard_blocks)])),
        (blocks,),
        [whole(blocks.shape)],
        [jax.ShapeDtypeStruct((slots, block_rows, width), query.dtype)] * chunks,
        [ANY] * chunks,
        [pltpu.SemaphoreType.DMA((2 * chunks * per_loader,))],
        "pack_query",
        cost_estimate=moved(4 * rows * columns),
    )


def pack_pair(key, value, block_place, loader, shard_blocks, slots):
    rows, columns = key.shape
    per_loader = block_place.shape[0] // slots
    block_rows = rows // per_loader
    keys, values = (x.reshape(per_loader, block_rows, columns) for x in (key, value))
    if block_rows % 16:
        both = jnp.stack([keys, values], axis=2).reshape(
            per_loader, block_rows, 2, 2, columns // 2
        )
        picked = pick_for_targets(both, block_place, loader, shard_blocks, slots // 2)
        return jnp.transpose(picked, (0, 3, 1, 2, 4)).reshape(slots, block_rows, columns)
    return call(
        pack_pair_kernel,
        (block_place, jnp.stack([loader, jnp.int32(shard_blocks)])),
        (keys, values),
        [whole(keys.shape)] * 2,
        jax.ShapeDtypeStruct((slots, block_rows, columns), key.dtype),
        ANY,
        [pltpu.SemaphoreType.DMA((4 * per_loader,))],
        "pack_pair",
        cost_estimate=moved(8 * rows * columns),
    )


def pick_kernel(rows_ref, blocks, out, sem):
    copies = []
    for i in range(out.shape[0]):
        copy = pltpu.make_async_copy(blocks.at[rows_ref[i]], out.at[i], sem.at[i])
        copy.start()
        copies.append(copy)
    for copy in copies:
        copy.wait()


def pick_unit(arrived, sources):
    count = sources.shape[0]
    block_rows, width = arrived.shape[1:]
    if block_rows % 16:
        unit = jnp.take(arrived, sources, axis=0)
    else:
        shape = (count, block_rows, width)
        unit = call(
            pick_kernel,
            (sources,),
            (arrived,),
            [ANY],
            jax.ShapeDtypeStruct(shape, arrived.dtype),
            whole(shape),
            [pltpu.SemaphoreType.DMA((count,))],
            "pick_unit",
            cost_estimate=moved(4 * count * block_rows * width),
        )
    return unit.reshape(count * block_rows, width)


def spread(unit, shard):
    shards = lax.axis_size("ctx")
    plane = SPAN // 2
    place = shard % plane

    def forward(x):
        return lax.ppermute(x, "ctx", [(s, s + plane) for s in range(shards - plane)])

    before = forward(unit)
    oldest = forward(before)
    units = [unit, before, oldest]
    places = [jnp.int32(SPAN), jnp.int32(plane), jnp.int32(0)]
    sent = {}
    for mask in range(1, plane):
        partner = place ^ mask
        lower = place < partner
        bit = mask.bit_length()
        if bit not in sent:
            sent[bit] = jnp.where(lower, unit, oldest)
        route = [(s, s ^ mask) for s in range(shards)]
        units.append(lax.ppermute(before, "ctx", route))
        places.append(plane - place + partner)
        units.append(lax.ppermute(sent[bit], "ctx", route))
        places.append(jnp.where(lower, 0, SPAN) - place + partner)
    return units, jnp.stack(places).astype(jnp.int32)


def attend_kernel(chunk, docs, heads, slot_ref, lengths_ref, shard_ref, places_ref, *refs):
    arrived, units = refs[0], refs[1 : SPAN + 2]
    out, queries, keys, values, maxes, sums, sem, key_sem = refs[-8:]
    blocks, block_rows, width = queries.shape
    rows = blocks * block_rows
    tiles, tile = keys.shape[:2]
    copies = []
    for i in range(blocks):
        copy = pltpu.make_async_copy(arrived.at[slot_ref[i]], queries.at[i], sem.at[i])
        copy.start()
        copies.append(copy)
    half = units[0].shape[1] // 2

    def fetch(unit, at, which):
        target = (keys, values)[which]
        columns = pl.ds(which * half + chunk * HD, HD)
        return pltpu.make_async_copy(unit.at[:, columns], target.at[at], key_sem.at[which, at])

    for unit, ref in enumerate(units):
        for which in range(2):
            fetch(ref, places_ref[unit], which).start()
    first_row = shard_ref[0] * rows
    query_rows = first_row + lax.broadcasted_iota(jnp.int32, (1, rows), 1)
    starts = jnp.zeros((1, rows), jnp.int32)
    first_start = jnp.int32(0)
    end = jnp.int32(0)
    for d in range(docs):
        length = lengths_ref[d]
        end = end + length
        starts = starts + jnp.where(query_rows >= end, length, 0)
        first_start = first_start + jnp.where(first_row >= end, length, 0)
    window_start = first_row + rows - tiles * tile
    diagonal = tiles - 1
    first_tile = (first_start - window_start) // tile
    for h in range(heads):
        maxes[h] = jnp.full((1, rows), MASKED, jnp.float32)
        sums[h] = jnp.zeros(sums.shape[1:], jnp.float32)
    for copy in copies:
        copy.wait()

    def landed(index):
        for which in range(2):
            fetch(units[0], index, which).wait()

    def unused(index, carry):
        landed(index)
        return carry

    lax.fori_loop(0, first_tile, unused, 0)

    def step(index, masked, last):
        landed(index)
        tile_keys = keys[index]
        tile_values = values[index]
        extended = jnp.concatenate([tile_values, jnp.ones((tile, HD), tile_values.dtype)], axis=1)
        turned = extended.T[: HD + 16]
        if masked:
            key_rows = window_start + index * tile + lax.broadcasted_iota(jnp.int32, (tile, rows), 0)
            visible = (key_rows >= starts) & (key_rows <= query_rows)
        if last:
            later = starts >= first_row

        def score(h):
            query = queries[:, :, h * HD : (h + 1) * HD].reshape(rows, HD)
            return lax.dot_general(
                tile_keys, query, (((1,), (1,)), ((), ())), preferred_element_type=jnp.float32
            )

        ahead = score(0)
        for h in range(heads):
            scores = ahead
            if h + 1 < heads:
                ahead = score(h + 1)
            if masked:
                scores = jnp.where(visible, scores, MASKED)
            old = maxes[h]
            if last:
                old = jnp.where(later, MASKED, old)
            new = jnp.maximum(old, jnp.max(scores, axis=0, keepdims=True))
            scaled = new * EXP2_SCALE
            weights = jnp.exp2(scores * EXP2_SCALE - scaled).astype(jnp.bfloat16)
            factor = jnp.exp2(old * EXP2_SCALE - scaled)
            product = jnp.dot(turned, weights, preferred_element_type=jnp.float32)
            total = sums[h] * factor + product
            if last:
                result = total[:HD] / total[HD : HD + 1]
                out[:, h * HD : (h + 1) * HD] = result.T.astype(out.dtype)
            else:
                maxes[h] = new
                sums[h] = total

    @pl.when(first_tile < diagonal)
    def _():
        step(first_tile, True, False)

    def middle(index, carry):
        step(index, False, False)
        return carry

    lax.fori_loop(first_tile + 1, diagonal, middle, 0)
    step(diagonal, True, True)


def attend(arrived, units, places, slots, doc_lengths, shard, chunk, chunks, result):
    block_rows, width = arrived.shape[1:]
    shard_rows = units[0].shape[0]
    blocks = shard_rows // block_rows
    if block_rows % 16:
        arrived = jnp.take(arrived, slots, axis=0).reshape(shard_rows // 16, 16, width)
        block_rows, blocks = 16, shard_rows // 16
        slots = jnp.arange(blocks, dtype=jnp.int32)
    heads = width // HD
    tiles = len(units)
    aliased = [] if result is None else [result]
    scalars = (slots, doc_lengths, shard, places)
    arrays = (arrived, *units, *aliased)
    return call(
        functools.partial(attend_kernel, chunk, doc_lengths.shape[0], heads),
        scalars,
        arrays,
        [ANY] * len(arrays),
        jax.ShapeDtypeStruct((shard_rows, chunks * width), arrived.dtype),
        pl.BlockSpec((shard_rows, width), lambda i, *_: (0, chunk)),
        [
            pltpu.VMEM((blocks, block_rows, width), arrived.dtype),
            pltpu.VMEM((tiles, shard_rows, HD), arrived.dtype),
            pltpu.VMEM((tiles, shard_rows, HD), arrived.dtype),
            pltpu.VMEM((heads, 1, shard_rows), jnp.float32),
            pltpu.VMEM((heads, HD + 16, shard_rows), jnp.float32),
            pltpu.SemaphoreType.DMA((blocks,)),
            pltpu.SemaphoreType.DMA((2, tiles)),
        ],
        f"attend{chunk}",
        input_output_aliases={len(scalars) + len(arrays) - 1: 0} if aliased else {},
        cost_estimate=pl.CostEstimate(
            flops=4 * shard_rows * shard_rows * tiles * width,
            transcendentals=shard_rows * shard_rows * tiles * heads,
            bytes_accessed=4 * shard_rows * (width + tiles * HD),
        ),
    )


def body(query, key, value, doc_lengths, block_place):
    ctx_count = lax.axis_size("ctx")
    head_count = lax.axis_size("head")
    loaded_rows = query.shape[0]
    shard_rows = loaded_rows * head_count
    block_rows = shard_rows // ctx_count
    per_loader = loaded_rows // block_rows
    shard_blocks = shard_rows // block_rows
    shard = lax.axis_index("ctx").astype(jnp.int32)
    group = lax.axis_index("head").astype(jnp.int32)
    loader = shard * head_count + group
    slots = ctx_count * head_count
    chunks = key.shape[1] // head_count // HD
    def exchange(sends):
        return lax.all_to_all(sends, ("ctx", "head"), split_axis=0, concat_axis=0, tiled=True)

    pair = exchange(pack_pair(key, value, block_place, loader, shard_blocks, slots))
    sends = list(pack_query(query, block_place, loader, shard_blocks, slots, chunks))
    wanted = shard * shard_blocks + jnp.arange(shard_blocks, dtype=jnp.int32)
    places = jnp.arange(block_place.shape[0], dtype=jnp.int32)
    inverse = jnp.sum(jnp.where(wanted[:, None] == block_place[None, :], places[None, :], 0), axis=1)
    sources = inverse // per_loader
    unit = pick_unit(pair, sources)
    sends[0], unit = lax.optimization_barrier((sends[0], unit))
    units, unit_places = spread(unit, shard)
    for chunk, stage in ((1, 1), (2, 2), (3, 2)):
        if chunk < chunks:
            sends[chunk], units[stage] = lax.optimization_barrier((sends[chunk], units[stage]))
    arrived = [exchange(send) for send in sends]
    result = None
    for chunk in range(chunks):
        result = attend(
            arrived[chunk],
            units,
            unit_places,
            sources,
            doc_lengths,
            shard[None],
            chunk,
            chunks,
            result,
        )
    return result


def solution(mesh):
    placed = (
        P(("ctx", "head"), None),
        P(("ctx", "head"), None),
        P(("ctx", "head"), None),
        P(),
        P(),
    )
    return jax.shard_map(
        body, mesh=mesh, in_specs=placed, out_specs=P("ctx", "head"), check_vma=False
    )
```

```python
import functools

import jax
import jax.numpy as jnp
import numpy as np
from jax import lax
from jax.experimental import pallas as pl
from jax.experimental.pallas import tpu as pltpu
from jax.sharding import PartitionSpec as P

HD = 128
SPAN = 8
MASKED = -1e30
EXP2_SCALE = float(HD ** (-0.5) * np.log2(np.e))
VMEM_LIMIT = 60 * 1024 * 1024
ANY = pl.BlockSpec(memory_space=pl.ANY)


def pack_query_kernel(chunks, place_ref, loader_ref, query, *refs):
    outs, sems = refs[:chunks], refs[chunks]
    per_loader = query.shape[0]
    width = outs[0].shape[2]
    copies = []
    for chunk in range(chunks):
        for j in range(per_loader):
            target = place_ref[loader_ref[0] * per_loader + j] // loader_ref[1]
            for side in range(2):
                copy = pltpu.make_async_copy(
                    query.at[j, :, pl.ds((side * chunks + chunk) * width, width)],
                    outs[chunk].at[target * 2 + side],
                    sems.at[len(copies)],
                )
                copy.start()
                copies.append(copy)
    for copy in copies:
        copy.wait()


def pack_pair_kernel(place_ref, loader_ref, key, value, out, sems):
    per_loader = key.shape[0]
    half = key.shape[2] // 2
    copies = []
    for j in range(per_loader):
        target = place_ref[loader_ref[0] * per_loader + j] // loader_ref[1]
        for side in range(2):
            for at, source in enumerate((key, value)):
                copy = pltpu.make_async_copy(
                    source.at[j, :, pl.ds(side * half, half)],
                    out.at[target * 2 + side, :, pl.ds(at * half, half)],
                    sems.at[len(copies)],
                )
                copy.start()
                copies.append(copy)
    for copy in copies:
        copy.wait()


def whole(shape):
    return pl.BlockSpec(shape, lambda i, *_: (0,) * len(shape))


def call(kernel, scalars, arrays, in_specs, outs, out_specs, scratch, name, **more):
    return pl.pallas_call(
        kernel,
        out_shape=outs,
        grid_spec=pltpu.PrefetchScalarGridSpec(
            num_scalar_prefetch=len(scalars),
            grid=(1,),
            in_specs=in_specs,
            out_specs=out_specs,
            scratch_shapes=scratch,
        ),
        compiler_params=pltpu.CompilerParams(vmem_limit_bytes=VMEM_LIMIT),
        name=name,
        **more,
    )(*scalars, *arrays)


def moved(count):
    return pl.CostEstimate(flops=0, transcendentals=0, bytes_accessed=count)


def pick_for_targets(blocks, block_place, loader, shard_blocks, shards):
    per_loader = blocks.shape[0]
    assigned = lax.dynamic_slice_in_dim(block_place, loader * per_loader, per_loader)
    matched = (assigned // shard_blocks)[None, :] == jnp.arange(shards, dtype=jnp.int32)[:, None]
    return jnp.take(blocks, jnp.argmax(matched, axis=1), axis=0)


def pack_query(query, block_place, loader, shard_blocks, slots, chunks):
    rows, columns = query.shape
    per_loader = block_place.shape[0] // slots
    block_rows = rows // per_loader
    width = columns // 2 // chunks
    blocks = query.reshape(per_loader, block_rows, columns)
    if block_rows % 16:
        picked = pick_for_targets(blocks, block_place, loader, shard_blocks, slots // 2)
        picked = picked.reshape(slots // 2, block_rows, 2, chunks, width)
        return [
            jnp.swapaxes(picked[:, :, :, chunk], 1, 2).reshape(slots, block_rows, width)
            for chunk in range(chunks)
        ]
    return call(
        functools.partial(pack_query_kernel, chunks),
        (block_place, jnp.stack([loader, jnp.int32(shard_blocks)])),
        (blocks,),
        [whole(blocks.shape)],
        [jax.ShapeDtypeStruct((slots, block_rows, width), query.dtype)] * chunks,
        [ANY] * chunks,
        [pltpu.SemaphoreType.DMA((2 * chunks * per_loader,))],
        "pack_query",
        cost_estimate=moved(4 * rows * columns),
    )


def pack_pair(key, value, block_place, loader, shard_blocks, slots):
    rows, columns = key.shape
    per_loader = block_place.shape[0] // slots
    block_rows = rows // per_loader
    keys, values = (x.reshape(per_loader, block_rows, columns) for x in (key, value))
    if block_rows % 16:
        both = jnp.stack([keys, values], axis=2).reshape(
            per_loader, block_rows, 2, 2, columns // 2
        )
        picked = pick_for_targets(both, block_place, loader, shard_blocks, slots // 2)
        return jnp.transpose(picked, (0, 3, 1, 2, 4)).reshape(slots, block_rows, columns)
    return call(
        pack_pair_kernel,
        (block_place, jnp.stack([loader, jnp.int32(shard_blocks)])),
        (keys, values),
        [whole(keys.shape)] * 2,
        jax.ShapeDtypeStruct((slots, block_rows, columns), key.dtype),
        ANY,
        [pltpu.SemaphoreType.DMA((4 * per_loader,))],
        "pack_pair",
        cost_estimate=moved(8 * rows * columns),
    )


def pick_kernel(rows_ref, blocks, out, sem):
    copies = []
    for i in range(out.shape[0]):
        copy = pltpu.make_async_copy(blocks.at[rows_ref[i]], out.at[i], sem.at[i])
        copy.start()
        copies.append(copy)
    for copy in copies:
        copy.wait()


def pick_unit(arrived, sources):
    count = sources.shape[0]
    block_rows, width = arrived.shape[1:]
    if block_rows % 16:
        unit = jnp.take(arrived, sources, axis=0)
    else:
        shape = (count, block_rows, width)
        unit = call(
            pick_kernel,
            (sources,),
            (arrived,),
            [ANY],
            jax.ShapeDtypeStruct(shape, arrived.dtype),
            whole(shape),
            [pltpu.SemaphoreType.DMA((count,))],
            "pick_unit",
            cost_estimate=moved(4 * count * block_rows * width),
        )
    return unit.reshape(count * block_rows, width)


def spread(unit, shard):
    shards = lax.axis_size("ctx")
    plane = SPAN // 2
    place = shard % plane

    def forward(x):
        return lax.ppermute(x, "ctx", [(s, s + plane) for s in range(shards - plane)])

    before = forward(unit)
    oldest = forward(before)
    units = [unit, before, oldest]
    places = [jnp.int32(SPAN), jnp.int32(plane), jnp.int32(0)]
    sent = {}
    stages = [[1], [2], []]
    for mask in range(1, plane):
        partner = place ^ mask
        lower = place < partner
        bit = mask.bit_length()
        if bit not in sent:
            sent[bit] = jnp.where(lower, unit, oldest)
        route = [(s, s ^ mask) for s in range(shards)]
        stages[1].append(len(units))
        units.append(lax.ppermute(before, "ctx", route))
        places.append(plane - place + partner)
        stages[2].append(len(units))
        units.append(lax.ppermute(sent[bit], "ctx", route))
        places.append(jnp.where(lower, 0, SPAN) - place + partner)
    return units, jnp.stack(places).astype(jnp.int32), stages


def attend_kernel(chunk, docs, heads, slot_ref, lengths_ref, shard_ref, places_ref, *refs):
    arrived, units = refs[0], refs[1 : SPAN + 2]
    out, queries, keys, values, maxes, sums, sem, key_sem = refs[-8:]
    blocks, block_rows, width = queries.shape
    rows = blocks * block_rows
    tiles, tile = keys.shape[:2]
    copies = []
    for i in range(blocks):
        copy = pltpu.make_async_copy(arrived.at[slot_ref[i]], queries.at[i], sem.at[i])
        copy.start()
        copies.append(copy)
    half = units[0].shape[1] // 2

    def fetch(unit, at, which):
        target = (keys, values)[which]
        columns = pl.ds(which * half + chunk * HD, HD)
        return pltpu.make_async_copy(unit.at[:, columns], target.at[at], key_sem.at[which, at])

    for unit, ref in enumerate(units):
        for which in range(2):
            fetch(ref, places_ref[unit], which).start()
    first_row = shard_ref[0] * rows
    query_rows = first_row + lax.broadcasted_iota(jnp.int32, (1, rows), 1)
    starts = jnp.zeros((1, rows), jnp.int32)
    first_start = jnp.int32(0)
    end = jnp.int32(0)
    for d in range(docs):
        length = lengths_ref[d]
        end = end + length
        starts = starts + jnp.where(query_rows >= end, length, 0)
        first_start = first_start + jnp.where(first_row >= end, length, 0)
    window_start = first_row + rows - tiles * tile
    diagonal = tiles - 1
    first_tile = (first_start - window_start) // tile
    for h in range(heads):
        maxes[h] = jnp.full((1, rows), MASKED, jnp.float32)
        sums[h] = jnp.zeros(sums.shape[1:], jnp.float32)
    for copy in copies:
        copy.wait()

    def landed(index):
        for which in range(2):
            fetch(units[0], index, which).wait()

    def unused(index, carry):
        landed(index)
        return carry

    lax.fori_loop(0, first_tile, unused, 0)

    def step(index, count, masked, last):
        for other in range(count):
            landed(index + other)
        span = count * tile
        tile_keys = keys[pl.ds(index, count)].reshape(span, HD)
        tile_values = values[pl.ds(index, count)].reshape(span, HD)
        extended = jnp.concatenate([tile_values, jnp.ones((span, HD), tile_values.dtype)], axis=1)
        turned = extended.T[: HD + 16]
        if masked:
            key_rows = window_start + index * tile + lax.broadcasted_iota(jnp.int32, (tile, rows), 0)
            visible = (key_rows >= starts) & (key_rows <= query_rows)
        if last:
            later = starts >= first_row

        def score(h):
            query = queries[:, :, h * HD : (h + 1) * HD].reshape(rows, HD)
            return lax.dot_general(
                tile_keys, query, (((1,), (1,)), ((), ())), preferred_element_type=jnp.float32
            )

        ahead = score(0)
        for h in range(heads):
            scores = ahead
            if h + 1 < heads:
                ahead = score(h + 1)
            if masked:
                scores = jnp.where(visible, scores, MASKED)
            old = maxes[h]
            if last:
                old = jnp.where(later, MASKED, old)
            new = jnp.maximum(old, jnp.max(scores, axis=0, keepdims=True))
            scaled = new * EXP2_SCALE
            weights = jnp.exp2(scores * EXP2_SCALE - scaled).astype(jnp.bfloat16)
            factor = jnp.exp2(old * EXP2_SCALE - scaled)
            product = jnp.dot(turned, weights, preferred_element_type=jnp.float32)
            total = sums[h] * factor + product
            if last:
                result = total[:HD] / total[HD : HD + 1]
                out[:, h * HD : (h + 1) * HD] = result.T.astype(out.dtype)
            else:
                maxes[h] = new
                sums[h] = total

    @pl.when(first_tile < diagonal)
    def _():
        step(first_tile, 1, True, False)

    between = jnp.maximum(diagonal - first_tile - 1, 0)

    @pl.when(between % 2 == 1)
    def _():
        step(first_tile + 1, 1, False, False)

    def middle(index, carry):
        step(first_tile + 1 + between % 2 + 2 * index, 2, False, False)
        return carry

    lax.fori_loop(0, between // 2, middle, 0)
    step(diagonal, 1, True, True)


def attend(arrived, units, places, slots, doc_lengths, shard, chunk, chunks, result):
    block_rows, width = arrived.shape[1:]
    shard_rows = units[0].shape[0]
    blocks = shard_rows // block_rows
    if block_rows % 16:
        arrived = jnp.take(arrived, slots, axis=0).reshape(shard_rows // 16, 16, width)
        block_rows, blocks = 16, shard_rows // 16
        slots = jnp.arange(blocks, dtype=jnp.int32)
    heads = width // HD
    tiles = len(units)
    aliased = [] if result is None else [result]
    scalars = (slots, doc_lengths, shard, places)
    arrays = (arrived, *units, *aliased)
    return call(
        functools.partial(attend_kernel, chunk, doc_lengths.shape[0], heads),
        scalars,
        arrays,
        [ANY] * len(arrays),
        jax.ShapeDtypeStruct((shard_rows, chunks * width), arrived.dtype),
        pl.BlockSpec((shard_rows, width), lambda i, *_: (0, chunk)),
        [
            pltpu.VMEM((blocks, block_rows, width), arrived.dtype),
            pltpu.VMEM((tiles, shard_rows, HD), arrived.dtype),
            pltpu.VMEM((tiles, shard_rows, HD), arrived.dtype),
            pltpu.VMEM((heads, 1, shard_rows), jnp.float32),
            pltpu.VMEM((heads, HD + 16, shard_rows), jnp.float32),
            pltpu.SemaphoreType.DMA((blocks,)),
            pltpu.SemaphoreType.DMA((2, tiles)),
        ],
        f"attend{chunk}",
        input_output_aliases={len(scalars) + len(arrays) - 1: 0} if aliased else {},
        cost_estimate=pl.CostEstimate(
            flops=4 * shard_rows * shard_rows * tiles * width,
            transcendentals=shard_rows * shard_rows * tiles * heads,
            bytes_accessed=4 * shard_rows * (width + tiles * HD),
        ),
    )


def body(query, key, value, doc_lengths, block_place):
    ctx_count = lax.axis_size("ctx")
    head_count = lax.axis_size("head")
    loaded_rows = query.shape[0]
    shard_rows = loaded_rows * head_count
    block_rows = shard_rows // ctx_count
    per_loader = loaded_rows // block_rows
    shard_blocks = shard_rows // block_rows
    shard = lax.axis_index("ctx").astype(jnp.int32)
    group = lax.axis_index("head").astype(jnp.int32)
    loader = shard * head_count + group
    slots = ctx_count * head_count
    chunks = key.shape[1] // head_count // HD
    def exchange(sends):
        return lax.all_to_all(sends, ("ctx", "head"), split_axis=0, concat_axis=0, tiled=True)

    pair = exchange(pack_pair(key, value, block_place, loader, shard_blocks, slots))
    sends = list(pack_query(query, block_place, loader, shard_blocks, slots, chunks))
    wanted = shard * shard_blocks + jnp.arange(shard_blocks, dtype=jnp.int32)
    places = jnp.arange(block_place.shape[0], dtype=jnp.int32)
    inverse = jnp.sum(jnp.where(wanted[:, None] == block_place[None, :], places[None, :], 0), axis=1)
    sources = inverse // per_loader
    unit = pick_unit(pair, sources)
    sends[0], unit = lax.optimization_barrier((sends[0], unit))
    units, unit_places, stages = spread(unit, shard)
    for chunk, stage in enumerate(stages[: chunks - 1]):
        held = [units[at] for at in stage]
        held, sends[chunk + 1] = lax.optimization_barrier((held, sends[chunk + 1]))
        for at, value in zip(stage, held):
            units[at] = value
    arrived = [exchange(send) for send in sends]
    result = None
    for chunk in range(chunks):
        result = attend(
            arrived[chunk],
            units,
            unit_places,
            sources,
            doc_lengths,
            shard[None],
            chunk,
            chunks,
            result,
        )
    return result


def solution(mesh):
    placed = (
        P(("ctx", "head"), None),
        P(("ctx", "head"), None),
        P(("ctx", "head"), None),
        P(),
        P(),
    )
    return jax.shard_map(
        body, mesh=mesh, in_specs=placed, out_specs=P("ctx", "head"), check_vma=False
    )
```

```python
import functools

import jax
import jax.numpy as jnp
import numpy as np
from jax import lax
from jax.experimental import pallas as pl
from jax.experimental.pallas import tpu as pltpu
from jax.sharding import PartitionSpec as P

HD = 128
SPAN = 8
MASKED = -1e30
EXP2_SCALE = float(HD ** (-0.5) * np.log2(np.e))
VMEM_LIMIT = 60 * 1024 * 1024
ANY = pl.BlockSpec(memory_space=pl.ANY)


def pack_query_kernel(chunks, place_ref, loader_ref, query, *refs):
    outs, sems = refs[:chunks], refs[chunks]
    per_loader = query.shape[0]
    width = outs[0].shape[2]
    copies = []
    for chunk in range(chunks):
        for j in range(per_loader):
            target = place_ref[loader_ref[0] * per_loader + j] // loader_ref[1]
            for side in range(2):
                copy = pltpu.make_async_copy(
                    query.at[j, :, pl.ds((side * chunks + chunk) * width, width)],
                    outs[chunk].at[target * 2 + side],
                    sems.at[len(copies)],
                )
                copy.start()
                copies.append(copy)
    for copy in copies:
        copy.wait()


def pack_pair_kernel(place_ref, loader_ref, key, value, out, sems):
    per_loader = key.shape[0]
    half = key.shape[2] // 2
    copies = []
    for j in range(per_loader):
        target = place_ref[loader_ref[0] * per_loader + j] // loader_ref[1]
        for side in range(2):
            for at, source in enumerate((key, value)):
                copy = pltpu.make_async_copy(
                    source.at[j, :, pl.ds(side * half, half)],
                    out.at[target * 2 + side, :, pl.ds(at * half, half)],
                    sems.at[len(copies)],
                )
                copy.start()
                copies.append(copy)
    for copy in copies:
        copy.wait()


def whole(shape):
    return pl.BlockSpec(shape, lambda i, *_: (0,) * len(shape))


def call(kernel, scalars, arrays, in_specs, outs, out_specs, scratch, name, **more):
    return pl.pallas_call(
        kernel,
        out_shape=outs,
        grid_spec=pltpu.PrefetchScalarGridSpec(
            num_scalar_prefetch=len(scalars),
            grid=(1,),
            in_specs=in_specs,
            out_specs=out_specs,
            scratch_shapes=scratch,
        ),
        compiler_params=pltpu.CompilerParams(vmem_limit_bytes=VMEM_LIMIT),
        name=name,
        **more,
    )(*scalars, *arrays)


def moved(count):
    return pl.CostEstimate(flops=0, transcendentals=0, bytes_accessed=count)


def pick_for_targets(blocks, block_place, loader, shard_blocks, shards):
    per_loader = blocks.shape[0]
    assigned = lax.dynamic_slice_in_dim(block_place, loader * per_loader, per_loader)
    matched = (assigned // shard_blocks)[None, :] == jnp.arange(shards, dtype=jnp.int32)[:, None]
    return jnp.take(blocks, jnp.argmax(matched, axis=1), axis=0)


def pack_query(query, block_place, loader, shard_blocks, slots, chunks):
    rows, columns = query.shape
    per_loader = block_place.shape[0] // slots
    block_rows = rows // per_loader
    width = columns // 2 // chunks
    blocks = query.reshape(per_loader, block_rows, columns)
    if block_rows % 16:
        picked = pick_for_targets(blocks, block_place, loader, shard_blocks, slots // 2)
        picked = picked.reshape(slots // 2, block_rows, 2, chunks, width)
        return [
            jnp.swapaxes(picked[:, :, :, chunk], 1, 2).reshape(slots, block_rows, width)
            for chunk in range(chunks)
        ]
    return call(
        functools.partial(pack_query_kernel, chunks),
        (block_place, jnp.stack([loader, jnp.int32(shard_blocks)])),
        (blocks,),
        [whole(blocks.shape)],
        [jax.ShapeDtypeStruct((slots, block_rows, width), query.dtype)] * chunks,
        [ANY] * chunks,
        [pltpu.SemaphoreType.DMA((2 * chunks * per_loader,))],
        "pack_query",
        cost_estimate=moved(4 * rows * columns),
    )


def pack_pair(key, value, block_place, loader, shard_blocks, slots):
    rows, columns = key.shape
    per_loader = block_place.shape[0] // slots
    block_rows = rows // per_loader
    keys, values = (x.reshape(per_loader, block_rows, columns) for x in (key, value))
    if block_rows % 16:
        both = jnp.stack([keys, values], axis=2).reshape(
            per_loader, block_rows, 2, 2, columns // 2
        )
        picked = pick_for_targets(both, block_place, loader, shard_blocks, slots // 2)
        return jnp.transpose(picked, (0, 3, 1, 2, 4)).reshape(slots, block_rows, columns)
    return call(
        pack_pair_kernel,
        (block_place, jnp.stack([loader, jnp.int32(shard_blocks)])),
        (keys, values),
        [whole(keys.shape)] * 2,
        jax.ShapeDtypeStruct((slots, block_rows, columns), key.dtype),
        ANY,
        [pltpu.SemaphoreType.DMA((4 * per_loader,))],
        "pack_pair",
        cost_estimate=moved(8 * rows * columns),
    )


def pick_kernel(rows_ref, blocks, out, sem):
    copies = []
    for i in range(out.shape[0]):
        copy = pltpu.make_async_copy(blocks.at[rows_ref[i]], out.at[i], sem.at[i])
        copy.start()
        copies.append(copy)
    for copy in copies:
        copy.wait()


def pick_unit(arrived, sources):
    count = sources.shape[0]
    block_rows, width = arrived.shape[1:]
    if block_rows % 16:
        unit = jnp.take(arrived, sources, axis=0)
    else:
        shape = (count, block_rows, width)
        unit = call(
            pick_kernel,
            (sources,),
            (arrived,),
            [ANY],
            jax.ShapeDtypeStruct(shape, arrived.dtype),
            whole(shape),
            [pltpu.SemaphoreType.DMA((count,))],
            "pick_unit",
            cost_estimate=moved(4 * count * block_rows * width),
        )
    return unit.reshape(count * block_rows, width)


def spread(unit, shard, sends):
    shards = lax.axis_size("ctx")
    plane = SPAN // 2
    place = shard % plane

    def forward(pieces):
        route = [(s, s + plane) for s in range(shards - plane)]
        return [lax.ppermute(piece, "ctx", route) for piece in pieces]

    first = unit.shape[0] // 4
    before_pieces = forward([unit[:first], unit[first:]])
    oldest_pieces = forward(before_pieces)
    before_pieces[0], sends[0] = lax.optimization_barrier((before_pieces[0], sends[0]))
    oldest_pieces[0], sends[1] = lax.optimization_barrier((oldest_pieces[0], sends[1]))
    before = jnp.concatenate(before_pieces)
    oldest = jnp.concatenate(oldest_pieces)
    units = [unit, before, oldest]
    places = [jnp.int32(SPAN), jnp.int32(plane), jnp.int32(0)]
    sent = {}
    stages = [[2], []]
    for mask in range(1, plane):
        partner = place ^ mask
        lower = place < partner
        bit = mask.bit_length()
        if bit not in sent:
            sent[bit] = jnp.where(lower, unit, oldest)
        route = [(s, s ^ mask) for s in range(shards)]
        stages[0].append(len(units))
        units.append(lax.ppermute(before, "ctx", route))
        places.append(plane - place + partner)
        stages[1].append(len(units))
        units.append(lax.ppermute(sent[bit], "ctx", route))
        places.append(jnp.where(lower, 0, SPAN) - place + partner)
    for chunk, stage in enumerate(stages, 2):
        held = [units[at] for at in stage]
        held, sends[chunk] = lax.optimization_barrier((held, sends[chunk]))
        for at, value in zip(stage, held):
            units[at] = value
    return units, jnp.stack(places).astype(jnp.int32)


def attend_kernel(chunk, docs, heads, slot_ref, lengths_ref, shard_ref, places_ref, *refs):
    arrived, units = refs[0], refs[1 : SPAN + 2]
    out, queries, keys, values, maxes, sums, sem, key_sem = refs[-8:]
    blocks, block_rows, width = queries.shape
    rows = blocks * block_rows
    tiles, tile = keys.shape[:2]
    copies = []
    for i in range(blocks):
        copy = pltpu.make_async_copy(arrived.at[slot_ref[i]], queries.at[i], sem.at[i])
        copy.start()
        copies.append(copy)
    half = units[0].shape[1] // 2

    def fetch(unit, at, which):
        target = (keys, values)[which]
        columns = pl.ds(which * half + chunk * HD, HD)
        return pltpu.make_async_copy(unit.at[:, columns], target.at[at], key_sem.at[which, at])

    for unit, ref in enumerate(units):
        for which in range(2):
            fetch(ref, places_ref[unit], which).start()
    first_row = shard_ref[0] * rows
    query_rows = first_row + lax.broadcasted_iota(jnp.int32, (1, rows), 1)
    starts = jnp.zeros((1, rows), jnp.int32)
    first_start = jnp.int32(0)
    end = jnp.int32(0)
    for d in range(docs):
        length = lengths_ref[d]
        end = end + length
        starts = starts + jnp.where(query_rows >= end, length, 0)
        first_start = first_start + jnp.where(first_row >= end, length, 0)
    window_start = first_row + rows - tiles * tile
    diagonal = tiles - 1
    first_tile = (first_start - window_start) // tile
    for h in range(heads):
        maxes[h] = jnp.full((1, rows), MASKED, jnp.float32)
        sums[h] = jnp.zeros(sums.shape[1:], jnp.float32)
    for copy in copies:
        copy.wait()

    def landed(index):
        for which in range(2):
            fetch(units[0], index, which).wait()

    def unused(index, carry):
        landed(index)
        return carry

    lax.fori_loop(0, first_tile, unused, 0)

    def step(index, count, masked, last):
        for other in range(count):
            landed(index + other)
        span = count * tile
        tile_keys = keys[pl.ds(index, count)].reshape(span, HD)
        tile_values = values[pl.ds(index, count)].reshape(span, HD)
        extended = jnp.concatenate([tile_values, jnp.ones((span, HD), tile_values.dtype)], axis=1)
        turned = extended.T[: HD + 16]
        if masked:
            key_rows = window_start + index * tile + lax.broadcasted_iota(jnp.int32, (tile, rows), 0)
            visible = (key_rows >= starts) & (key_rows <= query_rows)
        if last:
            later = starts >= first_row

        def score(h):
            query = queries[:, :, h * HD : (h + 1) * HD].reshape(rows, HD)
            return lax.dot_general(
                tile_keys, query, (((1,), (1,)), ((), ())), preferred_element_type=jnp.float32
            )

        ahead = score(0)
        for h in range(heads):
            scores = ahead
            if h + 1 < heads:
                ahead = score(h + 1)
            if masked:
                scores = jnp.where(visible, scores, MASKED)
            old = maxes[h]
            if last:
                old = jnp.where(later, MASKED, old)
            new = jnp.maximum(old, jnp.max(scores, axis=0, keepdims=True))
            scaled = new * EXP2_SCALE
            weights = jnp.exp2(scores * EXP2_SCALE - scaled).astype(jnp.bfloat16)
            factor = jnp.exp2(old * EXP2_SCALE - scaled)
            product = jnp.dot(turned, weights, preferred_element_type=jnp.float32)
            total = sums[h] * factor + product
            if last:
                result = total[:HD] / total[HD : HD + 1]
                out[:, h * HD : (h + 1) * HD] = result.T.astype(out.dtype)
            else:
                maxes[h] = new
                sums[h] = total

    @pl.when(first_tile < diagonal)
    def _():
        step(first_tile, 1, True, False)

    between = jnp.maximum(diagonal - first_tile - 1, 0)

    @pl.when(between % 2 == 1)
    def _():
        step(first_tile + 1, 1, False, False)

    def middle(index, carry):
        step(first_tile + 1 + between % 2 + 2 * index, 2, False, False)
        return carry

    lax.fori_loop(0, between // 2, middle, 0)
    step(diagonal, 1, True, True)


def attend(arrived, units, places, slots, doc_lengths, shard, chunk, chunks, result):
    block_rows, width = arrived.shape[1:]
    shard_rows = units[0].shape[0]
    blocks = shard_rows // block_rows
    if block_rows % 16:
        arrived = jnp.take(arrived, slots, axis=0).reshape(shard_rows // 16, 16, width)
        block_rows, blocks = 16, shard_rows // 16
        slots = jnp.arange(blocks, dtype=jnp.int32)
    heads = width // HD
    tiles = len(units)
    aliased = [] if result is None else [result]
    scalars = (slots, doc_lengths, shard, places)
    arrays = (arrived, *units, *aliased)
    return call(
        functools.partial(attend_kernel, chunk, doc_lengths.shape[0], heads),
        scalars,
        arrays,
        [ANY] * len(arrays),
        jax.ShapeDtypeStruct((shard_rows, chunks * width), arrived.dtype),
        pl.BlockSpec((shard_rows, width), lambda i, *_: (0, chunk)),
        [
            pltpu.VMEM((blocks, block_rows, width), arrived.dtype),
            pltpu.VMEM((tiles, shard_rows, HD), arrived.dtype),
            pltpu.VMEM((tiles, shard_rows, HD), arrived.dtype),
            pltpu.VMEM((heads, 1, shard_rows), jnp.float32),
            pltpu.VMEM((heads, HD + 16, shard_rows), jnp.float32),
            pltpu.SemaphoreType.DMA((blocks,)),
            pltpu.SemaphoreType.DMA((2, tiles)),
        ],
        f"attend{chunk}",
        input_output_aliases={len(scalars) + len(arrays) - 1: 0} if aliased else {},
        cost_estimate=pl.CostEstimate(
            flops=4 * shard_rows * shard_rows * tiles * width,
            transcendentals=shard_rows * shard_rows * tiles * heads,
            bytes_accessed=4 * shard_rows * (width + tiles * HD),
        ),
    )


def body(query, key, value, doc_lengths, block_place):
    ctx_count = lax.axis_size("ctx")
    head_count = lax.axis_size("head")
    loaded_rows = query.shape[0]
    shard_rows = loaded_rows * head_count
    block_rows = shard_rows // ctx_count
    per_loader = loaded_rows // block_rows
    shard_blocks = shard_rows // block_rows
    shard = lax.axis_index("ctx").astype(jnp.int32)
    group = lax.axis_index("head").astype(jnp.int32)
    loader = shard * head_count + group
    slots = ctx_count * head_count
    chunks = key.shape[1] // head_count // HD
    def exchange(sends):
        return lax.all_to_all(sends, ("ctx", "head"), split_axis=0, concat_axis=0, tiled=True)

    pair = exchange(pack_pair(key, value, block_place, loader, shard_blocks, slots))
    sends = list(pack_query(query, block_place, loader, shard_blocks, slots, chunks))
    wanted = shard * shard_blocks + jnp.arange(shard_blocks, dtype=jnp.int32)
    places = jnp.arange(block_place.shape[0], dtype=jnp.int32)
    inverse = jnp.sum(jnp.where(wanted[:, None] == block_place[None, :], places[None, :], 0), axis=1)
    sources = inverse // per_loader
    unit = pick_unit(pair, sources)
    units, unit_places = spread(unit, shard, sends)
    arrived = [exchange(send) for send in sends]
    result = None
    for chunk in range(chunks):
        result = attend(
            arrived[chunk],
            units,
            unit_places,
            sources,
            doc_lengths,
            shard[None],
            chunk,
            chunks,
            result,
        )
    return result


def solution(mesh):
    placed = (
        P(("ctx", "head"), None),
        P(("ctx", "head"), None),
        P(("ctx", "head"), None),
        P(),
        P(),
    )
    return jax.shard_map(
        body, mesh=mesh, in_specs=placed, out_specs=P("ctx", "head"), check_vma=False
    )
```

```python
import functools

import jax
import jax.numpy as jnp
import numpy as np
from jax import lax
from jax.experimental import pallas as pl
from jax.experimental.pallas import tpu as pltpu
from jax.sharding import Mesh
from jax.sharding import PartitionSpec as P

HD = 128
SPAN = 8
CHUNKS = 2
MASKED = -1e30
EXP2_SCALE = float(HD ** (-0.5) * np.log2(np.e))
VMEM_LIMIT = 60 * 1024 * 1024
ANY = pl.BlockSpec(memory_space=pl.ANY)


def whole(shape):
    return pl.BlockSpec(shape, lambda i, *_: (0,) * len(shape))


def call(kernel, scalars, arrays, in_specs, outs, out_specs, scratch, name, **more):
    return pl.pallas_call(
        kernel,
        out_shape=outs,
        grid_spec=pltpu.PrefetchScalarGridSpec(
            num_scalar_prefetch=len(scalars),
            grid=(1,),
            in_specs=in_specs,
            out_specs=out_specs,
            scratch_shapes=scratch,
        ),
        compiler_params=pltpu.CompilerParams(vmem_limit_bytes=VMEM_LIMIT),
        name=name,
        **more,
    )(*scalars, *arrays)


def moved(count):
    return pl.CostEstimate(flops=0, transcendentals=0, bytes_accessed=count)


def run_all(pairs, sems):
    copies = []
    for at, (source, target) in enumerate(pairs):
        copy = pltpu.make_async_copy(source, target, sems.at[at])
        copy.start()
        copies.append(copy)
    for copy in copies:
        copy.wait()


def split_kernel(near, query, key, value, *refs):
    outs, sems = refs[:-1], refs[-1]
    key_heads = outs[0].shape[0]
    pair = 2 * HD
    width = outs[-1].shape[2]
    group = query.shape[1] // key_heads
    pairs = []
    for at in range(key_heads):
        head = at % 2 * near + at // 2
        rows = pl.ds(head * HD, HD)
        pairs.append((key.at[:, rows], outs[0].at[at, :, pl.ds(0, HD)]))
        pairs.append((value.at[:, rows], outs[0].at[at, :, pl.ds(HD, HD)]))
        for chunk, out in enumerate(outs):
            offset = pair if chunk == 0 else 0
            source = query.at[:, pl.ds(head * group + chunk * width, width)]
            pairs.append((source, out.at[at, :, pl.ds(offset, width)]))
    run_all(pairs, sems)


def split(query, key, value, near):
    rows, columns = query.shape
    key_heads = key.shape[1] // HD
    width = columns // key_heads // CHUNKS
    shapes = [(key_heads, rows, width + (2 * HD if chunk == 0 else 0)) for chunk in range(CHUNKS)]
    return call(
        functools.partial(split_kernel, near),
        (),
        (query, key, value),
        [whole(query.shape), whole(key.shape), whole(value.shape)],
        [jax.ShapeDtypeStruct(shape, query.dtype) for shape in shapes],
        [ANY] * CHUNKS,
        [pltpu.SemaphoreType.DMA((key_heads * (2 + CHUNKS),))],
        "split",
        cost_estimate=moved(4 * rows * (columns + 2 * key.shape[1])),
    )


def pack_kernel(offset, slot_ref, blocks, *refs):
    out, sems = refs[-2], refs[-1]
    width = out.shape[2]
    pairs = []
    if offset:
        pairs.append((blocks.at[:, :, pl.ds(0, offset)], refs[0]))
    for b in range(blocks.shape[0]):
        pairs.append((blocks.at[b, :, pl.ds(offset, width)], out.at[slot_ref[b]]))
    run_all(pairs, sems)


def pack(blocks, offset, slots, count):
    total, block_rows, columns = blocks.shape
    width = columns - offset
    if block_rows % 16:
        every = jnp.arange(count, dtype=jnp.int32)
        sources = jnp.argmax(slots[None, :] == every[:, None], axis=1)
        packed = jnp.take(blocks[:, :, offset:], sources, axis=0)
        return [blocks[:, :, :offset], packed] if offset else [packed]
    shapes = [(count, block_rows, width)]
    if offset:
        shapes.insert(0, (total, block_rows, offset))
    return call(
        functools.partial(pack_kernel, offset),
        (slots,),
        (blocks,),
        [whole(blocks.shape)],
        [jax.ShapeDtypeStruct(shape, blocks.dtype) for shape in shapes],
        [ANY] * len(shapes),
        [pltpu.SemaphoreType.DMA((total + 1,))],
        "pack",
        cost_estimate=moved(4 * total * block_rows * columns),
    )


def window_kernel(count, rows_ref, blocks, out, sem):
    def start(w, carry):
        pltpu.make_async_copy(blocks.at[rows_ref[w]], out.at[w], sem).start()
        return carry

    lax.fori_loop(0, count, start, 0, unroll=8)
    pltpu.make_async_copy(out, out, sem).wait()


def pick_window(blocks, sources):
    count = sources.shape[0]
    block_rows, width = blocks.shape[1:]
    if block_rows % 16:
        window = jnp.take(blocks, sources, axis=0)
    else:
        shape = (count, block_rows, width)
        window = call(
            functools.partial(window_kernel, count),
            (sources,),
            (blocks,),
            [ANY],
            jax.ShapeDtypeStruct(shape, blocks.dtype),
            whole(shape),
            [pltpu.SemaphoreType.DMA(())],
            "window",
            cost_estimate=moved(4 * count * block_rows * width),
        )
    return window.reshape(count * block_rows, width)


def attend_kernel(near, docs, heads, slot_ref, lengths_ref, plane_ref, arrived, window, out, *refs):
    queries, maxes, sums, sem = refs
    blocks, block_rows, width = queries.shape
    rows = blocks * block_rows // near
    tile = rows
    window_tiles = window.shape[0] // tile
    per_shard = blocks // near
    copies = []
    for i in range(blocks):
        copy = pltpu.make_async_copy(arrived.at[slot_ref[i]], queries.at[i], sem.at[i])
        copy.start()
        copies.append(copy)
    plane_rows = near * rows
    window_start = (plane_ref[0] + 1) * plane_rows - window.shape[0]
    for copy in copies:
        copy.wait()

    def shard(j, carry):
        first_row = plane_ref[0] * plane_rows + j * rows
        query_rows = first_row + lax.broadcasted_iota(jnp.int32, (1, rows), 1)
        starts = jnp.zeros((1, rows), jnp.int32)
        first_start = jnp.int32(0)
        end = jnp.int32(0)
        for d in range(docs):
            length = lengths_ref[d]
            end = end + length
            starts = starts + jnp.where(query_rows >= end, length, 0)
            first_start = first_start + jnp.where(first_row >= end, length, 0)
        diagonal = window_tiles - near + j
        first_tile = (first_start - window_start) // tile
        for h in range(heads):
            maxes[h] = jnp.full((1, rows), MASKED, jnp.float32)
            sums[h] = jnp.zeros(sums.shape[1:], jnp.float32)

        def step(index, count, masked, last):
            span = count * tile
            at = pl.ds(pl.multiple_of(index * tile, tile), span)
            tile_keys = window[at, :HD]
            tile_values = window[at, HD:]
            extended = jnp.concatenate(
                [tile_values, jnp.ones((span, HD), tile_values.dtype)], axis=1
            )
            turned = extended.T[: HD + 16]
            if masked:
                key_rows = (
                    window_start + index * tile + lax.broadcasted_iota(jnp.int32, (span, rows), 0)
                )
                visible = (key_rows >= starts) & (key_rows <= query_rows)
            if last:
                later = starts >= first_row

            def score(h):
                query = queries[pl.ds(j * per_shard, per_shard), :, h * HD : (h + 1) * HD]
                return lax.dot_general(
                    tile_keys,
                    query.reshape(rows, HD),
                    (((1,), (1,)), ((), ())),
                    preferred_element_type=jnp.float32,
                )

            ahead = score(0)
            for h in range(heads):
                scores = ahead
                if h + 1 < heads:
                    ahead = score(h + 1)
                if masked:
                    scores = jnp.where(visible, scores, MASKED)
                old = maxes[h]
                if last:
                    old = jnp.where(later, MASKED, old)
                new = jnp.maximum(old, jnp.max(scores, axis=0, keepdims=True))
                scaled = new * EXP2_SCALE
                weights = jnp.exp2(scores * EXP2_SCALE - scaled).astype(jnp.bfloat16)
                factor = jnp.exp2(old * EXP2_SCALE - scaled)
                product = jnp.dot(turned, weights, preferred_element_type=jnp.float32)
                total = sums[h] * factor + product
                if last:
                    result = total[:HD] / total[HD : HD + 1]
                    out[j, :, h * HD : (h + 1) * HD] = result.T.astype(out.dtype)
                else:
                    maxes[h] = new
                    sums[h] = total

        @pl.when(first_tile < diagonal)
        def _():
            step(first_tile, 1, True, False)

        between = jnp.maximum(diagonal - first_tile - 1, 0)

        @pl.when(between % 2 == 1)
        def _():
            step(first_tile + 1, 1, False, False)

        def middle(index, carry):
            step(first_tile + 1 + between % 2 + 2 * index, 2, False, False)
            return carry

        lax.fori_loop(0, between // 2, middle, 0)
        step(diagonal, 1, True, True)
        return carry

    lax.fori_loop(0, near, shard, 0)


def attend(arrived, window, slots, doc_lengths, plane, near, rows):
    block_rows, width = arrived.shape[1:]
    if block_rows % 16:
        arrived = jnp.take(arrived, slots, axis=0).reshape(-1, 16, width)
        block_rows = 16
        slots = jnp.arange(arrived.shape[0], dtype=jnp.int32)
    blocks = slots.shape[0]
    heads = width // HD
    shape = (near, rows, width)
    pairs = near * rows * window.shape[0] * heads
    return call(
        functools.partial(attend_kernel, near, doc_lengths.shape[0], heads),
        (slots, doc_lengths, plane),
        (arrived, window),
        [ANY, whole(window.shape)],
        jax.ShapeDtypeStruct(shape, arrived.dtype),
        whole(shape),
        [
            pltpu.VMEM((blocks, block_rows, width), arrived.dtype),
            pltpu.VMEM((heads, 1, rows), jnp.float32),
            pltpu.VMEM((heads, HD + 16, rows), jnp.float32),
            pltpu.SemaphoreType.DMA((blocks,)),
        ],
        "attend",
        cost_estimate=pl.CostEstimate(
            flops=4 * pairs * HD, transcendentals=pairs, bytes_accessed=4 * near * rows * width
        ),
    )


def join_kernel(*refs):
    parts, out, sems = refs[:-2], refs[-2], refs[-1]
    near, rows, width = parts[0].shape
    pairs = []
    for chunk, part in enumerate(parts):
        for i in range(near):
            at = pl.ds((i * len(parts) + chunk) * width, width)
            pairs.append((part.at[i], out.at[:, at]))
    run_all(pairs, sems)


def join(parts):
    near, rows, width = parts[0].shape
    shape = (rows, near * len(parts) * width)
    return call(
        join_kernel,
        (),
        parts,
        [ANY] * len(parts),
        jax.ShapeDtypeStruct(shape, parts[0].dtype),
        whole(shape),
        [pltpu.SemaphoreType.DMA((near * len(parts),))],
        "join",
        cost_estimate=moved(4 * shape[0] * shape[1]),
    )


def body(query, key, value, doc_lengths, block_place):
    far = lax.axis_size("far")
    near = lax.axis_size("near")
    cores = lax.axis_size("head")
    loaded_rows = query.shape[0]
    rows = loaded_rows * cores
    block_rows = rows // (far * near)
    shard_blocks = rows // block_rows
    plane_blocks = near * shard_blocks
    plane = lax.axis_index("far").astype(jnp.int32)
    capacity = near * cores * min(near, loaded_rows // block_rows)

    def along(x, axis):
        return lax.all_to_all(x, axis, split_axis=0, concat_axis=0, tiled=True)

    sends = list(split(query, key, value, near))
    loaded = jnp.arange(block_place.shape[0], dtype=jnp.int32)
    origin = loaded // plane_blocks
    course = origin * far + block_place // plane_blocks
    ahead = (course[:, None] == course[None, :]) & (loaded[None, :] < loaded[:, None])
    rank = jnp.sum(ahead.astype(jnp.int32), axis=1)
    leaving = block_place // plane_blocks * capacity + rank
    leaving = lax.dynamic_slice_in_dim(leaving, plane * plane_blocks, plane_blocks)
    landing = origin * capacity + rank

    def at_packed(packed, values):
        found = packed[:, None] == block_place[None, :]
        return jnp.sum(jnp.where(found, values[None, :], 0), axis=1)

    window_blocks = SPAN * shard_blocks + plane_blocks
    wanted = (plane + 1) * plane_blocks - window_blocks + jnp.arange(window_blocks, dtype=jnp.int32)
    sources = at_packed(jnp.maximum(wanted, 0), loaded)
    slots = at_packed(wanted[window_blocks - plane_blocks :], landing)

    arrived = []
    for chunk in range(CHUNKS):
        offset = 2 * HD if chunk == 0 else 0
        received = along(sends[chunk], ("near", "head"))
        blocks = received.reshape(plane_blocks, block_rows, received.shape[2])
        packed = pack(blocks, offset, leaving, far * capacity)
        if chunk == 0:
            pair = lax.all_gather(packed[0], "far", tiled=True)
        sending = packed[-1]
        if chunk + 1 < CHUNKS:
            sending, sends[chunk + 1] = lax.optimization_barrier((sending, sends[chunk + 1]))
        arrived.append(along(sending, "far"))
    window = pick_window(pair, sources)
    parts = [
        along(attend(chunk, window, slots, doc_lengths, plane[None], near, rows), "near")
        for chunk in arrived
    ]
    return join(parts)


def solution(mesh):
    near = 4
    shape = (mesh.shape["ctx"] // near, near, mesh.shape["head"])
    planes = Mesh(mesh.devices.reshape(shape), ("far", "near", "head"))
    placed = (
        P(("far", "near", "head"), None),
        P(("far", "near", "head"), None),
        P(("far", "near", "head"), None),
        P(),
        P(),
    )
    return jax.shard_map(
        body, mesh=planes, in_specs=placed, out_specs=P(("far", "near"), "head"), check_vma=False
    )
```

```python
import functools

import jax
import jax.numpy as jnp
import numpy as np
from jax import lax
from jax.experimental import pallas as pl
from jax.experimental.pallas import tpu as pltpu
from jax.sharding import Mesh
from jax.sharding import PartitionSpec as P

HD = 128
SPAN = 8
CHUNKS = (3, 3, 2)
MASKED = -1e30
EXP2_SCALE = float(HD ** (-0.5) * np.log2(np.e))
VMEM_LIMIT = 60 * 1024 * 1024
ANY = pl.BlockSpec(memory_space=pl.ANY)


def whole(shape):
    return pl.BlockSpec(shape, lambda i, *_: (0,) * len(shape))


def call(kernel, scalars, arrays, in_specs, outs, out_specs, scratch, name, **more):
    return pl.pallas_call(
        kernel,
        out_shape=outs,
        grid_spec=pltpu.PrefetchScalarGridSpec(
            num_scalar_prefetch=len(scalars),
            grid=(1,),
            in_specs=in_specs,
            out_specs=out_specs,
            scratch_shapes=scratch,
        ),
        compiler_params=pltpu.CompilerParams(vmem_limit_bytes=VMEM_LIMIT),
        name=name,
        **more,
    )(*scalars, *arrays)


def moved(count):
    return pl.CostEstimate(flops=0, transcendentals=0, bytes_accessed=count)


def run_all(pairs, sems):
    copies = []
    for at, (source, target) in enumerate(pairs):
        copy = pltpu.make_async_copy(source, target, sems.at[at])
        copy.start()
        copies.append(copy)
    for copy in copies:
        copy.wait()


def split_kernel(near, query, key, value, out, sems):
    key_heads = out.shape[0]
    group = query.shape[1] // key_heads
    pairs = []
    for at in range(key_heads):
        head = at % 2 * near + at // 2
        for source, width, offset in ((key, HD, 0), (value, HD, HD), (query, group, 2 * HD)):
            columns = pl.ds(head * width, width)
            pairs.append((source.at[:, columns], out.at[at, :, pl.ds(offset, width)]))
    run_all(pairs, sems)


def split(query, key, value, near):
    rows, columns = query.shape
    key_heads = key.shape[1] // HD
    return call(
        functools.partial(split_kernel, near),
        (),
        (query, key, value),
        [whole(query.shape), whole(key.shape), whole(value.shape)],
        jax.ShapeDtypeStruct((key_heads, rows, columns // key_heads + 2 * HD), query.dtype),
        ANY,
        [pltpu.SemaphoreType.DMA((3 * key_heads,))],
        "split",
        cost_estimate=moved(4 * rows * (columns + 2 * key.shape[1])),
    )


def pack_kernel(offset, capacity, source_ref, counts_ref, received, *refs):
    blocks, in_sem, sem = refs[-3:]
    far = counts_ref.shape[0]
    outs = refs[-3 - far : -3]
    width = outs[0].shape[2]
    head = 0 if len(refs) > 3 + far else offset
    run_all([(received.at[:, :, pl.ds(head, blocks.shape[2])], blocks)], in_sem)
    columns = pl.ds(offset - head, width)
    for distance, out in enumerate(outs):

        def start(r, carry):
            source = source_ref[distance * capacity + r]
            pltpu.make_async_copy(blocks.at[source, :, columns], out.at[r], sem).start()
            return carry

        lax.fori_loop(0, counts_ref[distance], start, 0)
    if head < offset:
        run_all([(blocks.at[:, :, pl.ds(0, offset)], refs[0])], in_sem)
    moving = blocks.at[:, :, columns]
    pltpu.make_async_copy(moving, moving, sem).wait()


def pack(received, offset, width, paired, sources, counts, capacity):
    total, block_rows, _ = received.shape
    far = counts.shape[0]
    if block_rows % 16:
        packed = jnp.take(received[:, :, offset : offset + width], sources, axis=0)
        pieces = [packed[at * capacity :][:capacity] for at in range(far)]
        return [received[:, :, :offset]] + pieces if paired else pieces
    shapes = [(capacity, block_rows, width)] * far
    columns = width
    if paired:
        shapes.insert(0, (total, block_rows, offset))
        columns += offset
    return call(
        functools.partial(pack_kernel, offset, capacity),
        (sources, counts),
        (received,),
        [ANY],
        [jax.ShapeDtypeStruct(shape, received.dtype) for shape in shapes],
        [ANY] * len(shapes),
        [
            pltpu.VMEM((total, block_rows, columns), received.dtype),
            pltpu.SemaphoreType.DMA((1,)),
            pltpu.SemaphoreType.DMA(()),
        ],
        "pack",
        cost_estimate=moved(4 * total * block_rows * columns),
    )


def window_kernel(count, rows_ref, blocks, out, sem):
    def start(w, carry):
        pltpu.make_async_copy(blocks.at[rows_ref[w]], out.at[w], sem).start()
        return carry

    lax.fori_loop(0, count, start, 0, unroll=8)
    pltpu.make_async_copy(out, out, sem).wait()


def pick_window(blocks, sources):
    count = sources.shape[0]
    block_rows, width = blocks.shape[1:]
    if block_rows % 16:
        window = jnp.take(blocks, sources, axis=0)
    else:
        shape = (count, block_rows, width)
        window = call(
            functools.partial(window_kernel, count),
            (sources,),
            (blocks,),
            [ANY],
            jax.ShapeDtypeStruct(shape, blocks.dtype),
            whole(shape),
            [pltpu.SemaphoreType.DMA(())],
            "window",
            cost_estimate=moved(4 * count * block_rows * width),
        )
    return window.reshape(count * block_rows, width)


def attend_kernel(
    near, capacity, docs, heads, place_ref, counts_ref, lengths_ref, plane_ref, *refs
):
    far = counts_ref.shape[0]
    arrived, window = refs[:far], refs[far]
    outs, (queries, out, maxes, sums, sem, out_sems) = refs[far + 1 : -6], refs[-6:]
    blocks, block_rows, width = queries.shape
    rows = blocks * block_rows // near
    tile = rows
    window_tiles = window.shape[0] // tile
    per_shard = blocks // near
    for distance, piece in enumerate(arrived):

        def start(r, carry):
            place = place_ref[distance * capacity + r]
            pltpu.make_async_copy(piece.at[r], queries.at[place], sem).start()
            return carry

        lax.fori_loop(0, counts_ref[distance], start, 0)
    plane_rows = near * rows
    window_start = (plane_ref[0] + 1) * plane_rows - window.shape[0]
    pltpu.make_async_copy(queries, queries, sem).wait()

    def shard(j, carry):
        first_row = plane_ref[0] * plane_rows + j * rows
        query_rows = first_row + lax.broadcasted_iota(jnp.int32, (1, rows), 1)
        starts = jnp.zeros((1, rows), jnp.int32)
        first_start = jnp.int32(0)
        end = jnp.int32(0)
        for d in range(docs):
            length = lengths_ref[d]
            end = end + length
            starts = starts + jnp.where(query_rows >= end, length, 0)
            first_start = first_start + jnp.where(first_row >= end, length, 0)
        diagonal = window_tiles - near + j
        first_tile = (first_start - window_start) // tile
        for h in range(heads):
            maxes[h] = jnp.full((1, rows), MASKED, jnp.float32)
            sums[h] = jnp.zeros(sums.shape[1:], jnp.float32)

        def step(index, count, masked, last):
            span = count * tile
            at = pl.ds(pl.multiple_of(index * tile, tile), span)
            tile_keys = window[at, :HD]
            tile_values = window[at, HD:]
            extended = jnp.concatenate(
                [tile_values, jnp.ones((span, HD), tile_values.dtype)], axis=1
            )
            turned = extended.T[: HD + 16]
            if masked:
                key_rows = (
                    window_start + index * tile + lax.broadcasted_iota(jnp.int32, (span, rows), 0)
                )
                visible = (key_rows >= starts) & (key_rows <= query_rows)
            if last:
                later = starts >= first_row

            def score(h):
                query = queries[pl.ds(j * per_shard, per_shard), :, h * HD : (h + 1) * HD]
                return lax.dot_general(
                    tile_keys,
                    query.reshape(rows, HD),
                    (((1,), (1,)), ((), ())),
                    preferred_element_type=jnp.float32,
                )

            ahead = score(0)
            for h in range(heads):
                scores = ahead
                if h + 1 < heads:
                    ahead = score(h + 1)
                if masked:
                    scores = jnp.where(visible, scores, MASKED)
                old = maxes[h]
                if last:
                    old = jnp.where(later, MASKED, old)
                new = jnp.maximum(old, jnp.max(scores, axis=0, keepdims=True))
                scaled = new * EXP2_SCALE
                weights = jnp.exp2(scores * EXP2_SCALE - scaled).astype(jnp.bfloat16)
                factor = jnp.exp2(old * EXP2_SCALE - scaled)
                product = jnp.dot(turned, weights, preferred_element_type=jnp.float32)
                total = sums[h] * factor + product
                if last:
                    result = total[:HD] / total[HD : HD + 1]
                    out[j, :, h * HD : (h + 1) * HD] = result.T.astype(out.dtype)
                else:
                    maxes[h] = new
                    sums[h] = total

        @pl.when(first_tile < diagonal)
        def _():
            step(first_tile, 1, True, False)

        between = jnp.maximum(diagonal - first_tile - 1, 0)

        @pl.when(between % 2 == 1)
        def _():
            step(first_tile + 1, 1, False, False)

        def middle(index, carry):
            step(first_tile + 1 + between % 2 + 2 * index, 2, False, False)
            return carry

        lax.fori_loop(0, between // 2, middle, 0)
        step(diagonal, 1, True, True)
        return carry

    lax.fori_loop(0, near, shard, 0)
    run_all([(out.at[plane_ref[1] ^ at], target) for at, target in enumerate(outs)], out_sems)


def attend(arrived, window, places, slots, counts, doc_lengths, plane, index, near, rows):
    capacity, block_rows, width = arrived[0].shape
    blocks = slots.shape[0]
    if block_rows % 16:
        joined = jnp.take(jnp.concatenate(arrived), slots, axis=0).reshape(-1, 16, width)
        arrived = [joined]
        capacity, block_rows, width = joined.shape
        blocks = capacity
        places = jnp.arange(blocks, dtype=jnp.int32)
        counts = jnp.full((1,), blocks, jnp.int32)
    heads = width // HD
    shape = (rows, width)
    pairs = near * rows * window.shape[0] * heads
    return call(
        functools.partial(attend_kernel, near, capacity, doc_lengths.shape[0], heads),
        (places, counts, doc_lengths, jnp.stack([plane, index])),
        (*arrived, window),
        [ANY] * len(arrived) + [whole(window.shape)],
        [jax.ShapeDtypeStruct(shape, window.dtype)] * near,
        [ANY] * near,
        [
            pltpu.VMEM((blocks, block_rows, width), window.dtype),
            pltpu.VMEM((near, rows, width), window.dtype),
            pltpu.VMEM((heads, 1, rows), jnp.float32),
            pltpu.VMEM((heads, HD + 16, rows), jnp.float32),
            pltpu.SemaphoreType.DMA(()),
            pltpu.SemaphoreType.DMA((near,)),
        ],
        "attend",
        cost_estimate=pl.CostEstimate(
            flops=4 * pairs * HD, transcendentals=pairs, bytes_accessed=4 * near * rows * width
        ),
    )


def join_kernel(near, index_ref, *refs):
    parts, out, sems = refs[:-2], refs[-2], refs[-1]
    group = out.shape[1] // near
    offset = 0
    pairs = []
    for at, part in enumerate(parts):
        width = part.shape[1]
        column = (index_ref[0] ^ (at % near)) * group + offset
        pairs.append((part, out.at[:, pl.ds(pl.multiple_of(column, HD), width)]))
        if at % near == near - 1:
            offset += width
    run_all(pairs, sems)


def join(parts, index, near):
    rows = parts[0].shape[0]
    shape = (rows, sum(part.shape[1] for part in parts))
    return call(
        functools.partial(join_kernel, near),
        (index[None],),
        parts,
        [ANY] * len(parts),
        jax.ShapeDtypeStruct(shape, parts[0].dtype),
        whole(shape),
        [pltpu.SemaphoreType.DMA((len(parts),))],
        "join",
        cost_estimate=moved(4 * shape[0] * shape[1]),
    )


def body(query, key, value, doc_lengths, block_place):
    far = lax.axis_size("far")
    near = lax.axis_size("near")
    cores = lax.axis_size("head")
    loaded_rows = query.shape[0]
    rows = loaded_rows * cores
    block_rows = rows // (far * near)
    shard_blocks = rows // block_rows
    plane_blocks = near * shard_blocks
    plane = lax.axis_index("far").astype(jnp.int32)
    most = near * cores * min(near, loaded_rows // block_rows)

    def across(parts, axis, size):
        return [parts[0]] + [
            lax.ppermute(parts[at], axis, [(d, d ^ at) for d in range(size)])
            for at in range(1, size)
        ]

    index = lax.axis_index("near").astype(jnp.int32)
    received = lax.all_to_all(
        split(query, key, value, near), ("near", "head"), split_axis=0, concat_axis=0, tiled=True
    ).reshape(plane_blocks, block_rows, -1)
    loaded = jnp.arange(block_place.shape[0], dtype=jnp.int32)
    origin = loaded // plane_blocks
    target = block_place // plane_blocks
    course = origin * far + target
    ahead = (course[:, None] == course[None, :]) & (loaded[None, :] < loaded[:, None])
    rank = jnp.sum(ahead.astype(jnp.int32), axis=1)

    def where_sum(found, values):
        return jnp.sum(jnp.where(found, values[None, :], 0), axis=1)

    distances = jnp.arange(far, dtype=jnp.int32)[:, None]
    leaving = jnp.where(origin == plane, target ^ plane, far)
    landing = jnp.where(target == plane, origin ^ plane, far)
    ones = jnp.ones_like(loaded)
    leaving_counts = where_sum(distances == leaving[None, :], ones)
    landing_counts = where_sum(distances == landing[None, :], ones)
    window_blocks = SPAN * shard_blocks + plane_blocks
    wanted = (plane + 1) * plane_blocks - window_blocks + jnp.arange(window_blocks, dtype=jnp.int32)
    found = jnp.maximum(wanted, 0)[:, None] == block_place[None, :]
    window_sources = where_sum(found, loaded)

    def with_slots(capacity, received):
        every = jnp.arange(far * capacity, dtype=jnp.int32)[:, None]
        leaving_slot = leaving * capacity + rank
        landing_slot = landing * capacity + rank
        sources = where_sum(every == leaving_slot[None, :], loaded % plane_blocks)
        places = where_sum(every == landing_slot[None, :], block_place % plane_blocks)
        slots = where_sum(found[window_blocks - plane_blocks :], landing_slot)
        arrived = []
        offset = 2 * HD
        for chunk, heads in enumerate(CHUNKS):
            width = heads * HD
            packed = list(
                pack(received, offset, width, chunk == 0, sources, leaving_counts, capacity)
            )
            if chunk == 0:
                pair = lax.all_gather(packed.pop(0), "far", tiled=True)
            arrived.append(across(packed, "far", far))
            offset += width
        window = pick_window(pair, window_sources)
        parts = []
        for chunk in arrived:
            outs = attend(
                chunk,
                window,
                places,
                slots,
                landing_counts,
                doc_lengths,
                plane,
                index,
                near,
                rows,
            )
            parts += across(list(outs), "near", near)
        return join(parts, index, near)

    sizes = sorted({most * 5 // 8, most * 3 // 4, most})
    fullest = jnp.max(rank) + 1
    chosen = sum((fullest > size).astype(jnp.int32) for size in sizes[:-1])
    return lax.switch(chosen, [functools.partial(with_slots, size) for size in sizes], received)


def solution(mesh):
    near = 4
    shape = (mesh.shape["ctx"] // near, near, mesh.shape["head"])
    planes = Mesh(mesh.devices.reshape(shape), ("far", "near", "head"))
    placed = (
        P(("far", "near", "head"), None),
        P(("far", "near", "head"), None),
        P(("far", "near", "head"), None),
        P(),
        P(),
    )
    return jax.shard_map(
        body, mesh=planes, in_specs=placed, out_specs=P(("far", "near"), "head"), check_vma=False
    )
```

```python
import functools

import jax
import jax.numpy as jnp
import numpy as np
from jax import lax
from jax.experimental import pallas as pl
from jax.experimental.pallas import tpu as pltpu
from jax.sharding import Mesh
from jax.sharding import PartitionSpec as P

HD = 128
SPAN = 8
CHUNKS = (3, 3, 2)
MASKED = -1e30
EXP2_SCALE = float(HD ** (-0.5) * np.log2(np.e))
VMEM_LIMIT = 60 * 1024 * 1024
ANY = pl.BlockSpec(memory_space=pl.ANY)


def whole(shape):
    return pl.BlockSpec(shape, lambda i, *_: (0,) * len(shape))


def call(kernel, scalars, arrays, in_specs, outs, out_specs, scratch, name, **more):
    return pl.pallas_call(
        kernel,
        out_shape=outs,
        grid_spec=pltpu.PrefetchScalarGridSpec(
            num_scalar_prefetch=len(scalars),
            grid=(1,),
            in_specs=in_specs,
            out_specs=out_specs,
            scratch_shapes=scratch,
        ),
        compiler_params=pltpu.CompilerParams(vmem_limit_bytes=VMEM_LIMIT),
        name=name,
        **more,
    )(*scalars, *arrays)


def moved(count):
    return pl.CostEstimate(flops=0, transcendentals=0, bytes_accessed=count)


def run_all(pairs, sems):
    copies = []
    for at, (source, target) in enumerate(pairs):
        copy = pltpu.make_async_copy(source, target, sems.at[at])
        copy.start()
        copies.append(copy)
    for copy in copies:
        copy.wait()


def split_kernel(near, query, key, value, first, later, sems):
    key_heads = first.shape[0]
    group = query.shape[1] // key_heads
    early = CHUNKS[0] * HD
    pairs = []
    for at in range(key_heads):
        head = at % 2 * near + at // 2
        start = head * group
        own = pl.ds(head * HD, HD)
        pairs.append((key.at[:, own], first.at[at, :, pl.ds(0, HD)]))
        pairs.append((value.at[:, own], first.at[at, :, pl.ds(HD, HD)]))
        pairs.append((query.at[:, pl.ds(start, early)], first.at[at, :, pl.ds(2 * HD, early)]))
        pairs.append((query.at[:, pl.ds(start + early, group - early)], later.at[at]))
    run_all(pairs, sems)


def split(query, key, value, near):
    rows, columns = query.shape
    key_heads = key.shape[1] // HD
    early = CHUNKS[0] * HD
    widths = (early + 2 * HD, columns // key_heads - early)
    return call(
        functools.partial(split_kernel, near),
        (),
        (query, key, value),
        [whole(query.shape), whole(key.shape), whole(value.shape)],
        [jax.ShapeDtypeStruct((key_heads, rows, width), query.dtype) for width in widths],
        [ANY] * 2,
        [pltpu.SemaphoreType.DMA((4 * key_heads,))],
        "split",
        cost_estimate=moved(4 * rows * (columns + 2 * key.shape[1])),
    )


def pack_kernel(offset, stride, paired, capacity, source_ref, counts_ref, plane_ref, received, *refs):
    outs, (blocks, in_sem, sem) = refs[paired:-3], refs[-3:]
    far = counts_ref.shape[0]
    width = outs[0].shape[2]
    head = 0 if paired else offset
    run_all([(received.at[:, :, pl.ds(head, blocks.shape[2])], blocks)], in_sem)
    columns = pl.ds(offset - head, width)
    for distance in range(far):
        out, base = outs[0], (plane_ref[0] ^ distance) * capacity
        if len(outs) > 1:
            out, base = outs[distance], 0

        def start(r, carry):
            source = source_ref[distance * stride + r]
            pltpu.make_async_copy(blocks.at[source, :, columns], out.at[base + r], sem).start()
            return carry

        lax.fori_loop(0, counts_ref[distance], start, 0)
    if paired:
        run_all([(blocks.at[:, :, pl.ds(0, offset)], refs[0])], in_sem)
    moving = blocks.at[:, :, columns]
    pltpu.make_async_copy(moving, moving, sem).wait()


def by_distance(x, plane, far):
    parts = x.reshape((far, x.shape[0] // far) + x.shape[1:])
    return jnp.take(parts, plane ^ jnp.arange(far, dtype=jnp.int32), axis=0)


def pack(received, offset, width, first, sources, counts, plane, capacity):
    total, block_rows, _ = received.shape
    far = counts.shape[0]
    stride = sources.shape[0] // far
    if block_rows % 16:
        packed = jnp.take(received[:, :, offset : offset + width], sources, axis=0)
        packed = packed.reshape(far, stride, block_rows, width)[:, :capacity]
        if first:
            return [received[:, :, :offset]] + [packed[at] for at in range(far)]
        return [by_distance(packed.reshape(-1, block_rows, width), plane, far).reshape(packed.shape)]
    if first:
        shapes = [(total, block_rows, offset)] + [(capacity, block_rows, width)] * far
    else:
        shapes = [(far * capacity, block_rows, width)]
    return call(
        functools.partial(pack_kernel, offset, stride, int(first), capacity),
        (sources, counts, plane[None]),
        (received,),
        [ANY],
        [jax.ShapeDtypeStruct(shape, received.dtype) for shape in shapes],
        [ANY] * len(shapes),
        [
            pltpu.VMEM((total, block_rows, width + (offset if first else 0)), received.dtype),
            pltpu.SemaphoreType.DMA((1,)),
            pltpu.SemaphoreType.DMA(()),
        ],
        "pack",
        cost_estimate=moved(4 * total * block_rows * width),
    )


def window_kernel(rows_ref, blocks, keys, turned, held, sem):
    count, block_rows, _ = held.shape

    def start(w, carry):
        pltpu.make_async_copy(blocks.at[rows_ref[w]], held.at[w], sem).start()
        return carry

    lax.fori_loop(0, count, start, 0, unroll=8)
    turned[HD:] = jnp.ones((turned.shape[0] - HD, turned.shape[1]), turned.dtype)
    pltpu.make_async_copy(held, held, sem).wait()
    each = 256 // block_rows
    for part in range(count // each):
        at = pl.ds(part * 256, 256)
        blocks_at = pl.ds(part * each, each)
        keys[at] = held[blocks_at, :, :HD].reshape(256, HD)
        turned[:HD, at] = held[blocks_at, :, HD:].reshape(256, HD).T


def pick_window(blocks, sources):
    count = sources.shape[0]
    block_rows, width = blocks.shape[1:]
    rows = count * block_rows
    if block_rows % 16:
        window = jnp.take(blocks, sources, axis=0).reshape(rows, width)
        return window[:, :HD], jnp.concatenate([window[:, HD:].T, jnp.ones((16, rows), window.dtype)])
    shapes = [(rows, HD), (HD + 16, rows)]
    return call(
        window_kernel,
        (sources,),
        (blocks,),
        [ANY],
        [jax.ShapeDtypeStruct(shape, blocks.dtype) for shape in shapes],
        [whole(shape) for shape in shapes],
        [pltpu.VMEM((count, block_rows, width), blocks.dtype), pltpu.SemaphoreType.DMA(())],
        "window",
        cost_estimate=moved(4 * rows * width),
    )


def attend_kernel(
    near, pieces, stride, docs, heads, place_ref, counts_ref, lengths_ref, plane_ref, *refs
):
    far = counts_ref.shape[0]
    arrived, keys, turned = refs[:pieces], refs[pieces], refs[pieces + 1]
    outs, (queries, out, maxes, sums, sem, out_sems) = refs[pieces + 2 : -6], refs[-6:]
    blocks, block_rows, width = queries.shape
    rows = blocks * block_rows // near
    tile = rows
    window_tiles = keys.shape[0] // tile
    per_shard = blocks // near
    for distance in range(far):
        piece, base = arrived[0], (plane_ref[0] ^ distance) * (arrived[0].shape[0] // far)
        if pieces == far:
            piece, base = arrived[distance], 0

        def start(r, carry):
            place = place_ref[distance * stride + r]
            pltpu.make_async_copy(piece.at[base + r], queries.at[place], sem).start()
            return carry

        lax.fori_loop(0, counts_ref[distance], start, 0)
    plane_rows = near * rows
    window_start = (plane_ref[0] + 1) * plane_rows - keys.shape[0]
    pltpu.make_async_copy(queries, queries, sem).wait()

    def shard(j, carry):
        first_row = plane_ref[0] * plane_rows + j * rows
        query_rows = first_row + lax.broadcasted_iota(jnp.int32, (1, rows), 1)
        starts = jnp.zeros((1, rows), jnp.int32)
        first_start = jnp.int32(0)
        end = jnp.int32(0)
        for d in range(docs):
            length = lengths_ref[d]
            end = end + length
            starts = starts + jnp.where(query_rows >= end, length, 0)
            first_start = first_start + jnp.where(first_row >= end, length, 0)
        diagonal = window_tiles - near + j
        first_tile = (first_start - window_start) // tile
        for h in range(heads):
            maxes[h] = jnp.full((1, rows), MASKED, jnp.float32)
            sums[h] = jnp.zeros(sums.shape[1:], jnp.float32)

        def step(index, count, masked, last):
            span = count * tile
            at = pl.ds(pl.multiple_of(index * tile, tile), span)
            tile_keys = keys[at]
            tile_turned = turned[:, at]
            if masked:
                key_rows = (
                    window_start + index * tile + lax.broadcasted_iota(jnp.int32, (span, rows), 0)
                )
                visible = (key_rows >= starts) & (key_rows <= query_rows)
            if last:
                later = starts >= first_row

            def score(h):
                query = queries[pl.ds(j * per_shard, per_shard), :, h * HD : (h + 1) * HD]
                return lax.dot_general(
                    tile_keys,
                    query.reshape(rows, HD),
                    (((1,), (1,)), ((), ())),
                    preferred_element_type=jnp.float32,
                )

            ahead = score(0)
            for h in range(heads):
                scores = ahead
                if h + 1 < heads:
                    ahead = score(h + 1)
                if masked:
                    scores = jnp.where(visible, scores, MASKED)
                old = maxes[h]
                if last:
                    old = jnp.where(later, MASKED, old)
                new = jnp.maximum(old, jnp.max(scores, axis=0, keepdims=True))
                scaled = new * EXP2_SCALE
                weights = jnp.exp2(scores * EXP2_SCALE - scaled).astype(jnp.bfloat16)
                factor = jnp.exp2(old * EXP2_SCALE - scaled)
                product = jnp.dot(tile_turned, weights, preferred_element_type=jnp.float32)
                total = sums[h] * factor + product
                if last:
                    result = total[:HD] / total[HD : HD + 1]
                    out[j, :, h * HD : (h + 1) * HD] = result.T.astype(out.dtype)
                else:
                    maxes[h] = new
                    sums[h] = total

        @pl.when(first_tile < diagonal)
        def _():
            step(first_tile, 1, True, False)

        between = jnp.maximum(diagonal - first_tile - 1, 0)

        @pl.when(between % 2 == 1)
        def _():
            step(first_tile + 1, 1, False, False)

        def middle(index, carry):
            step(first_tile + 1 + between % 2 + 2 * index, 2, False, False)
            return carry

        lax.fori_loop(0, between // 2, middle, 0)
        step(diagonal, 1, True, True)
        return carry

    lax.fori_loop(0, near, shard, 0)
    run_all([(out.at[plane_ref[1] ^ at], target) for at, target in enumerate(outs)], out_sems)


def attend(arrived, keys, turned, places, slots, counts, doc_lengths, plane, index, near, rows):
    block_rows, width = arrived[0].shape[1:]
    far = counts.shape[0]
    blocks = slots.shape[0]
    stride = places.shape[0] // far
    if block_rows % 16:
        joined = jnp.concatenate(arrived)
        if len(arrived) == 1:
            joined = by_distance(joined, plane, far).reshape(joined.shape)
        joined = jnp.take(joined, slots, axis=0).reshape(-1, 16, width)
        arrived = [joined]
        block_rows = 16
        blocks = stride = joined.shape[0]
        places = jnp.arange(blocks, dtype=jnp.int32)
        counts = jnp.full((1,), blocks, jnp.int32)
    heads = width // HD
    shape = (rows, width)
    pairs = near * rows * keys.shape[0] * heads
    return call(
        functools.partial(
            attend_kernel, near, len(arrived), stride, doc_lengths.shape[0], heads
        ),
        (places, counts, doc_lengths, jnp.stack([plane, index])),
        (*arrived, keys, turned),
        [ANY] * len(arrived) + [whole(keys.shape), whole(turned.shape)],
        [jax.ShapeDtypeStruct(shape, keys.dtype)] * near,
        [ANY] * near,
        [
            pltpu.VMEM((blocks, block_rows, width), keys.dtype),
            pltpu.VMEM((near, rows, width), keys.dtype),
            pltpu.VMEM((heads, 1, rows), jnp.float32),
            pltpu.VMEM((heads, HD + 16, rows), jnp.float32),
            pltpu.SemaphoreType.DMA(()),
            pltpu.SemaphoreType.DMA((near,)),
        ],
        "attend",
        cost_estimate=pl.CostEstimate(
            flops=4 * pairs * HD, transcendentals=pairs, bytes_accessed=4 * near * rows * width
        ),
    )


def join_kernel(near, index_ref, *refs):
    parts, out, sems = refs[:-2], refs[-2], refs[-1]
    group = out.shape[1] // near
    offset = 0
    pairs = []
    for at, part in enumerate(parts):
        width = part.shape[1]
        column = (index_ref[0] ^ (at % near)) * group + offset
        pairs.append((part, out.at[:, pl.ds(pl.multiple_of(column, HD), width)]))
        if at % near == near - 1:
            offset += width
    run_all(pairs, sems)


def join(parts, index, near):
    rows = parts[0].shape[0]
    shape = (rows, sum(part.shape[1] for part in parts))
    return call(
        functools.partial(join_kernel, near),
        (index[None],),
        parts,
        [ANY] * len(parts),
        jax.ShapeDtypeStruct(shape, parts[0].dtype),
        whole(shape),
        [pltpu.SemaphoreType.DMA((len(parts),))],
        "join",
        cost_estimate=moved(4 * shape[0] * shape[1]),
    )


def body(query, key, value, doc_lengths, block_place):
    far = lax.axis_size("far")
    near = lax.axis_size("near")
    cores = lax.axis_size("head")
    loaded_rows = query.shape[0]
    rows = loaded_rows * cores
    block_rows = rows // (far * near)
    shard_blocks = rows // block_rows
    plane_blocks = near * shard_blocks
    plane = lax.axis_index("far").astype(jnp.int32)
    most = near * cores * min(near, loaded_rows // block_rows)

    def across(parts, axis, size):
        return [parts[0]] + [
            lax.ppermute(parts[at], axis, [(d, d ^ at) for d in range(size)])
            for at in range(1, size)
        ]

    index = lax.axis_index("near").astype(jnp.int32)

    def in_plane(x):
        x = lax.all_to_all(x, ("near", "head"), split_axis=0, concat_axis=0, tiled=True)
        return x.reshape(plane_blocks, block_rows, -1)

    first, later = split(query, key, value, near)
    received = in_plane(first)
    loaded = jnp.arange(block_place.shape[0], dtype=jnp.int32)
    origin = loaded // plane_blocks
    target = block_place // plane_blocks
    course = origin * far + target
    ahead = (course[:, None] == course[None, :]) & (loaded[None, :] < loaded[:, None])
    rank = jnp.sum(ahead.astype(jnp.int32), axis=1)

    def where_sum(found, values):
        return jnp.sum(jnp.where(found, values[None, :], 0), axis=1)

    distances = jnp.arange(far, dtype=jnp.int32)[:, None]
    leaving = jnp.where(origin == plane, target ^ plane, far)
    landing = jnp.where(target == plane, origin ^ plane, far)
    ones = jnp.ones_like(loaded)
    leaving_counts = where_sum(distances == leaving[None, :], ones)
    landing_counts = where_sum(distances == landing[None, :], ones)
    window_blocks = SPAN * shard_blocks + plane_blocks
    wanted = (plane + 1) * plane_blocks - window_blocks + jnp.arange(window_blocks, dtype=jnp.int32)
    found = jnp.maximum(wanted, 0)[:, None] == block_place[None, :]
    window_sources = where_sum(found, loaded)

    every = jnp.arange(far * most, dtype=jnp.int32)[:, None]
    leaving_slot = leaving * most + rank
    landing_slot = landing * most + rank
    sources = where_sum(every == leaving_slot[None, :], loaded % plane_blocks)
    places = where_sum(every == landing_slot[None, :], block_place % plane_blocks)

    def with_slots(capacity, received, later):
        slots = where_sum(
            found[window_blocks - plane_blocks :], landing * capacity + rank
        )

        def packed(received, offset, chunk):
            width = CHUNKS[chunk] * HD
            return list(
                pack(
                    received, offset, width, chunk == 0, sources, leaving_counts, plane, capacity
                )
            )

        def attended(arrived, keys, turned):
            return attend(
                arrived,
                keys,
                turned,
                places,
                slots,
                landing_counts,
                doc_lengths,
                plane,
                index,
                near,
                rows,
            )

        sending = packed(received, 2 * HD, 0)
        pair = sending.pop(0)
        sending[0], later = lax.optimization_barrier((sending[0], later))
        received = in_plane(later)
        pair = lax.all_gather(pair, "far", tiled=True)
        arrived = across(sending, "far", far)
        offset = 0
        parts = []
        for chunk in range(len(CHUNKS)):
            if chunk + 1 < len(CHUNKS):
                (sending,) = packed(received, offset, chunk + 1)
                offset += CHUNKS[chunk + 1] * HD
                if chunk == 0:
                    pair, sending = lax.optimization_barrier((pair, sending))
                    keys, turned = pick_window(pair, window_sources)
                else:
                    outs[0], sending = lax.optimization_barrier((outs[0], sending))
                sending = sending.reshape((-1,) + sending.shape[-2:])
                coming = lax.all_to_all(sending, "far", split_axis=0, concat_axis=0, tiled=True)
            if chunk > 0:
                parts += across(outs, "near", near)
            outs = list(attended(arrived, keys, turned))
            arrived = [coming]
        parts += across(outs, "near", near)
        return join(parts, index, near)

    sizes = sorted({most * 5 // 8, most * 3 // 4, most})
    fullest = jnp.max(rank) + 1
    chosen = sum((fullest > size).astype(jnp.int32) for size in sizes[:-1])
    return lax.switch(chosen, [functools.partial(with_slots, size) for size in sizes], received, later)


def solution(mesh):
    near = 4
    shape = (mesh.shape["ctx"] // near, near, mesh.shape["head"])
    planes = Mesh(mesh.devices.reshape(shape), ("far", "near", "head"))
    placed = (
        P(("far", "near", "head"), None),
        P(("far", "near", "head"), None),
        P(("far", "near", "head"), None),
        P(),
        P(),
    )
    return jax.shard_map(
        body, mesh=planes, in_specs=placed, out_specs=P(("far", "near"), "head"), check_vma=False
    )
```

```python
import functools

import jax
import jax.numpy as jnp
import numpy as np
from jax import lax
from jax.experimental import pallas as pl
from jax.experimental.pallas import tpu as pltpu
from jax.sharding import Mesh
from jax.sharding import PartitionSpec as P

HD = 128
SPAN = 8
CHUNKS = (3, 3, 2)
MASKED = -1e30
EXP2_SCALE = float(HD ** (-0.5) * np.log2(np.e))
VMEM_LIMIT = 60 * 1024 * 1024
ANY = pl.BlockSpec(memory_space=pl.ANY)


def whole(shape):
    return pl.BlockSpec(shape, lambda i, *_: (0,) * len(shape))


def call(kernel, scalars, arrays, in_specs, outs, out_specs, scratch, name, **more):
    return pl.pallas_call(
        kernel,
        out_shape=outs,
        grid_spec=pltpu.PrefetchScalarGridSpec(
            num_scalar_prefetch=len(scalars),
            grid=(1,),
            in_specs=in_specs,
            out_specs=out_specs,
            scratch_shapes=scratch,
        ),
        compiler_params=pltpu.CompilerParams(vmem_limit_bytes=VMEM_LIMIT),
        name=name,
        **more,
    )(*scalars, *arrays)


def moved(count):
    return pl.CostEstimate(flops=0, transcendentals=0, bytes_accessed=count)


def run_all(pairs, sems):
    copies = []
    for at, (source, target) in enumerate(pairs):
        copy = pltpu.make_async_copy(source, target, sems.at[at])
        copy.start()
        copies.append(copy)
    for copy in copies:
        copy.wait()


def split_kernel(near, query, key, value, first, later, sems):
    key_heads = first.shape[0]
    group = query.shape[1] // key_heads
    early = CHUNKS[0] * HD
    pairs = []
    for at in range(key_heads):
        head = at % 2 * near + at // 2
        start = head * group
        own = pl.ds(head * HD, HD)
        pairs.append((key.at[:, own], first.at[at, :, pl.ds(0, HD)]))
        pairs.append((value.at[:, own], first.at[at, :, pl.ds(HD, HD)]))
        pairs.append((query.at[:, pl.ds(start, early)], first.at[at, :, pl.ds(2 * HD, early)]))
        pairs.append((query.at[:, pl.ds(start + early, group - early)], later.at[at]))
    run_all(pairs, sems)


def split(query, key, value, near):
    rows, columns = query.shape
    key_heads = key.shape[1] // HD
    early = CHUNKS[0] * HD
    widths = (early + 2 * HD, columns // key_heads - early)
    return call(
        functools.partial(split_kernel, near),
        (),
        (query, key, value),
        [whole(query.shape), whole(key.shape), whole(value.shape)],
        [jax.ShapeDtypeStruct((key_heads, rows, width), query.dtype) for width in widths],
        [ANY] * 2,
        [pltpu.SemaphoreType.DMA((4 * key_heads,))],
        "split",
        cost_estimate=moved(4 * rows * (columns + 2 * key.shape[1])),
    )


def pack_kernel(offset, stride, source_ref, counts_ref, received, *refs):
    outs, (blocks, in_sem, sem) = refs[:-3], refs[-3:]
    run_all([(received.at[:, :, pl.ds(offset, blocks.shape[2])], blocks)], in_sem)
    for distance, out in enumerate(outs):

        def start(r, carry):
            source = source_ref[distance * stride + r]
            pltpu.make_async_copy(blocks.at[source], out.at[r], sem).start()
            return carry

        lax.fori_loop(0, counts_ref[distance], start, 0)
    pltpu.make_async_copy(blocks, blocks, sem).wait()


def pack(received, offset, width, sources, counts, capacity):
    total, block_rows, _ = received.shape
    far = counts.shape[0]
    stride = sources.shape[0] // far
    if block_rows % 16:
        packed = jnp.take(received[:, :, offset : offset + width], sources, axis=0)
        packed = packed.reshape(far, stride, block_rows, width)[:, :capacity]
        return [packed[at] for at in range(far)]
    return call(
        functools.partial(pack_kernel, offset, stride),
        (sources, counts),
        (received,),
        [ANY],
        [jax.ShapeDtypeStruct((capacity, block_rows, width), received.dtype)] * far,
        [ANY] * far,
        [
            pltpu.VMEM((total, block_rows, width), received.dtype),
            pltpu.SemaphoreType.DMA((1,)),
            pltpu.SemaphoreType.DMA(()),
        ],
        "pack",
        cost_estimate=moved(4 * total * block_rows * width),
    )


def window_kernel(pieces, rows_ref, *refs):
    arrived, (keys, turned, held, sem) = refs[:pieces], refs[pieces:]
    count, block_rows, _ = held.shape
    limit = arrived[0].shape[0]

    def start(w, carry):
        source = rows_ref[w]
        row = lax.rem(source, limit)
        for at, piece in enumerate(arrived):

            @pl.when(source // limit == at)
            def _():
                pltpu.make_async_copy(piece.at[row], held.at[w], sem).start()

        return carry

    lax.fori_loop(0, count, start, 0, unroll=4)
    turned[HD:] = jnp.ones((turned.shape[0] - HD, turned.shape[1]), turned.dtype)
    pltpu.make_async_copy(held, held, sem).wait()
    each = 256 // block_rows
    for part in range(count // each):
        at = pl.ds(part * 256, 256)
        blocks_at = pl.ds(part * each, each)
        keys[at] = held[blocks_at, :, :HD].reshape(256, HD)
        turned[:HD, at] = held[blocks_at, :, HD:].reshape(256, HD).T


def pick_window(arrived, sources):
    count = sources.shape[0]
    block_rows, width = arrived[0].shape[1:]
    rows = count * block_rows
    if block_rows % 16:
        window = jnp.take(jnp.concatenate(arrived), sources, axis=0).reshape(rows, width)
        return window[:, :HD], jnp.concatenate([window[:, HD:].T, jnp.ones((16, rows), window.dtype)])
    shapes = [(rows, HD), (HD + 16, rows)]
    return call(
        functools.partial(window_kernel, len(arrived)),
        (sources,),
        arrived,
        [ANY] * len(arrived),
        [jax.ShapeDtypeStruct(shape, arrived[0].dtype) for shape in shapes],
        [whole(shape) for shape in shapes],
        [pltpu.VMEM((count, block_rows, width), arrived[0].dtype), pltpu.SemaphoreType.DMA(())],
        "window",
        cost_estimate=moved(4 * rows * width),
    )


def attend_kernel(
    near, stride, docs, heads, place_ref, counts_ref, lengths_ref, plane_ref, *refs
):
    far = counts_ref.shape[0]
    arrived, keys, turned = refs[:far], refs[far], refs[far + 1]
    outs, (queries, out, maxes, sums, sem, out_sems) = refs[far + 2 : -6], refs[-6:]
    blocks, block_rows, width = queries.shape
    rows = blocks * block_rows // near
    tile = rows
    window_tiles = keys.shape[0] // tile
    per_shard = blocks // near
    for distance, piece in enumerate(arrived):

        def start(r, carry):
            place = place_ref[distance * stride + r]
            pltpu.make_async_copy(piece.at[r], queries.at[place], sem).start()
            return carry

        lax.fori_loop(0, counts_ref[distance], start, 0)
    plane_rows = near * rows
    window_start = (plane_ref[0] + 1) * plane_rows - keys.shape[0]
    pltpu.make_async_copy(queries, queries, sem).wait()

    shards = []
    for j in range(near):
        first_row = plane_ref[0] * plane_rows + j * rows
        query_rows = first_row + lax.broadcasted_iota(jnp.int32, (1, rows), 1)
        starts = jnp.zeros((1, rows), jnp.int32)
        first_start = jnp.int32(0)
        end = jnp.int32(0)
        for d in range(docs):
            length = lengths_ref[d]
            end = end + length
            starts = starts + jnp.where(query_rows >= end, length, 0)
            first_start = first_start + jnp.where(first_row >= end, length, 0)
        first_tile = (first_start - window_start) // tile
        shards.append((first_row, query_rows, starts, first_tile))
    for unit in range(near * heads):
        maxes[unit] = jnp.full((1, rows), MASKED, jnp.float32)
        sums[unit] = jnp.zeros(sums.shape[1:], jnp.float32)

    def step(number, masked, last):
        views = []
        for j, (first_row, query_rows, starts, first_tile) in enumerate(shards):
            diagonal = window_tiles - near + j
            index = jnp.int32(diagonal) if last else jnp.minimum(first_tile + number, diagonal)
            at = pl.ds(pl.multiple_of(index * tile, tile), tile)
            if masked:
                key_rows = (
                    window_start + index * tile + lax.broadcasted_iota(jnp.int32, (tile, rows), 0)
                )
                visible = (key_rows >= starts) & (key_rows <= query_rows)
                if not last:
                    visible = visible & (index < diagonal)
            else:
                visible = jnp.where(index < diagonal, 0.0, MASKED)
            views.append((at, visible))

        def score(unit):
            j, h = divmod(unit, heads)
            query = queries[pl.ds(j * per_shard, per_shard), :, h * HD : (h + 1) * HD]
            return lax.dot_general(
                keys[views[j][0]],
                query.reshape(rows, HD),
                (((1,), (1,)), ((), ())),
                preferred_element_type=jnp.float32,
            )

        ahead = score(0)
        for unit in range(near * heads):
            j, h = divmod(unit, heads)
            at, visible = views[j]
            first_row, _, starts, _ = shards[j]
            scores = ahead
            if unit + 1 < near * heads:
                ahead = score(unit + 1)
            old = maxes[unit]
            if masked:
                scores = jnp.where(visible, scores, MASKED)
                highest = jnp.max(scores, axis=0, keepdims=True)
                shift = 0.0
            else:
                highest = jnp.max(scores, axis=0, keepdims=True) + visible
                shift = visible
            if last:
                old = jnp.where(starts >= first_row, MASKED, old)
            new = jnp.maximum(old, highest)
            scaled = new * EXP2_SCALE - shift
            weights = jnp.exp2(scores * EXP2_SCALE - scaled).astype(jnp.bfloat16)
            factor = jnp.exp2(old * EXP2_SCALE - new * EXP2_SCALE)
            product = jnp.dot(turned[:, at], weights, preferred_element_type=jnp.float32)
            total = sums[unit] * factor + product
            if last:
                result = total[:HD] / total[HD : HD + 1]
                out[j, :, h * HD : (h + 1) * HD] = result.T.astype(out.dtype)
            else:
                maxes[unit] = new
                sums[unit] = total

    step(0, True, False)
    steps = jnp.int32(0)
    for j in range(near):
        steps = jnp.maximum(steps, window_tiles - near + j - shards[j][3])

    def middle(number, carry):
        step(number, False, False)
        return carry

    lax.fori_loop(1, steps, middle, 0)
    step(0, True, True)
    run_all([(out.at[plane_ref[1] ^ at], target) for at, target in enumerate(outs)], out_sems)


def attend(arrived, keys, turned, places, slots, counts, doc_lengths, plane, index, near, rows):
    block_rows, width = arrived[0].shape[1:]
    far = counts.shape[0]
    blocks = slots.shape[0]
    stride = places.shape[0] // far
    if block_rows % 16:
        joined = jnp.take(jnp.concatenate(arrived), slots, axis=0).reshape(-1, 16, width)
        arrived = [joined]
        block_rows = 16
        blocks = stride = joined.shape[0]
        places = jnp.arange(blocks, dtype=jnp.int32)
        counts = jnp.full((1,), blocks, jnp.int32)
    heads = width // HD
    shape = (rows, width)
    pairs = near * rows * keys.shape[0] * heads
    return call(
        functools.partial(attend_kernel, near, stride, doc_lengths.shape[0], heads),
        (places, counts, doc_lengths, jnp.stack([plane, index])),
        (*arrived, keys, turned),
        [ANY] * len(arrived) + [whole(keys.shape), whole(turned.shape)],
        [jax.ShapeDtypeStruct(shape, keys.dtype)] * near,
        [ANY] * near,
        [
            pltpu.VMEM((blocks, block_rows, width), keys.dtype),
            pltpu.VMEM((near, rows, width), keys.dtype),
            pltpu.VMEM((near * heads, 1, rows), jnp.float32),
            pltpu.VMEM((near * heads, HD + 16, rows), jnp.float32),
            pltpu.SemaphoreType.DMA(()),
            pltpu.SemaphoreType.DMA((near,)),
        ],
        "attend",
        cost_estimate=pl.CostEstimate(
            flops=4 * pairs * HD, transcendentals=pairs, bytes_accessed=4 * near * rows * width
        ),
    )


def join_kernel(near, index_ref, *refs):
    parts, out, sems = refs[:-2], refs[-2], refs[-1]
    group = out.shape[1] // near
    offset = 0
    pairs = []
    for at, part in enumerate(parts):
        width = part.shape[1]
        column = (index_ref[0] ^ (at % near)) * group + offset
        pairs.append((part, out.at[:, pl.ds(pl.multiple_of(column, HD), width)]))
        if at % near == near - 1:
            offset += width
    run_all(pairs, sems)


def join(parts, index, near):
    rows = parts[0].shape[0]
    shape = (rows, sum(part.shape[1] for part in parts))
    return call(
        functools.partial(join_kernel, near),
        (index[None],),
        parts,
        [ANY] * len(parts),
        jax.ShapeDtypeStruct(shape, parts[0].dtype),
        whole(shape),
        [pltpu.SemaphoreType.DMA((len(parts),))],
        "join",
        cost_estimate=moved(4 * shape[0] * shape[1]),
    )


def body(query, key, value, doc_lengths, block_place):
    far = lax.axis_size("far")
    near = lax.axis_size("near")
    cores = lax.axis_size("head")
    loaded_rows = query.shape[0]
    rows = loaded_rows * cores
    block_rows = rows // (far * near)
    shard_blocks = rows // block_rows
    plane_blocks = near * shard_blocks
    plane = lax.axis_index("far").astype(jnp.int32)
    most = near * cores * min(near, loaded_rows // block_rows)

    def across(parts, axis, size):
        return [parts[0]] + [
            lax.ppermute(parts[at], axis, [(d, d ^ at) for d in range(size)])
            for at in range(1, size)
        ]

    index = lax.axis_index("near").astype(jnp.int32)

    def in_plane(x):
        x = lax.all_to_all(x, ("near", "head"), split_axis=0, concat_axis=0, tiled=True)
        return x.reshape(plane_blocks, block_rows, -1)

    first, later = split(query, key, value, near)
    received = in_plane(first)
    loaded = jnp.arange(block_place.shape[0], dtype=jnp.int32)
    origin = loaded // plane_blocks
    target = block_place // plane_blocks
    course = origin * far + target
    ahead = (course[:, None] == course[None, :]) & (loaded[None, :] < loaded[:, None])
    rank = jnp.sum(ahead.astype(jnp.int32), axis=1)

    def where_sum(found, values):
        return jnp.sum(jnp.where(found, values[None, :], 0), axis=1)

    distances = jnp.arange(far, dtype=jnp.int32)[:, None]
    leaving = jnp.where(origin == plane, target ^ plane, far)
    landing = jnp.where(target == plane, origin ^ plane, far)
    ones = jnp.ones_like(loaded)
    leaving_counts = where_sum(distances == leaving[None, :], ones)
    landing_counts = where_sum(distances == landing[None, :], ones)
    window_blocks = SPAN * shard_blocks + plane_blocks
    wanted = (plane + 1) * plane_blocks - window_blocks + jnp.arange(window_blocks, dtype=jnp.int32)
    found = jnp.maximum(wanted, 0)[:, None] == block_place[None, :]
    window_sources = where_sum(found, (origin ^ plane) * plane_blocks + loaded % plane_blocks)

    every = jnp.arange(far * most, dtype=jnp.int32)[:, None]
    leaving_slot = leaving * most + rank
    landing_slot = landing * most + rank
    sources = where_sum(every == leaving_slot[None, :], loaded % plane_blocks)
    places = where_sum(every == landing_slot[None, :], block_place % plane_blocks)

    def with_slots(capacity, received, later):
        slots = where_sum(
            found[window_blocks - plane_blocks :], landing * capacity + rank
        )

        def attended(arrived):
            return attend(
                arrived,
                keys,
                turned,
                places,
                slots,
                landing_counts,
                doc_lengths,
                plane,
                index,
                near,
                rows,
            )

        def sent(received, offset, chunk):
            width = CHUNKS[chunk] * HD
            return list(pack(received, offset, width, sources, leaving_counts, capacity))

        pair = received[:, :, : 2 * HD]
        pair, received = lax.optimization_barrier((pair, received))
        window = across([pair] * far, "far", far)
        sending = sent(received, 2 * HD, 0)
        sending[0], later = lax.optimization_barrier((sending[0], later))
        arrived = [across(sending, "far", far)]
        received = in_plane(later)
        offset = 0
        for chunk in range(1, len(CHUNKS)):
            arrived.append(across(sent(received, offset, chunk), "far", far))
            offset += CHUNKS[chunk] * HD
        keys, turned = pick_window(window, window_sources)
        parts = []
        for chunk in arrived:
            parts += across(list(attended(chunk)), "near", near)
        return join(parts, index, near)

    sizes = sorted({most * 5 // 8, most * 3 // 4, most})
    fullest = jnp.max(rank) + 1
    chosen = sum((fullest > size).astype(jnp.int32) for size in sizes[:-1])
    return lax.switch(chosen, [functools.partial(with_slots, size) for size in sizes], received, later)


def solution(mesh):
    near = 4
    shape = (mesh.shape["ctx"] // near, near, mesh.shape["head"])
    planes = Mesh(mesh.devices.reshape(shape), ("far", "near", "head"))
    placed = (
        P(("far", "near", "head"), None),
        P(("far", "near", "head"), None),
        P(("far", "near", "head"), None),
        P(),
        P(),
    )
    return jax.shard_map(
        body, mesh=planes, in_specs=placed, out_specs=P(("far", "near"), "head"), check_vma=False
    )
```

```python
import functools

import jax
import jax.numpy as jnp
import numpy as np
from jax import lax
from jax.experimental import pallas as pl
from jax.experimental.pallas import tpu as pltpu
from jax.sharding import Mesh
from jax.sharding import PartitionSpec as P

HD = 128
SPAN = 8
CHUNKS = (4, 4)
MASKED = -1e30
EXP2_SCALE = float(HD ** (-0.5) * np.log2(np.e))
VMEM_LIMIT = 60 * 1024 * 1024
ANY = pl.BlockSpec(memory_space=pl.ANY)


def whole(shape):
    return pl.BlockSpec(shape, lambda i, *_: (0,) * len(shape))


def call(kernel, scalars, arrays, in_specs, outs, out_specs, scratch, name, **more):
    return pl.pallas_call(
        kernel,
        out_shape=outs,
        grid_spec=pltpu.PrefetchScalarGridSpec(
            num_scalar_prefetch=len(scalars),
            grid=(1,),
            in_specs=in_specs,
            out_specs=out_specs,
            scratch_shapes=scratch,
        ),
        compiler_params=pltpu.CompilerParams(vmem_limit_bytes=VMEM_LIMIT),
        name=name,
        **more,
    )(*scalars, *arrays)


def moved(count):
    return pl.CostEstimate(flops=0, transcendentals=0, bytes_accessed=count)


def run_all(pairs, sems):
    copies = []
    for at, (source, target) in enumerate(pairs):
        copy = pltpu.make_async_copy(source, target, sems.at[at])
        copy.start()
        copies.append(copy)
    for copy in copies:
        copy.wait()


def split_kernel(near, query, key, value, first, later, sems):
    key_heads = first.shape[0]
    group = query.shape[1] // key_heads
    early = CHUNKS[0] * HD
    pairs = []
    for at in range(key_heads):
        head = at % 2 * near + at // 2
        start = head * group
        own = pl.ds(head * HD, HD)
        pairs.append((key.at[:, own], first.at[at, :, pl.ds(0, HD)]))
        pairs.append((value.at[:, own], first.at[at, :, pl.ds(HD, HD)]))
        pairs.append((query.at[:, pl.ds(start, early)], first.at[at, :, pl.ds(2 * HD, early)]))
        pairs.append((query.at[:, pl.ds(start + early, group - early)], later.at[at]))
    run_all(pairs, sems)


def split(query, key, value, near):
    rows, columns = query.shape
    key_heads = key.shape[1] // HD
    early = CHUNKS[0] * HD
    widths = (early + 2 * HD, columns // key_heads - early)
    return call(
        functools.partial(split_kernel, near),
        (),
        (query, key, value),
        [whole(query.shape), whole(key.shape), whole(value.shape)],
        [jax.ShapeDtypeStruct((key_heads, rows, width), query.dtype) for width in widths],
        [ANY] * 2,
        [pltpu.SemaphoreType.DMA((4 * key_heads,))],
        "split",
        cost_estimate=moved(4 * rows * (columns + 2 * key.shape[1])),
    )


def pack_kernel(offset, stride, source_ref, counts_ref, received, *refs):
    outs, (blocks, in_sem, sem) = refs[:-3], refs[-3:]
    run_all([(received.at[:, :, pl.ds(offset, blocks.shape[2])], blocks)], in_sem)
    for distance, out in enumerate(outs):

        def start(r, carry):
            source = source_ref[distance * stride + r]
            pltpu.make_async_copy(blocks.at[source], out.at[r], sem).start()
            return carry

        lax.fori_loop(0, counts_ref[distance], start, 0)
    pltpu.make_async_copy(blocks, blocks, sem).wait()


def pack(received, offset, width, sources, counts, capacity):
    total, block_rows, _ = received.shape
    far = counts.shape[0]
    stride = sources.shape[0] // far
    if block_rows % 16:
        packed = jnp.take(received[:, :, offset : offset + width], sources, axis=0)
        packed = packed.reshape(far, stride, block_rows, width)[:, :capacity]
        return [packed[at] for at in range(far)]
    return call(
        functools.partial(pack_kernel, offset, stride),
        (sources, counts),
        (received,),
        [ANY],
        [jax.ShapeDtypeStruct((capacity, block_rows, width), received.dtype)] * far,
        [ANY] * far,
        [
            pltpu.VMEM((total, block_rows, width), received.dtype),
            pltpu.SemaphoreType.DMA((1,)),
            pltpu.SemaphoreType.DMA(()),
        ],
        "pack",
        cost_estimate=moved(4 * total * block_rows * width),
    )


def window_kernel(pieces, rows_ref, counts_ref, *refs):
    arrived, (keys, turned, held, sem) = refs[:pieces], refs[pieces:]
    count, block_rows, _ = held.shape
    limit = arrived[0].shape[0]
    for at, piece in enumerate(arrived):

        def start(b, carry):
            row = rows_ref[at * limit + b]

            @pl.when(row >= 0)
            def _():
                pltpu.make_async_copy(piece.at[b], held.at[row], sem).start()

            return carry

        lax.fori_loop(0, counts_ref[at], start, 0)
    turned[HD:] = jnp.ones((turned.shape[0] - HD, turned.shape[1]), turned.dtype)

    def wait(b, carry):
        pltpu.make_async_copy(held.at[0], held.at[0], sem).wait()
        return carry

    lax.fori_loop(0, counts_ref[pieces], wait, 0)
    each = 256 // block_rows
    for part in range(count // each):
        at = pl.ds(part * 256, 256)
        blocks_at = pl.ds(part * each, each)
        keys[at] = held[blocks_at, :, :HD].reshape(256, HD)
        turned[:HD, at] = held[blocks_at, :, HD:].reshape(256, HD).T


def pick_window(pair, count, block_place, plane):
    far = lax.axis_size("far")
    total, block_rows, width = pair.shape
    rows = count * block_rows
    first = (plane + 1) * total - count
    if block_rows % 16:
        wanted = jnp.maximum(first + jnp.arange(count, dtype=jnp.int32), 0)
        loaded = jnp.argmax(wanted[:, None] == block_place[None, :], axis=1)
        gathered = lax.all_gather(pair, "far", tiled=True)
        window = jnp.take(gathered, loaded, axis=0).reshape(rows, width)
        turned = jnp.concatenate([window[:, HD:].T, jnp.ones((16, rows), window.dtype)])
        return window[:, :HD], turned, [pair]
    up, down = [pair], [pair]
    for _ in range(far - 1):
        up.append(lax.ppermute(up[-1], "far", [(p, p + 1) for p in range(far - 1)]))
        down.append(lax.ppermute(down[-1], "far", [(p + 1, p) for p in range(far - 1)]))
    pieces = up + down[1:]
    planes = jnp.array(list(range(far)) + list(range(-1, -far, -1)), dtype=jnp.int32)
    planes = plane - planes
    real = (planes >= 0) & (planes < far)
    places = jnp.take(block_place.reshape(far, total), jnp.clip(planes, 0, far - 1), axis=0) - first
    places = jnp.where((places >= 0) & (places < count), places, -1)
    counts = jnp.where(real, total, 0).astype(jnp.int32)
    inside = jnp.sum(((places >= 0) & real[:, None]).astype(jnp.int32))
    shapes = [(rows, HD), (HD + 16, rows)]
    keys, turned = call(
        functools.partial(window_kernel, len(pieces)),
        (places.reshape(-1), jnp.concatenate([counts, inside[None]])),
        pieces,
        [ANY] * len(pieces),
        [jax.ShapeDtypeStruct(shape, pair.dtype) for shape in shapes],
        [whole(shape) for shape in shapes],
        [pltpu.VMEM((count, block_rows, width), pair.dtype), pltpu.SemaphoreType.DMA(())],
        "window",
        cost_estimate=moved(4 * rows * width),
    )
    return keys, turned, [up[far // 2], down[far // 2]]


def attend_kernel(
    near, stride, docs, heads, place_ref, counts_ref, lengths_ref, plane_ref, *refs
):
    far = counts_ref.shape[0]
    arrived, keys, turned = refs[:far], refs[far], refs[far + 1]
    outs, (queries, out, maxes, sums, sem, out_sems) = refs[far + 2 : -6], refs[-6:]
    blocks, block_rows, width = queries.shape
    rows = blocks * block_rows // near
    tile = rows
    window_tiles = keys.shape[0] // tile
    per_shard = blocks // near
    for distance, piece in enumerate(arrived):

        def start(r, carry):
            place = place_ref[distance * stride + r]
            pltpu.make_async_copy(piece.at[r], queries.at[place], sem).start()
            return carry

        lax.fori_loop(0, counts_ref[distance], start, 0)
    plane_rows = near * rows
    window_start = (plane_ref[0] + 1) * plane_rows - keys.shape[0]
    pltpu.make_async_copy(queries, queries, sem).wait()

    def shard(j, carry):
        first_row = plane_ref[0] * plane_rows + j * rows
        query_rows = first_row + lax.broadcasted_iota(jnp.int32, (1, rows), 1)
        starts = jnp.zeros((1, rows), jnp.int32)
        first_start = jnp.int32(0)
        end = jnp.int32(0)
        for d in range(docs):
            length = lengths_ref[d]
            end = end + length
            starts = starts + jnp.where(query_rows >= end, length, 0)
            first_start = first_start + jnp.where(first_row >= end, length, 0)
        diagonal = window_tiles - near + j
        first_tile = (first_start - window_start) // tile
        for h in range(heads):
            maxes[h] = jnp.full((1, rows), MASKED, jnp.float32)
            sums[h] = jnp.zeros(sums.shape[1:], jnp.float32)

        def step(index, count, masked, last):
            span = count * tile
            at = pl.ds(pl.multiple_of(index * tile, tile), span)
            tile_keys = keys[at]
            tile_turned = turned[:, at]
            if masked:
                key_rows = (
                    window_start + index * tile + lax.broadcasted_iota(jnp.int32, (span, rows), 0)
                )
                visible = (key_rows >= starts) & (key_rows <= query_rows)
            if last:
                later = starts >= first_row

            def score(h):
                query = queries[pl.ds(j * per_shard, per_shard), :, h * HD : (h + 1) * HD]
                return lax.dot_general(
                    tile_keys,
                    query.reshape(rows, HD),
                    (((1,), (1,)), ((), ())),
                    preferred_element_type=jnp.float32,
                )

            ahead = score(0)
            for h in range(heads):
                scores = ahead
                if h + 1 < heads:
                    ahead = score(h + 1)
                if masked:
                    scores = jnp.where(visible, scores, MASKED)
                old = maxes[h]
                if last:
                    old = jnp.where(later, MASKED, old)
                new = jnp.maximum(old, jnp.max(scores, axis=0, keepdims=True))
                scaled = new * EXP2_SCALE
                weights = jnp.exp2(scores * EXP2_SCALE - scaled).astype(jnp.bfloat16)
                factor = jnp.exp2(old * EXP2_SCALE - scaled)
                product = jnp.dot(tile_turned, weights, preferred_element_type=jnp.float32)
                total = sums[h] * factor + product
                if last:
                    result = total[:HD] / total[HD : HD + 1]
                    out[j, :, h * HD : (h + 1) * HD] = result.T.astype(out.dtype)
                else:
                    maxes[h] = new
                    sums[h] = total

        @pl.when(first_tile < diagonal)
        def _():
            step(first_tile, 1, True, False)

        between = jnp.maximum(diagonal - first_tile - 1, 0)

        @pl.when(between % 2 == 1)
        def _():
            step(first_tile + 1, 1, False, False)

        def middle(index, carry):
            step(first_tile + 1 + between % 2 + 2 * index, 2, False, False)
            return carry

        lax.fori_loop(0, between // 2, middle, 0)
        step(diagonal, 1, True, True)
        return carry

    lax.fori_loop(0, near, shard, 0)
    run_all([(out.at[plane_ref[1] ^ at], target) for at, target in enumerate(outs)], out_sems)


def attend(arrived, keys, turned, places, slots, counts, doc_lengths, plane, index, near, rows):
    block_rows, width = arrived[0].shape[1:]
    far = counts.shape[0]
    blocks = slots.shape[0]
    stride = places.shape[0] // far
    if block_rows % 16:
        joined = jnp.take(jnp.concatenate(arrived), slots, axis=0).reshape(-1, 16, width)
        arrived = [joined]
        block_rows = 16
        blocks = stride = joined.shape[0]
        places = jnp.arange(blocks, dtype=jnp.int32)
        counts = jnp.full((1,), blocks, jnp.int32)
    heads = width // HD
    shape = (rows, width)
    pairs = near * rows * keys.shape[0] * heads
    return call(
        functools.partial(attend_kernel, near, stride, doc_lengths.shape[0], heads),
        (places, counts, doc_lengths, jnp.stack([plane, index])),
        (*arrived, keys, turned),
        [ANY] * len(arrived) + [whole(keys.shape), whole(turned.shape)],
        [jax.ShapeDtypeStruct(shape, keys.dtype)] * near,
        [ANY] * near,
        [
            pltpu.VMEM((blocks, block_rows, width), keys.dtype),
            pltpu.VMEM((near, rows, width), keys.dtype),
            pltpu.VMEM((heads, 1, rows), jnp.float32),
            pltpu.VMEM((heads, HD + 16, rows), jnp.float32),
            pltpu.SemaphoreType.DMA(()),
            pltpu.SemaphoreType.DMA((near,)),
        ],
        "attend",
        cost_estimate=pl.CostEstimate(
            flops=4 * pairs * HD, transcendentals=pairs, bytes_accessed=4 * near * rows * width
        ),
    )


def join_kernel(near, index_ref, *refs):
    parts, out, sems = refs[:-2], refs[-2], refs[-1]
    group = out.shape[1] // near
    offset = 0
    pairs = []
    for at, part in enumerate(parts):
        width = part.shape[1]
        column = (index_ref[0] ^ (at % near)) * group + offset
        pairs.append((part, out.at[:, pl.ds(pl.multiple_of(column, HD), width)]))
        if at % near == near - 1:
            offset += width
    run_all(pairs, sems)


def join(parts, index, near):
    rows = parts[0].shape[0]
    shape = (rows, sum(part.shape[1] for part in parts))
    return call(
        functools.partial(join_kernel, near),
        (index[None],),
        parts,
        [ANY] * len(parts),
        jax.ShapeDtypeStruct(shape, parts[0].dtype),
        whole(shape),
        [pltpu.SemaphoreType.DMA((len(parts),))],
        "join",
        cost_estimate=moved(4 * shape[0] * shape[1]),
    )


def body(query, key, value, doc_lengths, block_place):
    far = lax.axis_size("far")
    near = lax.axis_size("near")
    cores = lax.axis_size("head")
    loaded_rows = query.shape[0]
    rows = loaded_rows * cores
    block_rows = rows // (far * near)
    shard_blocks = rows // block_rows
    plane_blocks = near * shard_blocks
    plane = lax.axis_index("far").astype(jnp.int32)
    most = near * cores * min(near, loaded_rows // block_rows)

    def across(parts, axis, size):
        return [parts[0]] + [
            lax.ppermute(parts[at], axis, [(d, d ^ at) for d in range(size)])
            for at in range(1, size)
        ]

    index = lax.axis_index("near").astype(jnp.int32)

    def in_plane(x):
        x = lax.all_to_all(x, ("near", "head"), split_axis=0, concat_axis=0, tiled=True)
        return x.reshape(plane_blocks, block_rows, -1)

    first, later = split(query, key, value, near)
    received = in_plane(first)
    loaded = jnp.arange(block_place.shape[0], dtype=jnp.int32)
    origin = loaded // plane_blocks
    target = block_place // plane_blocks
    course = origin * far + target
    ahead = (course[:, None] == course[None, :]) & (loaded[None, :] < loaded[:, None])
    rank = jnp.sum(ahead.astype(jnp.int32), axis=1)

    def where_sum(found, values):
        return jnp.sum(jnp.where(found, values[None, :], 0), axis=1)

    distances = jnp.arange(far, dtype=jnp.int32)[:, None]
    leaving = jnp.where(origin == plane, target ^ plane, far)
    landing = jnp.where(target == plane, origin ^ plane, far)
    ones = jnp.ones_like(loaded)
    leaving_counts = where_sum(distances == leaving[None, :], ones)
    landing_counts = where_sum(distances == landing[None, :], ones)
    window_blocks = SPAN * shard_blocks + plane_blocks
    wanted = (plane + 1) * plane_blocks - window_blocks + jnp.arange(window_blocks, dtype=jnp.int32)
    found = jnp.maximum(wanted, 0)[:, None] == block_place[None, :]

    every = jnp.arange(far * most, dtype=jnp.int32)[:, None]
    leaving_slot = leaving * most + rank
    landing_slot = landing * most + rank
    sources = where_sum(every == leaving_slot[None, :], loaded % plane_blocks)
    places = where_sum(every == landing_slot[None, :], block_place % plane_blocks)

    def with_slots(capacity, received, later):
        slots = where_sum(
            found[window_blocks - plane_blocks :], landing * capacity + rank
        )

        def attended(arrived):
            return attend(
                arrived,
                keys,
                turned,
                places,
                slots,
                landing_counts,
                doc_lengths,
                plane,
                index,
                near,
                rows,
            )

        def sent(received, offset, chunk):
            width = CHUNKS[chunk] * HD
            return list(pack(received, offset, width, sources, leaving_counts, capacity))

        pair = received[:, :, : 2 * HD]
        pair, received = lax.optimization_barrier((pair, received))
        keys, turned, hops = pick_window(pair, window_blocks, block_place, plane)
        arrived = [across(sent(received, 2 * HD, 0), "far", far)]
        hops, later = lax.optimization_barrier((hops, later))
        received = in_plane(later)
        offset = 0
        for chunk in range(1, len(CHUNKS)):
            arrived.append(across(sent(received, offset, chunk), "far", far))
            offset += CHUNKS[chunk] * HD
        parts = []
        for chunk in arrived:
            parts += across(list(attended(chunk)), "near", near)
        return join(parts, index, near)

    sizes = sorted({most * 5 // 8, most * 3 // 4, most})
    fullest = jnp.max(rank) + 1
    chosen = sum((fullest > size).astype(jnp.int32) for size in sizes[:-1])
    return lax.switch(chosen, [functools.partial(with_slots, size) for size in sizes], received, later)


def solution(mesh):
    near = 4
    shape = (mesh.shape["ctx"] // near, near, mesh.shape["head"])
    planes = Mesh(mesh.devices.reshape(shape), ("far", "near", "head"))
    placed = (
        P(("far", "near", "head"), None),
        P(("far", "near", "head"), None),
        P(("far", "near", "head"), None),
        P(),
        P(),
    )
    return jax.shard_map(
        body, mesh=planes, in_specs=placed, out_specs=P(("far", "near"), "head"), check_vma=False
    )
```

```python
import functools

import jax
import jax.numpy as jnp
import numpy as np
from jax import lax
from jax.experimental import pallas as pl
from jax.experimental.pallas import tpu as pltpu
from jax.sharding import Mesh
from jax.sharding import PartitionSpec as P

HD = 128
SPAN = 8
CHUNKS = (4, 4)
MASKED = -1e30
EXP2_SCALE = float(HD ** (-0.5) * np.log2(np.e))
VMEM_LIMIT = 60 * 1024 * 1024
ANY = pl.BlockSpec(memory_space=pl.ANY)


def whole(shape):
    return pl.BlockSpec(shape, lambda i, *_: (0,) * len(shape))


def call(kernel, scalars, arrays, in_specs, outs, out_specs, scratch, name, **more):
    return pl.pallas_call(
        kernel,
        out_shape=outs,
        grid_spec=pltpu.PrefetchScalarGridSpec(
            num_scalar_prefetch=len(scalars),
            grid=(1,),
            in_specs=in_specs,
            out_specs=out_specs,
            scratch_shapes=scratch,
        ),
        compiler_params=pltpu.CompilerParams(vmem_limit_bytes=VMEM_LIMIT),
        name=name,
        **more,
    )(*scalars, *arrays)


def moved(count):
    return pl.CostEstimate(flops=0, transcendentals=0, bytes_accessed=count)


def run_all(pairs, sems):
    copies = []
    for at, (source, target) in enumerate(pairs):
        copy = pltpu.make_async_copy(source, target, sems.at[at])
        copy.start()
        copies.append(copy)
    for copy in copies:
        copy.wait()


def split_kernel(near, query, key, value, out, sems):
    key_heads = out.shape[0]
    group = query.shape[1] // key_heads
    pairs = []
    for at in range(key_heads):
        head = at % 2 * near + at // 2
        for source, width, offset in ((key, HD, 0), (value, HD, HD), (query, group, 2 * HD)):
            columns = pl.ds(head * width, width)
            pairs.append((source.at[:, columns], out.at[at, :, pl.ds(offset, width)]))
    run_all(pairs, sems)


def split(query, key, value, near):
    rows, columns = query.shape
    key_heads = key.shape[1] // HD
    return call(
        functools.partial(split_kernel, near),
        (),
        (query, key, value),
        [whole(query.shape), whole(key.shape), whole(value.shape)],
        jax.ShapeDtypeStruct((key_heads, rows, columns // key_heads + 2 * HD), query.dtype),
        ANY,
        [pltpu.SemaphoreType.DMA((3 * key_heads,))],
        "split",
        cost_estimate=moved(4 * rows * (columns + 2 * key.shape[1])),
    )


def pack_kernel(offset, stride, source_ref, counts_ref, received, *refs):
    outs, (blocks, in_sem, sem) = refs[:-3], refs[-3:]
    run_all([(received.at[:, :, pl.ds(offset, blocks.shape[2])], blocks)], in_sem)
    for distance, out in enumerate(outs):

        def start(r, carry):
            source = source_ref[distance * stride + r]
            pltpu.make_async_copy(blocks.at[source], out.at[r], sem).start()
            return carry

        lax.fori_loop(0, counts_ref[distance], start, 0)
    pltpu.make_async_copy(blocks, blocks, sem).wait()


def pack(received, offset, width, sources, counts, capacity):
    total, block_rows, _ = received.shape
    far = counts.shape[0]
    stride = sources.shape[0] // far
    if block_rows % 16:
        packed = jnp.take(received[:, :, offset : offset + width], sources, axis=0)
        packed = packed.reshape(far, stride, block_rows, width)[:, :capacity]
        return [packed[at] for at in range(far)]
    return call(
        functools.partial(pack_kernel, offset, stride),
        (sources, counts),
        (received,),
        [ANY],
        [jax.ShapeDtypeStruct((capacity, block_rows, width), received.dtype)] * far,
        [ANY] * far,
        [
            pltpu.VMEM((total, block_rows, width), received.dtype),
            pltpu.SemaphoreType.DMA((1,)),
            pltpu.SemaphoreType.DMA(()),
        ],
        "pack",
        cost_estimate=moved(4 * total * block_rows * width),
    )


def window_kernel(pieces, rows_ref, counts_ref, *refs):
    arrived, (keys, turned, held, sem) = refs[:pieces], refs[pieces:]
    count, block_rows, _ = held.shape
    limit = arrived[0].shape[0]
    for at, piece in enumerate(arrived):

        def start(b, carry):
            row = rows_ref[at * limit + b]

            @pl.when(row >= 0)
            def _():
                pltpu.make_async_copy(piece.at[b], held.at[row], sem).start()

            return carry

        lax.fori_loop(0, counts_ref[at], start, 0)
    turned[HD:] = jnp.ones((turned.shape[0] - HD, turned.shape[1]), turned.dtype)

    def wait(b, carry):
        pltpu.make_async_copy(held.at[0], held.at[0], sem).wait()
        return carry

    lax.fori_loop(0, counts_ref[pieces], wait, 0)
    each = 256 // block_rows
    for part in range(count // each):
        at = pl.ds(part * 256, 256)
        blocks_at = pl.ds(part * each, each)
        keys[at] = held[blocks_at, :, :HD].reshape(256, HD)
        turned[:HD, at] = held[blocks_at, :, HD:].reshape(256, HD).T


def pick_window(pair, count, block_place, plane):
    far = lax.axis_size("far")
    total, block_rows, width = pair.shape
    rows = count * block_rows
    first = (plane + 1) * total - count
    if block_rows % 16:
        wanted = jnp.maximum(first + jnp.arange(count, dtype=jnp.int32), 0)
        loaded = jnp.argmax(wanted[:, None] == block_place[None, :], axis=1)
        gathered = lax.all_gather(pair, "far", tiled=True)
        window = jnp.take(gathered, loaded, axis=0).reshape(rows, width)
        turned = jnp.concatenate([window[:, HD:].T, jnp.ones((16, rows), window.dtype)])
        return window[:, :HD], turned, [pair]
    up, down = [pair], [pair]
    for _ in range(far - 1):
        up.append(lax.ppermute(up[-1], "far", [(p, p + 1) for p in range(far - 1)]))
        down.append(lax.ppermute(down[-1], "far", [(p + 1, p) for p in range(far - 1)]))
    pieces = up + down[1:]
    planes = jnp.array(list(range(far)) + list(range(-1, -far, -1)), dtype=jnp.int32)
    planes = plane - planes
    real = (planes >= 0) & (planes < far)
    places = jnp.take(block_place.reshape(far, total), jnp.clip(planes, 0, far - 1), axis=0) - first
    places = jnp.where((places >= 0) & (places < count), places, -1)
    counts = jnp.where(real, total, 0).astype(jnp.int32)
    inside = jnp.sum(((places >= 0) & real[:, None]).astype(jnp.int32))
    shapes = [(rows, HD), (HD + 16, rows)]
    keys, turned = call(
        functools.partial(window_kernel, len(pieces)),
        (places.reshape(-1), jnp.concatenate([counts, inside[None]])),
        pieces,
        [ANY] * len(pieces),
        [jax.ShapeDtypeStruct(shape, pair.dtype) for shape in shapes],
        [whole(shape) for shape in shapes],
        [pltpu.VMEM((count, block_rows, width), pair.dtype), pltpu.SemaphoreType.DMA(())],
        "window",
        cost_estimate=moved(4 * rows * width),
    )
    return keys, turned, [up[far // 2], down[far // 2]]


def attend_kernel(
    near, stride, docs, heads, place_ref, counts_ref, lengths_ref, plane_ref, *refs
):
    far = counts_ref.shape[0]
    arrived, keys, turned = refs[:far], refs[far], refs[far + 1]
    outs, (queries, out, maxes, sums, sem, out_sems) = refs[far + 2 : -6], refs[-6:]
    blocks, block_rows, width = queries.shape
    rows = blocks * block_rows // near
    tile = rows
    window_tiles = keys.shape[0] // tile
    per_shard = blocks // near
    for distance, piece in enumerate(arrived):

        def start(r, carry):
            place = place_ref[distance * stride + r]
            pltpu.make_async_copy(piece.at[r], queries.at[place], sem).start()
            return carry

        lax.fori_loop(0, counts_ref[distance], start, 0)
    plane_rows = near * rows
    window_start = (plane_ref[0] + 1) * plane_rows - keys.shape[0]
    pltpu.make_async_copy(queries, queries, sem).wait()

    def shard(j, carry):
        first_row = plane_ref[0] * plane_rows + j * rows
        query_rows = first_row + lax.broadcasted_iota(jnp.int32, (1, rows), 1)
        starts = jnp.zeros((1, rows), jnp.int32)
        first_start = jnp.int32(0)
        end = jnp.int32(0)
        for d in range(docs):
            length = lengths_ref[d]
            end = end + length
            starts = starts + jnp.where(query_rows >= end, length, 0)
            first_start = first_start + jnp.where(first_row >= end, length, 0)
        diagonal = window_tiles - near + j
        first_tile = (first_start - window_start) // tile
        for h in range(heads):
            maxes[h] = jnp.full((1, rows), MASKED, jnp.float32)
            sums[h] = jnp.zeros(sums.shape[1:], jnp.float32)

        def step(index, count, masked, last):
            span = count * tile
            at = pl.ds(pl.multiple_of(index * tile, tile), span)
            tile_keys = keys[at]
            tile_turned = turned[:, at]
            if masked:
                key_rows = (
                    window_start + index * tile + lax.broadcasted_iota(jnp.int32, (span, rows), 0)
                )
                visible = (key_rows >= starts) & (key_rows <= query_rows)
            if last:
                later = starts >= first_row

            def score(h):
                query = queries[pl.ds(j * per_shard, per_shard), :, h * HD : (h + 1) * HD]
                return lax.dot_general(
                    tile_keys,
                    query.reshape(rows, HD),
                    (((1,), (1,)), ((), ())),
                    preferred_element_type=jnp.float32,
                )

            ahead = score(0)
            for h in range(heads):
                scores = ahead
                if h + 1 < heads:
                    ahead = score(h + 1)
                if masked:
                    scores = jnp.where(visible, scores, MASKED)
                old = maxes[h]
                if last:
                    old = jnp.where(later, MASKED, old)
                new = jnp.maximum(old, jnp.max(scores, axis=0, keepdims=True))
                scaled = new * EXP2_SCALE
                weights = jnp.exp2(scores * EXP2_SCALE - scaled).astype(jnp.bfloat16)
                factor = jnp.exp2(old * EXP2_SCALE - scaled)
                product = jnp.dot(tile_turned, weights, preferred_element_type=jnp.float32)
                total = sums[h] * factor + product
                if last:
                    result = total[:HD] / total[HD : HD + 1]
                    out[j, :, h * HD : (h + 1) * HD] = result.T.astype(out.dtype)
                else:
                    maxes[h] = new
                    sums[h] = total

        @pl.when(first_tile < diagonal)
        def _():
            step(first_tile, 1, True, False)

        between = jnp.maximum(diagonal - first_tile - 1, 0)

        @pl.when(between % 2 == 1)
        def _():
            step(first_tile + 1, 1, False, False)

        def middle(index, carry):
            step(first_tile + 1 + between % 2 + 2 * index, 2, False, False)
            return carry

        lax.fori_loop(0, between // 2, middle, 0)
        step(diagonal, 1, True, True)
        return carry

    lax.fori_loop(0, near, shard, 0)
    run_all([(out.at[plane_ref[1] ^ at], target) for at, target in enumerate(outs)], out_sems)


def attend(arrived, keys, turned, places, slots, counts, doc_lengths, plane, index, near, rows):
    block_rows, width = arrived[0].shape[1:]
    far = counts.shape[0]
    blocks = slots.shape[0]
    stride = places.shape[0] // far
    if block_rows % 16:
        joined = jnp.take(jnp.concatenate(arrived), slots, axis=0).reshape(-1, 16, width)
        arrived = [joined]
        block_rows = 16
        blocks = stride = joined.shape[0]
        places = jnp.arange(blocks, dtype=jnp.int32)
        counts = jnp.full((1,), blocks, jnp.int32)
    heads = width // HD
    shape = (rows, width)
    pairs = near * rows * keys.shape[0] * heads
    return call(
        functools.partial(attend_kernel, near, stride, doc_lengths.shape[0], heads),
        (places, counts, doc_lengths, jnp.stack([plane, index])),
        (*arrived, keys, turned),
        [ANY] * len(arrived) + [whole(keys.shape), whole(turned.shape)],
        [jax.ShapeDtypeStruct(shape, keys.dtype)] * near,
        [ANY] * near,
        [
            pltpu.VMEM((blocks, block_rows, width), keys.dtype),
            pltpu.VMEM((near, rows, width), keys.dtype),
            pltpu.VMEM((heads, 1, rows), jnp.float32),
            pltpu.VMEM((heads, HD + 16, rows), jnp.float32),
            pltpu.SemaphoreType.DMA(()),
            pltpu.SemaphoreType.DMA((near,)),
        ],
        "attend",
        cost_estimate=pl.CostEstimate(
            flops=4 * pairs * HD, transcendentals=pairs, bytes_accessed=4 * near * rows * width
        ),
    )


def join_kernel(near, index_ref, *refs):
    parts, out, sems = refs[:-2], refs[-2], refs[-1]
    group = out.shape[1] // near
    offset = 0
    pairs = []
    for at, part in enumerate(parts):
        width = part.shape[1]
        column = (index_ref[0] ^ (at % near)) * group + offset
        pairs.append((part, out.at[:, pl.ds(pl.multiple_of(column, HD), width)]))
        if at % near == near - 1:
            offset += width
    run_all(pairs, sems)


def join(parts, index, near):
    rows = parts[0].shape[0]
    shape = (rows, sum(part.shape[1] for part in parts))
    return call(
        functools.partial(join_kernel, near),
        (index[None],),
        parts,
        [ANY] * len(parts),
        jax.ShapeDtypeStruct(shape, parts[0].dtype),
        whole(shape),
        [pltpu.SemaphoreType.DMA((len(parts),))],
        "join",
        cost_estimate=moved(4 * shape[0] * shape[1]),
    )


def body(query, key, value, doc_lengths, block_place):
    far = lax.axis_size("far")
    near = lax.axis_size("near")
    cores = lax.axis_size("head")
    loaded_rows = query.shape[0]
    rows = loaded_rows * cores
    block_rows = rows // (far * near)
    shard_blocks = rows // block_rows
    plane_blocks = near * shard_blocks
    plane = lax.axis_index("far").astype(jnp.int32)
    most = near * cores * min(near, loaded_rows // block_rows)

    def across(parts, axis, size):
        return [parts[0]] + [
            lax.ppermute(parts[at], axis, [(d, d ^ at) for d in range(size)])
            for at in range(1, size)
        ]

    index = lax.axis_index("near").astype(jnp.int32)

    def in_plane(x):
        x = lax.all_to_all(x, ("near", "head"), split_axis=0, concat_axis=0, tiled=True)
        return x.reshape(plane_blocks, block_rows, -1)

    received = in_plane(split(query, key, value, near))
    loaded = jnp.arange(block_place.shape[0], dtype=jnp.int32)
    origin = loaded // plane_blocks
    target = block_place // plane_blocks
    course = origin * far + target
    ahead = (course[:, None] == course[None, :]) & (loaded[None, :] < loaded[:, None])
    rank = jnp.sum(ahead.astype(jnp.int32), axis=1)

    def where_sum(found, values):
        return jnp.sum(jnp.where(found, values[None, :], 0), axis=1)

    distances = jnp.arange(far, dtype=jnp.int32)[:, None]
    leaving = jnp.where(origin == plane, target ^ plane, far)
    landing = jnp.where(target == plane, origin ^ plane, far)
    ones = jnp.ones_like(loaded)
    leaving_counts = where_sum(distances == leaving[None, :], ones)
    landing_counts = where_sum(distances == landing[None, :], ones)
    window_blocks = SPAN * shard_blocks + plane_blocks
    wanted = (plane + 1) * plane_blocks - window_blocks + jnp.arange(window_blocks, dtype=jnp.int32)
    found = jnp.maximum(wanted, 0)[:, None] == block_place[None, :]

    every = jnp.arange(far * most, dtype=jnp.int32)[:, None]
    leaving_slot = leaving * most + rank
    landing_slot = landing * most + rank
    sources = where_sum(every == leaving_slot[None, :], loaded % plane_blocks)
    places = where_sum(every == landing_slot[None, :], block_place % plane_blocks)

    def with_slots(capacity, received):
        slots = where_sum(
            found[window_blocks - plane_blocks :], landing * capacity + rank
        )

        def attended(arrived):
            return attend(
                arrived,
                keys,
                turned,
                places,
                slots,
                landing_counts,
                doc_lengths,
                plane,
                index,
                near,
                rows,
            )

        def sent(received, offset, chunk):
            width = CHUNKS[chunk] * HD
            return list(pack(received, offset, width, sources, leaving_counts, capacity))

        pair = received[:, :, : 2 * HD]
        pair, received = lax.optimization_barrier((pair, received))
        keys, turned, hops = pick_window(pair, window_blocks, block_place, plane)
        arrived = []
        offset = 2 * HD
        for chunk in range(len(CHUNKS)):
            sending = sent(received, offset, chunk)
            offset += CHUNKS[chunk] * HD
            if chunk > 0:
                hops, sending = lax.optimization_barrier((hops, sending))
            arrived.append(across(sending, "far", far))
        parts = []
        for chunk in arrived:
            parts += across(list(attended(chunk)), "near", near)
        return join(parts, index, near)

    sizes = sorted({most * 5 // 8, most * 3 // 4, most})
    fullest = jnp.max(rank) + 1
    chosen = sum((fullest > size).astype(jnp.int32) for size in sizes[:-1])
    return lax.switch(chosen, [functools.partial(with_slots, size) for size in sizes], received)


def solution(mesh):
    near = 4
    shape = (mesh.shape["ctx"] // near, near, mesh.shape["head"])
    planes = Mesh(mesh.devices.reshape(shape), ("far", "near", "head"))
    placed = (
        P(("far", "near", "head"), None),
        P(("far", "near", "head"), None),
        P(("far", "near", "head"), None),
        P(),
        P(),
    )
    return jax.shard_map(
        body, mesh=planes, in_specs=placed, out_specs=P(("far", "near"), "head"), check_vma=False
    )
```

```python
import functools

import jax
import jax.numpy as jnp
import numpy as np
from jax import lax
from jax.experimental import pallas as pl
from jax.experimental.pallas import tpu as pltpu
from jax.sharding import Mesh
from jax.sharding import PartitionSpec as P

HD = 128
SPAN = 8
CHUNKS = (4, 4)
MASKED = -1e30
EXP2_SCALE = float(HD ** (-0.5) * np.log2(np.e))
VMEM_LIMIT = 60 * 1024 * 1024
ANY = pl.BlockSpec(memory_space=pl.ANY)


def whole(shape):
    return pl.BlockSpec(shape, lambda i, *_: (0,) * len(shape))


def call(kernel, scalars, arrays, in_specs, outs, out_specs, scratch, name, **more):
    return pl.pallas_call(
        kernel,
        out_shape=outs,
        grid_spec=pltpu.PrefetchScalarGridSpec(
            num_scalar_prefetch=len(scalars),
            grid=(1,),
            in_specs=in_specs,
            out_specs=out_specs,
            scratch_shapes=scratch,
        ),
        compiler_params=pltpu.CompilerParams(vmem_limit_bytes=VMEM_LIMIT),
        name=name,
        **more,
    )(*scalars, *arrays)


def moved(count):
    return pl.CostEstimate(flops=0, transcendentals=0, bytes_accessed=count)


def run_all(pairs, sems):
    copies = []
    for at, (source, target) in enumerate(pairs):
        copy = pltpu.make_async_copy(source, target, sems.at[at])
        copy.start()
        copies.append(copy)
    for copy in copies:
        copy.wait()


def split_kernel(near, query, key, value, first, later, sems):
    key_heads = first.shape[0]
    group = query.shape[1] // key_heads
    early = CHUNKS[0] * HD
    pairs = []
    for at in range(key_heads):
        head = at % 2 * near + at // 2
        start = head * group
        own = pl.ds(head * HD, HD)
        pairs.append((key.at[:, own], first.at[at, :, pl.ds(0, HD)]))
        pairs.append((value.at[:, own], first.at[at, :, pl.ds(HD, HD)]))
        pairs.append((query.at[:, pl.ds(start, early)], first.at[at, :, pl.ds(2 * HD, early)]))
        pairs.append((query.at[:, pl.ds(start + early, group - early)], later.at[at]))
    run_all(pairs, sems)


def split(query, key, value, near):
    rows, columns = query.shape
    key_heads = key.shape[1] // HD
    early = CHUNKS[0] * HD
    widths = (early + 2 * HD, columns // key_heads - early)
    return call(
        functools.partial(split_kernel, near),
        (),
        (query, key, value),
        [whole(query.shape), whole(key.shape), whole(value.shape)],
        [jax.ShapeDtypeStruct((key_heads, rows, width), query.dtype) for width in widths],
        [ANY] * 2,
        [pltpu.SemaphoreType.DMA((4 * key_heads,))],
        "split",
        cost_estimate=moved(4 * rows * (columns + 2 * key.shape[1])),
    )


def pack_kernel(offset, stride, source_ref, counts_ref, received, *refs):
    outs, (blocks, in_sem, sem) = refs[:-3], refs[-3:]
    run_all([(received.at[:, :, pl.ds(offset, blocks.shape[2])], blocks)], in_sem)
    for distance, out in enumerate(outs):

        def start(r, carry):
            source = source_ref[distance * stride + r]
            pltpu.make_async_copy(blocks.at[source], out.at[r], sem).start()
            return carry

        lax.fori_loop(0, counts_ref[distance], start, 0)
    pltpu.make_async_copy(blocks, blocks, sem).wait()


def pack(received, offset, width, sources, counts, capacity):
    total, block_rows, _ = received.shape
    far = counts.shape[0]
    stride = sources.shape[0] // far
    if block_rows % 16:
        packed = jnp.take(received[:, :, offset : offset + width], sources, axis=0)
        packed = packed.reshape(far, stride, block_rows, width)[:, :capacity]
        return [packed[at] for at in range(far)]
    return call(
        functools.partial(pack_kernel, offset, stride),
        (sources, counts),
        (received,),
        [ANY],
        [jax.ShapeDtypeStruct((capacity, block_rows, width), received.dtype)] * far,
        [ANY] * far,
        [
            pltpu.VMEM((total, block_rows, width), received.dtype),
            pltpu.SemaphoreType.DMA((1,)),
            pltpu.SemaphoreType.DMA(()),
        ],
        "pack",
        cost_estimate=moved(4 * total * block_rows * width),
    )


def window_kernel(pieces, rows_ref, counts_ref, *refs):
    arrived, (keys, turned, held, sem) = refs[:pieces], refs[pieces:]
    count, block_rows, _ = held.shape
    limit = arrived[0].shape[0]
    for at, piece in enumerate(arrived):

        def start(b, carry):
            row = rows_ref[at * limit + b]

            @pl.when(row >= 0)
            def _():
                pltpu.make_async_copy(piece.at[b], held.at[row], sem).start()

            return carry

        lax.fori_loop(0, counts_ref[at], start, 0)
    turned[HD:] = jnp.ones((turned.shape[0] - HD, turned.shape[1]), turned.dtype)

    def wait(b, carry):
        pltpu.make_async_copy(held.at[0], held.at[0], sem).wait()
        return carry

    lax.fori_loop(0, counts_ref[pieces], wait, 0)
    each = 256 // block_rows
    for part in range(count // each):
        at = pl.ds(part * 256, 256)
        blocks_at = pl.ds(part * each, each)
        keys[at] = held[blocks_at, :, :HD].reshape(256, HD)
        turned[:HD, at] = held[blocks_at, :, HD:].reshape(256, HD).T


def window_rows(block_place, plane, far, count):
    total = block_place.shape[0] // far
    first = (plane + 1) * total - count
    hops = np.array(list(range(far)) + list(range(-1, -far, -1)), dtype=np.int32)
    planes = plane - hops
    real = (planes >= 0) & (planes < far)
    places = jnp.take(block_place.reshape(far, total), jnp.clip(planes, 0, far - 1), axis=0) - first
    inside = (places >= 0) & (places < count)
    places = jnp.where(inside, places, -1)
    counts = jnp.where(real, total, 0).astype(jnp.int32)
    moving = jnp.sum((inside & real[:, None]).astype(jnp.int32))
    return places.reshape(-1), jnp.concatenate([counts, moving[None]])


def pick_window(pair, count, block_place, plane, places, counts):
    far = lax.axis_size("far")
    total, block_rows, width = pair.shape
    rows = count * block_rows
    if block_rows % 16:
        first = (plane + 1) * total - count
        wanted = jnp.maximum(first + jnp.arange(count, dtype=jnp.int32), 0)
        loaded = jnp.argmax(wanted[:, None] == block_place[None, :], axis=1)
        gathered = lax.all_gather(pair, "far", tiled=True)
        window = jnp.take(gathered, loaded, axis=0).reshape(rows, width)
        turned = jnp.concatenate([window[:, HD:].T, jnp.ones((16, rows), window.dtype)])
        return window[:, :HD], turned, [pair]
    up, down = [pair], [pair]
    for _ in range(far - 1):
        up.append(lax.ppermute(up[-1], "far", [(p, p + 1) for p in range(far - 1)]))
        down.append(lax.ppermute(down[-1], "far", [(p + 1, p) for p in range(far - 1)]))
    pieces = up + down[1:]
    shapes = [(rows, HD), (HD + 16, rows)]
    keys, turned = call(
        functools.partial(window_kernel, len(pieces)),
        (places, counts),
        pieces,
        [ANY] * len(pieces),
        [jax.ShapeDtypeStruct(shape, pair.dtype) for shape in shapes],
        [whole(shape) for shape in shapes],
        [pltpu.VMEM((count, block_rows, width), pair.dtype), pltpu.SemaphoreType.DMA(())],
        "window",
        cost_estimate=moved(4 * rows * width),
    )
    return keys, turned, [up[1], down[1]]


def attend_kernel(
    near, stride, docs, heads, place_ref, counts_ref, lengths_ref, plane_ref, *refs
):
    far = counts_ref.shape[0]
    arrived, keys, turned = refs[:far], refs[far], refs[far + 1]
    outs, (queries, out, maxes, sums, sem, out_sems) = refs[far + 2 : -6], refs[-6:]
    blocks, block_rows, width = queries.shape
    rows = blocks * block_rows // near
    tile = rows
    window_tiles = keys.shape[0] // tile
    per_shard = blocks // near
    for distance, piece in enumerate(arrived):

        def start(r, carry):
            place = place_ref[distance * stride + r]
            pltpu.make_async_copy(piece.at[r], queries.at[place], sem).start()
            return carry

        lax.fori_loop(0, counts_ref[distance], start, 0)
    plane_rows = near * rows
    window_start = (plane_ref[0] + 1) * plane_rows - keys.shape[0]
    pltpu.make_async_copy(queries, queries, sem).wait()

    def shard(j, carry):
        first_row = plane_ref[0] * plane_rows + j * rows
        query_rows = first_row + lax.broadcasted_iota(jnp.int32, (1, rows), 1)
        starts = jnp.zeros((1, rows), jnp.int32)
        first_start = jnp.int32(0)
        end = jnp.int32(0)
        for d in range(docs):
            length = lengths_ref[d]
            end = end + length
            starts = starts + jnp.where(query_rows >= end, length, 0)
            first_start = first_start + jnp.where(first_row >= end, length, 0)
        diagonal = window_tiles - near + j
        first_tile = (first_start - window_start) // tile
        for h in range(heads):
            maxes[h] = jnp.full((1, rows), MASKED, jnp.float32)
            sums[h] = jnp.zeros(sums.shape[1:], jnp.float32)

        def step(index, count, masked, last):
            span = count * tile
            at = pl.ds(pl.multiple_of(index * tile, tile), span)
            tile_keys = keys[at]
            tile_turned = turned[:, at]
            if masked:
                key_rows = (
                    window_start + index * tile + lax.broadcasted_iota(jnp.int32, (span, rows), 0)
                )
                visible = (key_rows >= starts) & (key_rows <= query_rows)
            if last:
                later = starts >= first_row

            def score(h):
                query = queries[pl.ds(j * per_shard, per_shard), :, h * HD : (h + 1) * HD]
                return lax.dot_general(
                    tile_keys,
                    query.reshape(rows, HD),
                    (((1,), (1,)), ((), ())),
                    preferred_element_type=jnp.float32,
                )

            ahead = score(0)
            for h in range(heads):
                scores = ahead
                if h + 1 < heads:
                    ahead = score(h + 1)
                if masked:
                    scores = jnp.where(visible, scores, MASKED)
                old = maxes[h]
                if last:
                    old = jnp.where(later, MASKED, old)
                new = jnp.maximum(old, jnp.max(scores, axis=0, keepdims=True))
                scaled = new * EXP2_SCALE
                weights = jnp.exp2(scores * EXP2_SCALE - scaled).astype(jnp.bfloat16)
                factor = jnp.exp2(old * EXP2_SCALE - scaled)
                product = jnp.dot(tile_turned, weights, preferred_element_type=jnp.float32)
                total = sums[h] * factor + product
                if last:
                    result = total[:HD] / total[HD : HD + 1]
                    out[j, :, h * HD : (h + 1) * HD] = result.T.astype(out.dtype)
                else:
                    maxes[h] = new
                    sums[h] = total

        @pl.when(first_tile < diagonal)
        def _():
            step(first_tile, 1, True, False)

        between = jnp.maximum(diagonal - first_tile - 1, 0)

        @pl.when(between % 2 == 1)
        def _():
            step(first_tile + 1, 1, False, False)

        def middle(index, carry):
            step(first_tile + 1 + between % 2 + 2 * index, 2, False, False)
            return carry

        lax.fori_loop(0, between // 2, middle, 0)
        step(diagonal, 1, True, True)
        return carry

    lax.fori_loop(0, near, shard, 0)
    run_all([(out.at[plane_ref[1] ^ at], target) for at, target in enumerate(outs)], out_sems)


def attend(arrived, keys, turned, places, slots, counts, doc_lengths, position, near, rows):
    block_rows, width = arrived[0].shape[1:]
    far = counts.shape[0]
    blocks = slots.shape[0]
    stride = places.shape[0] // far
    if block_rows % 16:
        joined = jnp.take(jnp.concatenate(arrived), slots, axis=0).reshape(-1, 16, width)
        arrived = [joined]
        block_rows = 16
        blocks = stride = joined.shape[0]
        places = jnp.arange(blocks, dtype=jnp.int32)
        counts = jnp.full((1,), blocks, jnp.int32)
    heads = width // HD
    shape = (rows, width)
    pairs = near * rows * keys.shape[0] * heads
    return call(
        functools.partial(attend_kernel, near, stride, doc_lengths.shape[0], heads),
        (places, counts, doc_lengths, position),
        (*arrived, keys, turned),
        [ANY] * len(arrived) + [whole(keys.shape), whole(turned.shape)],
        [jax.ShapeDtypeStruct(shape, keys.dtype)] * near,
        [ANY] * near,
        [
            pltpu.VMEM((blocks, block_rows, width), keys.dtype),
            pltpu.VMEM((near, rows, width), keys.dtype),
            pltpu.VMEM((heads, 1, rows), jnp.float32),
            pltpu.VMEM((heads, HD + 16, rows), jnp.float32),
            pltpu.SemaphoreType.DMA(()),
            pltpu.SemaphoreType.DMA((near,)),
        ],
        "attend",
        cost_estimate=pl.CostEstimate(
            flops=4 * pairs * HD, transcendentals=pairs, bytes_accessed=4 * near * rows * width
        ),
    )


def join_kernel(near, index_ref, *refs):
    parts, out, sems = refs[:-2], refs[-2], refs[-1]
    group = out.shape[1] // near
    offset = 0
    pairs = []
    for at, part in enumerate(parts):
        width = part.shape[1]
        column = (index_ref[0] ^ (at % near)) * group + offset
        pairs.append((part, out.at[:, pl.ds(pl.multiple_of(column, HD), width)]))
        if at % near == near - 1:
            offset += width
    run_all(pairs, sems)


def join(parts, index, near):
    rows = parts[0].shape[0]
    shape = (rows, sum(part.shape[1] for part in parts))
    return call(
        functools.partial(join_kernel, near),
        (index[None],),
        parts,
        [ANY] * len(parts),
        jax.ShapeDtypeStruct(shape, parts[0].dtype),
        whole(shape),
        [pltpu.SemaphoreType.DMA((len(parts),))],
        "join",
        cost_estimate=moved(4 * shape[0] * shape[1]),
    )


def body(query, key, value, doc_lengths, block_place):
    far = lax.axis_size("far")
    near = lax.axis_size("near")
    cores = lax.axis_size("head")
    loaded_rows = query.shape[0]
    rows = loaded_rows * cores
    block_rows = rows // (far * near)
    shard_blocks = rows // block_rows
    plane_blocks = near * shard_blocks
    plane = lax.axis_index("far").astype(jnp.int32)
    most = near * cores * min(near, loaded_rows // block_rows)

    def across(parts, axis, size):
        return [parts[0]] + [
            lax.ppermute(parts[at], axis, [(d, d ^ at) for d in range(size)])
            for at in range(1, size)
        ]

    index = lax.axis_index("near").astype(jnp.int32)

    def in_plane(x):
        x = lax.all_to_all(x, ("near", "head"), split_axis=0, concat_axis=0, tiled=True)
        return x.reshape(plane_blocks, block_rows, -1)

    first, later = split(query, key, value, near)
    received = in_plane(first)
    loaded = jnp.arange(block_place.shape[0], dtype=jnp.int32)
    origin = loaded // plane_blocks
    target = block_place // plane_blocks
    course = origin * far + target
    ahead = (course[:, None] == course[None, :]) & (loaded[None, :] < loaded[:, None])
    rank = jnp.sum(ahead.astype(jnp.int32), axis=1)

    def where_sum(found, values):
        return jnp.sum(jnp.where(found, values[None, :], 0), axis=1)

    distances = jnp.arange(far, dtype=jnp.int32)[:, None]
    leaving = jnp.where(origin == plane, target ^ plane, far)
    landing = jnp.where(target == plane, origin ^ plane, far)
    ones = jnp.ones_like(loaded)
    leaving_counts = where_sum(distances == leaving[None, :], ones)
    landing_counts = where_sum(distances == landing[None, :], ones)
    window_blocks = SPAN * shard_blocks + plane_blocks
    wanted = (plane + 1) * plane_blocks - window_blocks + jnp.arange(window_blocks, dtype=jnp.int32)
    found = jnp.maximum(wanted, 0)[:, None] == block_place[None, :]

    every = jnp.arange(far * most, dtype=jnp.int32)[:, None]
    leaving_slot = leaving * most + rank
    landing_slot = landing * most + rank
    sources = where_sum(every == leaving_slot[None, :], loaded % plane_blocks)
    places = where_sum(every == landing_slot[None, :], block_place % plane_blocks)

    window_places, window_counts = window_rows(block_place, plane, far, window_blocks)
    held = (leaving_counts, landing_counts, sources, places, window_places, window_counts)
    received, held, position = lax.optimization_barrier(
        (received, held, jnp.stack([plane, index]))
    )
    leaving_counts, landing_counts, sources, places, window_places, window_counts = held

    def with_slots(capacity, received, later):
        slots = where_sum(
            found[window_blocks - plane_blocks :], landing * capacity + rank
        )

        def attended(arrived):
            return attend(
                arrived,
                keys,
                turned,
                places,
                slots,
                landing_counts,
                doc_lengths,
                position,
                near,
                rows,
            )

        def sent(received, offset, chunk):
            width = CHUNKS[chunk] * HD
            return list(pack(received, offset, width, sources, leaving_counts, capacity))

        pair = received[:, :, : 2 * HD]
        pair, received = lax.optimization_barrier((pair, received))
        keys, turned, hops = pick_window(
            pair, window_blocks, block_place, plane, window_places, window_counts
        )
        arrived = [across(sent(received, 2 * HD, 0), "far", far)]
        hops, later = lax.optimization_barrier((hops, later))
        received = in_plane(later)
        offset = 0
        for chunk in range(1, len(CHUNKS)):
            arrived.append(across(sent(received, offset, chunk), "far", far))
            offset += CHUNKS[chunk] * HD
        parts = []
        for chunk in arrived:
            parts += across(list(attended(chunk)), "near", near)
        return join(parts, index, near)

    sizes = sorted({most * 5 // 8, most * 3 // 4, most})
    fullest = jnp.max(rank) + 1
    chosen = sum((fullest > size).astype(jnp.int32) for size in sizes[:-1])
    return lax.switch(chosen, [functools.partial(with_slots, size) for size in sizes], received, later)


def solution(mesh):
    near = 4
    shape = (mesh.shape["ctx"] // near, near, mesh.shape["head"])
    planes = Mesh(mesh.devices.reshape(shape), ("far", "near", "head"))
    placed = (
        P(("far", "near", "head"), None),
        P(("far", "near", "head"), None),
        P(("far", "near", "head"), None),
        P(),
        P(),
    )
    return jax.shard_map(
        body, mesh=planes, in_specs=placed, out_specs=P(("far", "near"), "head"), check_vma=False
    )
```

```python
import functools

import jax
import jax.numpy as jnp
import numpy as np
from jax import lax
from jax.experimental import pallas as pl
from jax.experimental.pallas import tpu as pltpu
from jax.sharding import Mesh
from jax.sharding import PartitionSpec as P

HD = 128
SPAN = 8
CHUNKS = (4, 4)
MASKED = -1e30
EXP2_SCALE = float(HD ** (-0.5) * np.log2(np.e))
VMEM_LIMIT = 60 * 1024 * 1024
ANY = pl.BlockSpec(memory_space=pl.ANY)


def whole(shape):
    return pl.BlockSpec(shape, lambda i, *_: (0,) * len(shape))


def call(kernel, scalars, arrays, in_specs, outs, out_specs, scratch, name, **more):
    return pl.pallas_call(
        kernel,
        out_shape=outs,
        grid_spec=pltpu.PrefetchScalarGridSpec(
            num_scalar_prefetch=len(scalars),
            grid=(1,),
            in_specs=in_specs,
            out_specs=out_specs,
            scratch_shapes=scratch,
        ),
        compiler_params=pltpu.CompilerParams(vmem_limit_bytes=VMEM_LIMIT),
        name=name,
        **more,
    )(*scalars, *arrays)


def moved(count):
    return pl.CostEstimate(flops=0, transcendentals=0, bytes_accessed=count)


def run_all(pairs, sems):
    copies = []
    for at, (source, target) in enumerate(pairs):
        copy = pltpu.make_async_copy(source, target, sems.at[at])
        copy.start()
        copies.append(copy)
    for copy in copies:
        copy.wait()


def split_kernel(near, query, key, value, first, later, sems):
    key_heads = first.shape[0]
    group = query.shape[1] // key_heads
    early = CHUNKS[0] * HD
    pairs = []
    for at in range(key_heads):
        head = at % 2 * near + at // 2
        start = head * group
        own = pl.ds(head * HD, HD)
        pairs.append((key.at[:, own], first.at[at, :, pl.ds(0, HD)]))
        pairs.append((value.at[:, own], first.at[at, :, pl.ds(HD, HD)]))
        pairs.append((query.at[:, pl.ds(start, early)], first.at[at, :, pl.ds(2 * HD, early)]))
        pairs.append((query.at[:, pl.ds(start + early, group - early)], later.at[at]))
    run_all(pairs, sems)


def split(query, key, value, near):
    rows, columns = query.shape
    key_heads = key.shape[1] // HD
    early = CHUNKS[0] * HD
    widths = (early + 2 * HD, columns // key_heads - early)
    return call(
        functools.partial(split_kernel, near),
        (),
        (query, key, value),
        [whole(query.shape), whole(key.shape), whole(value.shape)],
        [jax.ShapeDtypeStruct((key_heads, rows, width), query.dtype) for width in widths],
        [ANY] * 2,
        [pltpu.SemaphoreType.DMA((4 * key_heads,))],
        "split",
        cost_estimate=moved(4 * rows * (columns + 2 * key.shape[1])),
    )


def pack_kernel(offset, stride, source_ref, counts_ref, received, *refs):
    outs, (blocks, in_sem, sem) = refs[:-3], refs[-3:]
    run_all([(received.at[:, :, pl.ds(offset, blocks.shape[2])], blocks)], in_sem)
    for distance, out in enumerate(outs):

        def start(r, carry):
            source = source_ref[distance * stride + r]
            pltpu.make_async_copy(blocks.at[source], out.at[r], sem).start()
            return carry

        lax.fori_loop(0, counts_ref[distance], start, 0)
    pltpu.make_async_copy(blocks, blocks, sem).wait()


def pack(received, offset, width, sources, counts, capacity):
    total, block_rows, _ = received.shape
    far = counts.shape[0]
    stride = sources.shape[0] // far
    if block_rows % 16:
        packed = jnp.take(received[:, :, offset : offset + width], sources, axis=0)
        packed = packed.reshape(far, stride, block_rows, width)[:, :capacity]
        return [packed[at] for at in range(far)]
    return call(
        functools.partial(pack_kernel, offset, stride),
        (sources, counts),
        (received,),
        [ANY],
        [jax.ShapeDtypeStruct((capacity, block_rows, width), received.dtype)] * far,
        [ANY] * far,
        [
            pltpu.VMEM((total, block_rows, width), received.dtype),
            pltpu.SemaphoreType.DMA((1,)),
            pltpu.SemaphoreType.DMA(()),
        ],
        "pack",
        cost_estimate=moved(4 * total * block_rows * width),
    )


def window_kernel(pieces, rows_ref, counts_ref, *refs):
    arrived, (keys, turned, held, sem) = refs[:pieces], refs[pieces:]
    count, block_rows, _ = held.shape
    limit = arrived[0].shape[0]
    for at, piece in enumerate(arrived):

        def start(b, carry):
            row = rows_ref[at * limit + b]

            @pl.when(row >= 0)
            def _():
                pltpu.make_async_copy(piece.at[b], held.at[row], sem).start()

            return carry

        lax.fori_loop(0, counts_ref[at], start, 0)
    turned[HD:] = jnp.ones((turned.shape[0] - HD, turned.shape[1]), turned.dtype)

    def wait(b, carry):
        pltpu.make_async_copy(held.at[0], held.at[0], sem).wait()
        return carry

    lax.fori_loop(0, counts_ref[pieces], wait, 0)
    each = 256 // block_rows
    for part in range(count // each):
        at = pl.ds(part * 256, 256)
        blocks_at = pl.ds(part * each, each)
        keys[at] = held[blocks_at, :, :HD].reshape(256, HD)
        turned[:HD, at] = held[blocks_at, :, HD:].reshape(256, HD).T


def window_rows(block_place, plane, far, count):
    total = block_place.shape[0] // far
    first = (plane + 1) * total - count
    hops = np.array(list(range(far)) + list(range(-1, -far, -1)), dtype=np.int32)
    planes = plane - hops
    real = (planes >= 0) & (planes < far)
    places = jnp.take(block_place.reshape(far, total), jnp.clip(planes, 0, far - 1), axis=0) - first
    inside = (places >= 0) & (places < count)
    places = jnp.where(inside, places, -1)
    counts = jnp.where(real, total, 0).astype(jnp.int32)
    moving = jnp.sum((inside & real[:, None]).astype(jnp.int32))
    return places.reshape(-1), jnp.concatenate([counts, moving[None]])


def pick_window(pair, count, block_place, plane, places, counts, early):
    far = lax.axis_size("far")
    total, block_rows, width = pair.shape
    rows = count * block_rows
    if block_rows % 16:
        first = (plane + 1) * total - count
        wanted = jnp.maximum(first + jnp.arange(count, dtype=jnp.int32), 0)
        loaded = jnp.argmax(wanted[:, None] == block_place[None, :], axis=1)
        gathered = lax.all_gather(pair, "far", tiled=True)
        window = jnp.take(gathered, loaded, axis=0).reshape(rows, width)
        turned = jnp.concatenate([window[:, HD:].T, jnp.ones((16, rows), window.dtype)])
        return window[:, :HD], turned, [pair], early
    up, down = [pair], [pair]
    for hop in range(far - 1):
        if hop == far - 2:
            early, up[-1], down[-1] = lax.optimization_barrier((early, up[-1], down[-1]))
        up.append(lax.ppermute(up[-1], "far", [(p, p + 1) for p in range(far - 1)]))
        down.append(lax.ppermute(down[-1], "far", [(p + 1, p) for p in range(far - 1)]))
    pieces = up + down[1:]
    shapes = [(rows, HD), (HD + 16, rows)]
    keys, turned = call(
        functools.partial(window_kernel, len(pieces)),
        (places, counts),
        pieces,
        [ANY] * len(pieces),
        [jax.ShapeDtypeStruct(shape, pair.dtype) for shape in shapes],
        [whole(shape) for shape in shapes],
        [pltpu.VMEM((count, block_rows, width), pair.dtype), pltpu.SemaphoreType.DMA(())],
        "window",
        cost_estimate=moved(4 * rows * width),
    )
    return keys, turned, [up[1], down[1]], early


def attend_kernel(
    near, stride, docs, heads, place_ref, counts_ref, lengths_ref, plane_ref, *refs
):
    far = counts_ref.shape[0]
    arrived, keys, turned = refs[:far], refs[far], refs[far + 1]
    outs, (queries, out, maxes, sums, sem, out_sems) = refs[far + 2 : -6], refs[-6:]
    blocks, block_rows, width = queries.shape
    rows = blocks * block_rows // near
    tile = rows
    window_tiles = keys.shape[0] // tile
    per_shard = blocks // near
    for distance, piece in enumerate(arrived):

        def start(r, carry):
            place = place_ref[distance * stride + r]
            pltpu.make_async_copy(piece.at[r], queries.at[place], sem).start()
            return carry

        lax.fori_loop(0, counts_ref[distance], start, 0)
    plane_rows = near * rows
    window_start = (plane_ref[0] + 1) * plane_rows - keys.shape[0]
    pltpu.make_async_copy(queries, queries, sem).wait()

    def shard(j, carry):
        first_row = plane_ref[0] * plane_rows + j * rows
        query_rows = first_row + lax.broadcasted_iota(jnp.int32, (1, rows), 1)
        starts = jnp.zeros((1, rows), jnp.int32)
        first_start = jnp.int32(0)
        end = jnp.int32(0)
        for d in range(docs):
            length = lengths_ref[d]
            end = end + length
            starts = starts + jnp.where(query_rows >= end, length, 0)
            first_start = first_start + jnp.where(first_row >= end, length, 0)
        diagonal = window_tiles - near + j
        first_tile = (first_start - window_start) // tile
        for h in range(heads):
            maxes[h] = jnp.full((1, rows), MASKED, jnp.float32)
            sums[h] = jnp.zeros(sums.shape[1:], jnp.float32)

        def step(index, count, masked, last):
            span = count * tile
            at = pl.ds(pl.multiple_of(index * tile, tile), span)
            tile_keys = keys[at]
            tile_turned = turned[:, at]
            if masked:
                key_rows = (
                    window_start + index * tile + lax.broadcasted_iota(jnp.int32, (span, rows), 0)
                )
                visible = (key_rows >= starts) & (key_rows <= query_rows)
            if last:
                later = starts >= first_row

            def score(h):
                query = queries[pl.ds(j * per_shard, per_shard), :, h * HD : (h + 1) * HD]
                return lax.dot_general(
                    tile_keys,
                    query.reshape(rows, HD),
                    (((1,), (1,)), ((), ())),
                    preferred_element_type=jnp.float32,
                )

            ahead = score(0)
            for h in range(heads):
                scores = ahead
                if h + 1 < heads:
                    ahead = score(h + 1)
                if masked:
                    scores = jnp.where(visible, scores, MASKED)
                old = maxes[h]
                if last:
                    old = jnp.where(later, MASKED, old)
                new = jnp.maximum(old, jnp.max(scores, axis=0, keepdims=True))
                scaled = new * EXP2_SCALE
                weights = jnp.exp2(scores * EXP2_SCALE - scaled).astype(jnp.bfloat16)
                factor = jnp.exp2(old * EXP2_SCALE - scaled)
                product = jnp.dot(tile_turned, weights, preferred_element_type=jnp.float32)
                total = sums[h] * factor + product
                if last:
                    result = total[:HD] / total[HD : HD + 1]
                    out[j, :, h * HD : (h + 1) * HD] = result.T.astype(out.dtype)
                else:
                    maxes[h] = new
                    sums[h] = total

        @pl.when(first_tile < diagonal)
        def _():
            step(first_tile, 1, True, False)

        between = jnp.maximum(diagonal - first_tile - 1, 0)

        @pl.when(between % 2 == 1)
        def _():
            step(first_tile + 1, 1, False, False)

        def middle(index, carry):
            step(first_tile + 1 + between % 2 + 2 * index, 2, False, False)
            return carry

        lax.fori_loop(0, between // 2, middle, 0)
        step(diagonal, 1, True, True)
        return carry

    lax.fori_loop(0, near, shard, 0)
    run_all([(out.at[plane_ref[1] ^ at], target) for at, target in enumerate(outs)], out_sems)


def attend(arrived, keys, turned, places, slots, counts, doc_lengths, position, near, rows):
    block_rows, width = arrived[0].shape[1:]
    far = counts.shape[0]
    blocks = slots.shape[0]
    stride = places.shape[0] // far
    if block_rows % 16:
        joined = jnp.take(jnp.concatenate(arrived), slots, axis=0).reshape(-1, 16, width)
        arrived = [joined]
        block_rows = 16
        blocks = stride = joined.shape[0]
        places = jnp.arange(blocks, dtype=jnp.int32)
        counts = jnp.full((1,), blocks, jnp.int32)
    heads = width // HD
    shape = (rows, width)
    pairs = near * rows * keys.shape[0] * heads
    return call(
        functools.partial(attend_kernel, near, stride, doc_lengths.shape[0], heads),
        (places, counts, doc_lengths, position),
        (*arrived, keys, turned),
        [ANY] * len(arrived) + [whole(keys.shape), whole(turned.shape)],
        [jax.ShapeDtypeStruct(shape, keys.dtype)] * near,
        [ANY] * near,
        [
            pltpu.VMEM((blocks, block_rows, width), keys.dtype),
            pltpu.VMEM((near, rows, width), keys.dtype),
            pltpu.VMEM((heads, 1, rows), jnp.float32),
            pltpu.VMEM((heads, HD + 16, rows), jnp.float32),
            pltpu.SemaphoreType.DMA(()),
            pltpu.SemaphoreType.DMA((near,)),
        ],
        "attend",
        cost_estimate=pl.CostEstimate(
            flops=4 * pairs * HD, transcendentals=pairs, bytes_accessed=4 * near * rows * width
        ),
    )


def join_kernel(near, index_ref, *refs):
    parts, out, sems = refs[:-2], refs[-2], refs[-1]
    group = out.shape[1] // near
    offset = 0
    pairs = []
    for at, part in enumerate(parts):
        width = part.shape[1]
        column = (index_ref[0] ^ (at % near)) * group + offset
        pairs.append((part, out.at[:, pl.ds(pl.multiple_of(column, HD), width)]))
        if at % near == near - 1:
            offset += width
    run_all(pairs, sems)


def join(parts, index, near):
    rows = parts[0].shape[0]
    shape = (rows, sum(part.shape[1] for part in parts))
    return call(
        functools.partial(join_kernel, near),
        (index[None],),
        parts,
        [ANY] * len(parts),
        jax.ShapeDtypeStruct(shape, parts[0].dtype),
        whole(shape),
        [pltpu.SemaphoreType.DMA((len(parts),))],
        "join",
        cost_estimate=moved(4 * shape[0] * shape[1]),
    )


def body(query, key, value, doc_lengths, block_place):
    far = lax.axis_size("far")
    near = lax.axis_size("near")
    cores = lax.axis_size("head")
    loaded_rows = query.shape[0]
    rows = loaded_rows * cores
    block_rows = rows // (far * near)
    shard_blocks = rows // block_rows
    plane_blocks = near * shard_blocks
    plane = lax.axis_index("far").astype(jnp.int32)
    most = near * cores * min(near, loaded_rows // block_rows)

    def across(parts, axis, size):
        return [parts[0]] + [
            lax.ppermute(parts[at], axis, [(d, d ^ at) for d in range(size)])
            for at in range(1, size)
        ]

    index = lax.axis_index("near").astype(jnp.int32)

    def in_plane(x):
        x = lax.all_to_all(x, ("near", "head"), split_axis=0, concat_axis=0, tiled=True)
        return x.reshape(plane_blocks, block_rows, -1)

    first, later = split(query, key, value, near)
    received = in_plane(first)
    loaded = jnp.arange(block_place.shape[0], dtype=jnp.int32)
    origin = loaded // plane_blocks
    target = block_place // plane_blocks
    course = origin * far + target
    ahead = (course[:, None] == course[None, :]) & (loaded[None, :] < loaded[:, None])
    rank = jnp.sum(ahead.astype(jnp.int32), axis=1)

    def where_sum(found, values):
        return jnp.sum(jnp.where(found, values[None, :], 0), axis=1)

    distances = jnp.arange(far, dtype=jnp.int32)[:, None]
    leaving = jnp.where(origin == plane, target ^ plane, far)
    landing = jnp.where(target == plane, origin ^ plane, far)
    ones = jnp.ones_like(loaded)
    leaving_counts = where_sum(distances == leaving[None, :], ones)
    landing_counts = where_sum(distances == landing[None, :], ones)
    window_blocks = SPAN * shard_blocks + plane_blocks
    wanted = (plane + 1) * plane_blocks - window_blocks + jnp.arange(window_blocks, dtype=jnp.int32)
    found = jnp.maximum(wanted, 0)[:, None] == block_place[None, :]

    every = jnp.arange(far * most, dtype=jnp.int32)[:, None]
    leaving_slot = leaving * most + rank
    landing_slot = landing * most + rank
    sources = where_sum(every == leaving_slot[None, :], loaded % plane_blocks)
    places = where_sum(every == landing_slot[None, :], block_place % plane_blocks)

    window_places, window_counts = window_rows(block_place, plane, far, window_blocks)
    held = (leaving_counts, landing_counts, sources, places, window_places, window_counts)
    received, held, position = lax.optimization_barrier(
        (received, held, jnp.stack([plane, index]))
    )
    leaving_counts, landing_counts, sources, places, window_places, window_counts = held

    def with_slots(capacity, received, later):
        slots = where_sum(
            found[window_blocks - plane_blocks :], landing * capacity + rank
        )

        def attended(arrived):
            return attend(
                arrived,
                keys,
                turned,
                places,
                slots,
                landing_counts,
                doc_lengths,
                position,
                near,
                rows,
            )

        def sent(received, offset, chunk):
            width = CHUNKS[chunk] * HD
            return list(pack(received, offset, width, sources, leaving_counts, capacity))

        pair = received[:, :, : 2 * HD]
        pair, received = lax.optimization_barrier((pair, received))
        early = across(sent(received, 2 * HD, 0), "far", far)
        keys, turned, hops, early = pick_window(
            pair, window_blocks, block_place, plane, window_places, window_counts, early
        )
        arrived = [early]
        hops, later = lax.optimization_barrier((hops, later))
        received = in_plane(later)
        offset = 0
        for chunk in range(1, len(CHUNKS)):
            arrived.append(across(sent(received, offset, chunk), "far", far))
            offset += CHUNKS[chunk] * HD
        parts = []
        for chunk in arrived:
            parts += across(list(attended(chunk)), "near", near)
        return join(parts, index, near)

    sizes = sorted({most * 5 // 8, most * 3 // 4, most})
    fullest = jnp.max(rank) + 1
    chosen = sum((fullest > size).astype(jnp.int32) for size in sizes[:-1])
    return lax.switch(chosen, [functools.partial(with_slots, size) for size in sizes], received, later)


def solution(mesh):
    near = 4
    shape = (mesh.shape["ctx"] // near, near, mesh.shape["head"])
    planes = Mesh(mesh.devices.reshape(shape), ("far", "near", "head"))
    placed = (
        P(("far", "near", "head"), None),
        P(("far", "near", "head"), None),
        P(("far", "near", "head"), None),
        P(),
        P(),
    )
    return jax.shard_map(
        body, mesh=planes, in_specs=placed, out_specs=P(("far", "near"), "head"), check_vma=False
    )
```

```python
import functools

import jax
import jax.numpy as jnp
import numpy as np
from jax import lax
from jax.experimental import pallas as pl
from jax.experimental.pallas import tpu as pltpu
from jax.sharding import Mesh
from jax.sharding import PartitionSpec as P

HD = 128
SPAN = 8
CHUNKS = (4, 4)
MASKED = -1e30
EXP2_SCALE = float(HD ** (-0.5) * np.log2(np.e))
VMEM_LIMIT = 60 * 1024 * 1024
ANY = pl.BlockSpec(memory_space=pl.ANY)


def whole(shape):
    return pl.BlockSpec(shape, lambda i, *_: (0,) * len(shape))


def call(kernel, scalars, arrays, in_specs, outs, out_specs, scratch, name, **more):
    return pl.pallas_call(
        kernel,
        out_shape=outs,
        grid_spec=pltpu.PrefetchScalarGridSpec(
            num_scalar_prefetch=len(scalars),
            grid=(1,),
            in_specs=in_specs,
            out_specs=out_specs,
            scratch_shapes=scratch,
        ),
        compiler_params=pltpu.CompilerParams(vmem_limit_bytes=VMEM_LIMIT),
        name=name,
        **more,
    )(*scalars, *arrays)


def moved(count):
    return pl.CostEstimate(flops=0, transcendentals=0, bytes_accessed=count)


def run_all(pairs, sems):
    copies = []
    for at, (source, target) in enumerate(pairs):
        copy = pltpu.make_async_copy(source, target, sems.at[at])
        copy.start()
        copies.append(copy)
    for copy in copies:
        copy.wait()


def split_kernel(near, query, key, value, first, later, sems):
    key_heads = first.shape[0]
    group = query.shape[1] // key_heads
    early = CHUNKS[0] * HD
    pairs = []
    for at in range(key_heads):
        head = at % 2 * near + at // 2
        start = head * group
        own = pl.ds(head * HD, HD)
        pairs.append((key.at[:, own], first.at[at, :, pl.ds(0, HD)]))
        pairs.append((value.at[:, own], first.at[at, :, pl.ds(HD, HD)]))
        pairs.append((query.at[:, pl.ds(start, early)], first.at[at, :, pl.ds(2 * HD, early)]))
        pairs.append((query.at[:, pl.ds(start + early, group - early)], later.at[at]))
    run_all(pairs, sems)


def split(query, key, value, near):
    rows, columns = query.shape
    key_heads = key.shape[1] // HD
    early = CHUNKS[0] * HD
    widths = (early + 2 * HD, columns // key_heads - early)
    return call(
        functools.partial(split_kernel, near),
        (),
        (query, key, value),
        [whole(query.shape), whole(key.shape), whole(value.shape)],
        [jax.ShapeDtypeStruct((key_heads, rows, width), query.dtype) for width in widths],
        [ANY] * 2,
        [pltpu.SemaphoreType.DMA((4 * key_heads,))],
        "split",
        cost_estimate=moved(4 * rows * (columns + 2 * key.shape[1])),
    )


def pack_kernel(offset, stride, source_ref, counts_ref, received, *refs):
    outs, (blocks, in_sem, sem) = refs[:-3], refs[-3:]
    run_all([(received.at[:, :, pl.ds(offset, blocks.shape[2])], blocks)], in_sem)
    for distance, out in enumerate(outs):

        def start(r, carry):
            source = source_ref[distance * stride + r]
            pltpu.make_async_copy(blocks.at[source], out.at[r], sem).start()
            return carry

        lax.fori_loop(0, counts_ref[distance], start, 0)
    pltpu.make_async_copy(blocks, blocks, sem).wait()


def pack(received, offset, width, sources, counts, capacity):
    total, block_rows, _ = received.shape
    far = counts.shape[0]
    stride = sources.shape[0] // far
    if block_rows % 16:
        packed = jnp.take(received[:, :, offset : offset + width], sources, axis=0)
        packed = packed.reshape(far, stride, block_rows, width)[:, :capacity]
        return [packed[at] for at in range(far)]
    return call(
        functools.partial(pack_kernel, offset, stride),
        (sources, counts),
        (received,),
        [ANY],
        [jax.ShapeDtypeStruct((capacity, block_rows, width), received.dtype)] * far,
        [ANY] * far,
        [
            pltpu.VMEM((total, block_rows, width), received.dtype),
            pltpu.SemaphoreType.DMA((1,)),
            pltpu.SemaphoreType.DMA(()),
        ],
        "pack",
        cost_estimate=moved(4 * total * block_rows * width),
    )


def window_kernel(pieces, rows_ref, counts_ref, *refs):
    arrived, (keys, turned, held, sem) = refs[:pieces], refs[pieces:]
    count, block_rows, _ = held.shape
    limit = arrived[0].shape[0]
    for at, piece in enumerate(arrived):

        def start(b, carry):
            row = rows_ref[at * limit + b]

            @pl.when(row >= 0)
            def _():
                pltpu.make_async_copy(piece.at[b], held.at[row], sem).start()

            return carry

        lax.fori_loop(0, counts_ref[at], start, 0)
    turned[HD:] = jnp.ones((turned.shape[0] - HD, turned.shape[1]), turned.dtype)

    def wait(b, carry):
        pltpu.make_async_copy(held.at[0], held.at[0], sem).wait()
        return carry

    lax.fori_loop(0, counts_ref[pieces], wait, 0)
    each = 256 // block_rows
    for part in range(count // each):
        at = pl.ds(part * 256, 256)
        blocks_at = pl.ds(part * each, each)
        keys[at] = held[blocks_at, :, :HD].reshape(256, HD)
        turned[:HD, at] = held[blocks_at, :, HD:].reshape(256, HD).T


def window_rows(block_place, plane, far, count):
    total = block_place.shape[0] // far
    first = (plane + 1) * total - count
    hops = np.array(list(range(far)) + list(range(-1, -far, -1)), dtype=np.int32)
    planes = plane - hops
    real = (planes >= 0) & (planes < far)
    places = jnp.take(block_place.reshape(far, total), jnp.clip(planes, 0, far - 1), axis=0) - first
    inside = (places >= 0) & (places < count)
    places = jnp.where(inside, places, -1)
    counts = jnp.where(real, total, 0).astype(jnp.int32)
    moving = jnp.sum((inside & real[:, None]).astype(jnp.int32))
    return places.reshape(-1), jnp.concatenate([counts, moving[None]])


def pick_window(pair, count, block_place, plane, places, counts, early):
    far = lax.axis_size("far")
    total, block_rows, width = pair.shape
    rows = count * block_rows
    if block_rows % 16:
        first = (plane + 1) * total - count
        wanted = jnp.maximum(first + jnp.arange(count, dtype=jnp.int32), 0)
        loaded = jnp.argmax(wanted[:, None] == block_place[None, :], axis=1)
        gathered = lax.all_gather(pair, "far", tiled=True)
        window = jnp.take(gathered, loaded, axis=0).reshape(rows, width)
        turned = jnp.concatenate([window[:, HD:].T, jnp.ones((16, rows), window.dtype)])
        return window[:, :HD], turned, [pair], early
    up, down = [pair], [pair]
    for hop in range(far - 1):
        if hop == far - 2:
            early[1], up[-1], down[-1] = lax.optimization_barrier((early[1], up[-1], down[-1]))
        up.append(lax.ppermute(up[-1], "far", [(p, p + 1) for p in range(far - 1)]))
        down.append(lax.ppermute(down[-1], "far", [(p + 1, p) for p in range(far - 1)]))
    pieces = up + down[1:]
    shapes = [(rows, HD), (HD + 16, rows)]
    keys, turned = call(
        functools.partial(window_kernel, len(pieces)),
        (places, counts),
        pieces,
        [ANY] * len(pieces),
        [jax.ShapeDtypeStruct(shape, pair.dtype) for shape in shapes],
        [whole(shape) for shape in shapes],
        [pltpu.VMEM((count, block_rows, width), pair.dtype), pltpu.SemaphoreType.DMA(())],
        "window",
        cost_estimate=moved(4 * rows * width),
    )
    return keys, turned, [up[1], down[1]], early


def attend_kernel(
    near, stride, docs, heads, place_ref, counts_ref, lengths_ref, plane_ref, *refs
):
    far = counts_ref.shape[0]
    arrived, keys, turned = refs[:far], refs[far], refs[far + 1]
    outs, (queries, out, maxes, sums, sem, out_sems) = refs[far + 2 : -6], refs[-6:]
    blocks, block_rows, width = queries.shape
    rows = blocks * block_rows // near
    tile = rows
    window_tiles = keys.shape[0] // tile
    per_shard = blocks // near
    for distance, piece in enumerate(arrived):

        def start(r, carry):
            place = place_ref[distance * stride + r]
            pltpu.make_async_copy(piece.at[r], queries.at[place], sem).start()
            return carry

        lax.fori_loop(0, counts_ref[distance], start, 0)
    plane_rows = near * rows
    window_start = (plane_ref[0] + 1) * plane_rows - keys.shape[0]
    pltpu.make_async_copy(queries, queries, sem).wait()

    def shard(j, carry):
        first_row = plane_ref[0] * plane_rows + j * rows
        query_rows = first_row + lax.broadcasted_iota(jnp.int32, (1, rows), 1)
        starts = jnp.zeros((1, rows), jnp.int32)
        first_start = jnp.int32(0)
        end = jnp.int32(0)
        for d in range(docs):
            length = lengths_ref[d]
            end = end + length
            starts = starts + jnp.where(query_rows >= end, length, 0)
            first_start = first_start + jnp.where(first_row >= end, length, 0)
        diagonal = window_tiles - near + j
        first_tile = (first_start - window_start) // tile
        for h in range(heads):
            maxes[h] = jnp.full((1, rows), MASKED, jnp.float32)
            sums[h] = jnp.zeros(sums.shape[1:], jnp.float32)

        def step(index, count, masked, last):
            span = count * tile
            at = pl.ds(pl.multiple_of(index * tile, tile), span)
            tile_keys = keys[at]
            tile_turned = turned[:, at]
            if masked:
                key_rows = (
                    window_start + index * tile + lax.broadcasted_iota(jnp.int32, (span, rows), 0)
                )
                visible = (key_rows >= starts) & (key_rows <= query_rows)
            if last:
                later = starts >= first_row

            def score(h):
                query = queries[pl.ds(j * per_shard, per_shard), :, h * HD : (h + 1) * HD]
                return lax.dot_general(
                    tile_keys,
                    query.reshape(rows, HD),
                    (((1,), (1,)), ((), ())),
                    preferred_element_type=jnp.float32,
                )

            ahead = score(0)
            for h in range(heads):
                scores = ahead
                if h + 1 < heads:
                    ahead = score(h + 1)
                if masked:
                    scores = jnp.where(visible, scores, MASKED)
                old = maxes[h]
                if last:
                    old = jnp.where(later, MASKED, old)
                new = jnp.maximum(old, jnp.max(scores, axis=0, keepdims=True))
                scaled = new * EXP2_SCALE
                weights = jnp.exp2(scores * EXP2_SCALE - scaled).astype(jnp.bfloat16)
                factor = jnp.exp2(old * EXP2_SCALE - scaled)
                product = jnp.dot(tile_turned, weights, preferred_element_type=jnp.float32)
                total = sums[h] * factor + product
                if last:
                    result = total[:HD] / total[HD : HD + 1]
                    out[j, :, h * HD : (h + 1) * HD] = result.T.astype(out.dtype)
                else:
                    maxes[h] = new
                    sums[h] = total

        @pl.when(first_tile < diagonal)
        def _():
            step(first_tile, 1, True, False)

        between = jnp.maximum(diagonal - first_tile - 1, 0)

        @pl.when(between % 2 == 1)
        def _():
            step(first_tile + 1, 1, False, False)

        def middle(index, carry):
            step(first_tile + 1 + between % 2 + 2 * index, 2, False, False)
            return carry

        lax.fori_loop(0, between // 2, middle, 0)
        step(diagonal, 1, True, True)
        return carry

    lax.fori_loop(0, near, shard, 0)
    run_all([(out.at[plane_ref[1] ^ at], target) for at, target in enumerate(outs)], out_sems)


def attend(arrived, keys, turned, places, slots, counts, doc_lengths, position, near, rows):
    block_rows, width = arrived[0].shape[1:]
    far = counts.shape[0]
    blocks = slots.shape[0]
    stride = places.shape[0] // far
    if block_rows % 16:
        joined = jnp.take(jnp.concatenate(arrived), slots, axis=0).reshape(-1, 16, width)
        arrived = [joined]
        block_rows = 16
        blocks = stride = joined.shape[0]
        places = jnp.arange(blocks, dtype=jnp.int32)
        counts = jnp.full((1,), blocks, jnp.int32)
    heads = width // HD
    shape = (rows, width)
    pairs = near * rows * keys.shape[0] * heads
    return call(
        functools.partial(attend_kernel, near, stride, doc_lengths.shape[0], heads),
        (places, counts, doc_lengths, position),
        (*arrived, keys, turned),
        [ANY] * len(arrived) + [whole(keys.shape), whole(turned.shape)],
        [jax.ShapeDtypeStruct(shape, keys.dtype)] * near,
        [ANY] * near,
        [
            pltpu.VMEM((blocks, block_rows, width), keys.dtype),
            pltpu.VMEM((near, rows, width), keys.dtype),
            pltpu.VMEM((heads, 1, rows), jnp.float32),
            pltpu.VMEM((heads, HD + 16, rows), jnp.float32),
            pltpu.SemaphoreType.DMA(()),
            pltpu.SemaphoreType.DMA((near,)),
        ],
        "attend",
        cost_estimate=pl.CostEstimate(
            flops=4 * pairs * HD, transcendentals=pairs, bytes_accessed=4 * near * rows * width
        ),
    )


def join_kernel(near, index_ref, *refs):
    parts, out, sems = refs[:-2], refs[-2], refs[-1]
    group = out.shape[1] // near
    offset = 0
    pairs = []
    for at, part in enumerate(parts):
        width = part.shape[1]
        column = (index_ref[0] ^ (at % near)) * group + offset
        pairs.append((part, out.at[:, pl.ds(pl.multiple_of(column, HD), width)]))
        if at % near == near - 1:
            offset += width
    run_all(pairs, sems)


def join(parts, index, near):
    rows = parts[0].shape[0]
    shape = (rows, sum(part.shape[1] for part in parts))
    return call(
        functools.partial(join_kernel, near),
        (index[None],),
        parts,
        [ANY] * len(parts),
        jax.ShapeDtypeStruct(shape, parts[0].dtype),
        whole(shape),
        [pltpu.SemaphoreType.DMA((len(parts),))],
        "join",
        cost_estimate=moved(4 * shape[0] * shape[1]),
    )


def body(query, key, value, doc_lengths, block_place):
    far = lax.axis_size("far")
    near = lax.axis_size("near")
    cores = lax.axis_size("head")
    loaded_rows = query.shape[0]
    rows = loaded_rows * cores
    block_rows = rows // (far * near)
    shard_blocks = rows // block_rows
    plane_blocks = near * shard_blocks
    plane = lax.axis_index("far").astype(jnp.int32)
    most = near * cores * min(near, loaded_rows // block_rows)

    def across(parts, axis, size):
        return [parts[0]] + [
            lax.ppermute(parts[at], axis, [(d, d ^ at) for d in range(size)])
            for at in range(1, size)
        ]

    index = lax.axis_index("near").astype(jnp.int32)

    def in_plane(x):
        x = lax.all_to_all(x, ("near", "head"), split_axis=0, concat_axis=0, tiled=True)
        return x.reshape(plane_blocks, block_rows, -1)

    first, later = split(query, key, value, near)
    received = in_plane(first)
    loaded = jnp.arange(block_place.shape[0], dtype=jnp.int32)
    origin = loaded // plane_blocks
    target = block_place // plane_blocks
    course = origin * far + target
    ahead = (course[:, None] == course[None, :]) & (loaded[None, :] < loaded[:, None])
    rank = jnp.sum(ahead.astype(jnp.int32), axis=1)

    def where_sum(found, values):
        return jnp.sum(jnp.where(found, values[None, :], 0), axis=1)

    distances = jnp.arange(far, dtype=jnp.int32)[:, None]
    leaving = jnp.where(origin == plane, target ^ plane, far)
    landing = jnp.where(target == plane, origin ^ plane, far)
    ones = jnp.ones_like(loaded)
    leaving_counts = where_sum(distances == leaving[None, :], ones)
    landing_counts = where_sum(distances == landing[None, :], ones)
    window_blocks = SPAN * shard_blocks + plane_blocks
    wanted = (plane + 1) * plane_blocks - window_blocks + jnp.arange(window_blocks, dtype=jnp.int32)
    found = jnp.maximum(wanted, 0)[:, None] == block_place[None, :]

    every = jnp.arange(far * most, dtype=jnp.int32)[:, None]
    leaving_slot = leaving * most + rank
    landing_slot = landing * most + rank
    sources = where_sum(every == leaving_slot[None, :], loaded % plane_blocks)
    places = where_sum(every == landing_slot[None, :], block_place % plane_blocks)

    window_places, window_counts = window_rows(block_place, plane, far, window_blocks)
    held = (leaving_counts, landing_counts, sources, places, window_places, window_counts)
    received, held, position = lax.optimization_barrier(
        (received, held, jnp.stack([plane, index]))
    )
    leaving_counts, landing_counts, sources, places, window_places, window_counts = held

    def with_slots(capacity, received, later):
        slots = where_sum(
            found[window_blocks - plane_blocks :], landing * capacity + rank
        )

        def attended(arrived):
            return attend(
                arrived,
                keys,
                turned,
                places,
                slots,
                landing_counts,
                doc_lengths,
                position,
                near,
                rows,
            )

        def sent(received, offset, chunk):
            width = CHUNKS[chunk] * HD
            return list(pack(received, offset, width, sources, leaving_counts, capacity))

        pair = received[:, :, : 2 * HD]
        pair, received = lax.optimization_barrier((pair, received))
        early = across(sent(received, 2 * HD, 0), "far", far)
        keys, turned, hops, early = pick_window(
            pair, window_blocks, block_place, plane, window_places, window_counts, early
        )
        arrived = [early]
        hops, later = lax.optimization_barrier((hops, later))
        received = in_plane(later)
        offset = 0
        for chunk in range(1, len(CHUNKS)):
            arrived.append(across(sent(received, offset, chunk), "far", far))
            offset += CHUNKS[chunk] * HD
        parts = []
        for chunk in arrived:
            parts += across(list(attended(chunk)), "near", near)
        return join(parts, index, near)

    sizes = sorted({most * 5 // 8, most * 3 // 4, most})
    fullest = jnp.max(rank) + 1
    chosen = sum((fullest > size).astype(jnp.int32) for size in sizes[:-1])
    return lax.switch(chosen, [functools.partial(with_slots, size) for size in sizes], received, later)


def solution(mesh):
    near = 4
    shape = (mesh.shape["ctx"] // near, near, mesh.shape["head"])
    planes = Mesh(mesh.devices.reshape(shape), ("far", "near", "head"))
    placed = (
        P(("far", "near", "head"), None),
        P(("far", "near", "head"), None),
        P(("far", "near", "head"), None),
        P(),
        P(),
    )
    return jax.shard_map(
        body, mesh=planes, in_specs=placed, out_specs=P(("far", "near"), "head"), check_vma=False
    )
```
